256 devices in a mesh: box: 32 (over x, y, core), sub: 8 (over z).
Axes of the slice: x: 4, y: 4, z: 8, core: 2. Of those that a mesh axis runs over, the one named last changes fastest.
Arguments:
- source: float32 [256, 32, 4096], P('sub', None, 'box'), may hold values from -8 to 8
- beta: float32 [256, 32, 4096], P('sub', None, 'box'), may hold values from 0.1 to 10
- counts: int32 [32], replicated, may hold values from 1 to 4, 64 in all
Outputs:
- potential: float32 [256, 32, 4096], P('sub', None, 'box')
The draws below stay inside these ranges and needn't reach their ends.
Inputs may be any that keep to these rules, and one draw needn't show every extreme that they name: Columns are owned in order along x: index i of box owns the counts[i] columns after those of lower indices, in its first slots; the counts sum to 64, and some index owns exactly 4.
All inputs are finite; a program needn't handle non-finite values.
Results may differ from the reference program's by a relative error of at most 0.0001.
Values sent between devices are 32-bit elements; how exact they have to be, the bound alone decides.
A program may use at most 192 MiB of HBM per device.

```python
import math
import jax
import jax.numpy as jnp
import numpy as np

BS = 32
CAP = 4
COLS = 64
NZ = 256
WIDE = 4096
LEVELS = 3
PRE = 1
POST = 1
COARSE_SWEEPS = 8
N_BOX = 32


def steps_of(rng, shape, split, smallest, high):
    def one(position, blocks):
        draws = jax.random.uniform(jax.random.fold_in(jax.random.fold_in(rng, 6), position), (blocks,), jnp.float32, smallest / len(split), high / len(split))
        return jnp.repeat(jnp.exp(draws), shape[position] // blocks).reshape((-1,) + (1,) * (len(shape) - position - 1))

    factor_of = one(*split[0])
    for cut in split[1:]:
        factor_of = factor_of * one(*cut)
    return factor_of


def length_profile(number_of, total, reach, lean):
    loads = [(1 << 20) // math.isqrt(rank ** lean) + 1 for rank in range(2, number_of + 1)]
    rest, holding = total - reach - (number_of - 1), [1] * (number_of - 1)
    while rest > 0:
        free = [i for i in range(number_of - 1) if holding[i] < reach]
        pool, budget = sum([loads[i] for i in free]), rest
        for i in free:
            more = min(reach - holding[i], max(1, budget * loads[i] // pool), rest)
            holding[i] = holding[i] + more
            rest = rest - more
    return np.array([reach] + holding)


def ragged(stream_key, amount, total, bound, slope):
    if amount == 2:
        one = jax.random.randint(stream_key, (), max(1, total - bound), min(bound, total - 1) + 1)
        return jnp.stack([one, total - one])
    tallies = jnp.asarray(length_profile(amount, total, bound, slope), jnp.int32)
    pairs = (amount - 1) // 2
    donor, sink = tallies[1:1 + 2 * pairs:2], tallies[2:2 + 2 * pairs:2]
    room = jnp.minimum(donor - 1, bound - sink)
    shifted = jax.random.randint(jax.random.fold_in(stream_key, 1), (pairs,), 0, 1 << 20) % (room + 1)
    tallies = tallies.at[1:1 + 2 * pairs:2].set(donor - shifted).at[2:2 + 2 * pairs:2].set(sink + shifted)
    return tallies[jax.random.permutation(jax.random.fold_in(stream_key, 2), amount)]


def centred(key, shape, deviation, most, pieces=(), kind=jnp.bfloat16):
    result = deviation * jax.random.normal(key, shape, jnp.float32)
    if pieces:
        result = result * steps_of(key, shape, pieces, -0.22, 0.18)
    return jnp.clip(result, -most, most).astype(kind)


def setup_inputs(seed: int = 0) -> dict:
    keys = jax.random.split(jax.random.key(seed), 4)
    source = centred(keys[0], (NZ, BS, WIDE), 1.0, 8.0, ((0, 8), (2, 32)), jnp.float32)
    beta = jnp.clip(jnp.exp(math.log(10.0) - 4.6051702 * jax.random.uniform(keys[1], (NZ, BS, WIDE), jnp.float32) ** steps_of(keys[1], (NZ, BS, WIDE), ((0, 8), (2, 32)), -0.2, 0.2)), 0.1, 10.0)
    counts = ragged(keys[2], N_BOX, COLS, CAP, 2).astype(jnp.int32)
    return dict(source=source, beta=beta, counts=counts)


OMEGA = 0.8


def shifted_z(field, upward):
    zero_plane = jnp.zeros_like(field[:1])
    if upward:
        return jnp.concatenate([field[1:], zero_plane], 0)
    return jnp.concatenate([zero_plane, field[:-1]], 0)


def global_near(field):
    return (jnp.roll(field, 1, 2), jnp.roll(field, -1, 2), jnp.roll(field, 1, 1),
            jnp.roll(field, -1, 1), shifted_z(field, False), shifted_z(field, True))


def face_coefs(beta_level, nearby):
    beside_all = nearby(beta_level)
    couple = tuple(0.5 * (beta_level + other) for other in beside_all)
    diagonal = couple[0] + couple[1] + couple[2] + couple[3] + couple[4] + couple[5]
    return couple, diagonal


def apply_operator(field, nearby, couple, diagonal):
    beside_all = nearby(field)
    total = couple[0] * beside_all[0]
    for which in range(1, 6):
        total = total + couple[which] * beside_all[which]
    return diagonal * field - total


def relax(potential, source_level, nearby, couple, diagonal):
    return potential + OMEGA * (source_level - apply_operator(potential, nearby, couple, diagonal)) / diagonal


def children_sum(field):
    plane_count, row_count, col_count = field.shape
    return field.reshape(plane_count // 2, 2, row_count // 2, 2, col_count // 2, 2).sum(axis=(1, 3, 5))


def prolong(field):
    return jnp.repeat(jnp.repeat(jnp.repeat(field, 2, 0), 2, 1), 2, 2)


def column_index(counts, columns_total, width):
    ends = jnp.cumsum(counts).astype(jnp.int32)
    starts = ends - counts
    column = jnp.arange(columns_total, dtype=jnp.int32)
    owner = jnp.sum((column[:, None] >= ends[None, :]).astype(jnp.int32), axis=1).astype(jnp.int32)
    device_ids = jnp.arange(counts.shape[0], dtype=jnp.int32)
    owner_start = jnp.sum(jnp.where(owner[:, None] == device_ids[None, :], starts[None, :], 0), axis=1).astype(jnp.int32)
    base = owner * CAP + column - owner_start
    return (base[:, None] * width + jnp.arange(width, dtype=jnp.int32)[None, :]).reshape(-1).astype(jnp.int32)


def coarse_solve(source_level, beta_level):
    couple, diagonal = face_coefs(beta_level, global_near)
    potential = jnp.zeros_like(source_level)
    residual = source_level
    direction = residual / diagonal
    norm_now = jnp.sum(residual * residual / diagonal)
    for repeat in range(COARSE_SWEEPS):
        image = apply_operator(direction, global_near, couple, diagonal)
        alpha = norm_now / jnp.sum(direction * image)
        potential = potential + alpha * direction
        residual = residual - alpha * image
        norm_next = jnp.sum(residual * residual / diagonal)
        direction = residual / diagonal + (norm_next / norm_now) * direction
        norm_now = norm_next
    return potential


def vcycle(level, source_level, beta_level):
    if level == LEVELS:
        return coarse_solve(source_level, beta_level)
    couple, diagonal = face_coefs(beta_level, global_near)
    potential = jnp.zeros_like(source_level)
    for repeat in range(PRE):
        potential = relax(potential, source_level, global_near, couple, diagonal)
    residual = source_level - apply_operator(potential, global_near, couple, diagonal)
    correction = vcycle(level + 1, 0.5 * children_sum(residual), 0.125 * children_sum(beta_level))
    potential = potential + prolong(correction)
    for repeat in range(POST):
        potential = relax(potential, source_level, global_near, couple, diagonal)
    return potential


def reference(source, beta, counts):
    columns = column_index(counts, COLS, BS)
    compact_source = jnp.take(source, columns, axis=2)
    compact_beta = jnp.take(beta, columns, axis=2)
    solved = vcycle(0, compact_source, compact_beta)
    return jnp.zeros_like(source).at[:, :, columns].set(solved)
```

```python
import functools
import jax
import jax.numpy as jnp
from jax import lax
from jax.experimental import pallas as pl
from jax.experimental.pallas import tpu as pltpu
from jax.sharding import PartitionSpec as P

CAP = 4
SWEEPS = 8
OMEGA = 0.8
REST = 0.2
TINY = 1e-20
F32 = jnp.float32
BF16 = jnp.bfloat16
MESH = pl.DeviceIdType.MESH


def split(x):
    high = x.astype(BF16)
    rest = x - high.astype(F32)
    middle = rest.astype(BF16)
    low = (rest - middle.astype(F32)).astype(BF16)
    return (high, middle, low)


def pick_right(x, chosen):
    return sum(jnp.dot(part, chosen, preferred_element_type=F32) for part in split(x))


def pick_left(chosen, x):
    return sum(jnp.dot(chosen, part, preferred_element_type=F32) for part in split(x))


def pick_left_t(chosen, x):
    return sum(
        lax.dot_general(chosen, part, (((1,), (1,)), ((), ())), preferred_element_type=F32)
        for part in split(x)
    )


def ones_where(mask):
    return jnp.where(mask, 1.0, 0.0).astype(BF16)


def iota(shape, dim):
    return lax.broadcasted_iota(jnp.int32, shape, dim)


def turn(x, shift, axis):
    return pltpu.roll(x, shift, axis)


def around(x, step):
    rows = x.shape[-2]
    ax, ay = x.ndim - 1, x.ndim - 2
    return (
        turn(x, step, ax) + turn(x, 128 - step, ax) + turn(x, 1, ay) + turn(x, rows - 1, ay)
    )


def kernel(
    nb, ns,
    counts, source, beta, out,
    b0, f0, u0, v0, w0, rs, xs0, xr0, e0m, e0g,
    b1, f1, u1, v1, w1, xs1b, xr1b, xs1f, xr1f, y1, e1x,
    b2, f2, u2, v2, w2, xs2b, xr2b, xs2f, xr2f, y2,
    t3, tx, xa, ga, xb, gb_all, onehot, b3, f3, d3, i3, p3, r3, s3,
    in_sem, send_sem, recv_sem, zsend, zrecv, bsend, brecv,
):
    lanes_n = 16 * ns
    nz3 = 4 * ns
    vn = nb
    me, sub = lax.axis_index("box"), lax.axis_index("sub")
    left, right = lax.rem(me + nb - 1, nb), lax.rem(me + 1, nb)
    down, up = lax.rem(sub + ns - 1, ns), lax.rem(sub + 1, ns)
    floor, roof = sub == 0, sub == ns - 1

    get_b = pltpu.make_async_copy(beta, b0.at[pl.ds(2, 32)], in_sem.at[0])
    get_f = pltpu.make_async_copy(source, f0.at[pl.ds(1, 32)], in_sem.at[1])
    get_b.start()
    get_f.start()

    barrier = pltpu.get_barrier_semaphore()

    def greet_sub(k, carry):
        pl.semaphore_signal(
            barrier, inc=1, device_id=(me, lax.rem(sub + k, ns)), device_id_type=MESH
        )
        return carry

    def greet_box(k, carry):
        pl.semaphore_signal(
            barrier, inc=1, device_id=(lax.rem(me + k, nb), sub), device_id_type=MESH
        )
        return carry

    lax.fori_loop(1, ns, greet_sub, 0)
    lax.fori_loop(1, nb, greet_box, 0)
    for there in (left, right):
        for level in (down, up):
            pl.semaphore_signal(barrier, inc=1, device_id=(there, level), device_id_type=MESH)

    width = 32 * counts[me]
    width_left = 32 * counts[left]
    half = width // 2
    half_left = width_left // 2
    kk = iota((1, nb * 16), 1)
    kd, kj = kk // 16, kk % 16

    def place(d, carry):
        where_from, begin, mine = carry
        here = counts[d]
        value = jnp.where(kj < 4 * here, 4 * begin + kj, -1)
        where_from = jnp.where(kd == d, value, where_from)
        mine = jnp.where(d == me, begin, mine)
        return where_from, begin + here, mine

    where_from, _, my_start = lax.fori_loop(
        0, nb, place, (jnp.full((1, nb * 16), -1, jnp.int32), jnp.int32(0), jnp.int32(0))
    )
    row = iota((8 * vn, nb * 16), 0)
    onehot[...] = ones_where((row % 8) * vn + row // 8 == where_from)

    lane = iota((32, 128), 1)
    live = lane < width
    edge = (lane == 0) | (lane == width - 1)
    first_lane, last_lane = lane == 0, lane == 127
    mask_b = (lane < 2) | ((lane >= width - 2) & live)
    mask_f = edge

    ll = iota((128, 128), 0)
    lc = iota((128, 128), 1)
    squeeze = ones_where((ll // 2 == lc) & (ll < width))

    get_b.wait()
    get_f.wait()

    def load_plane(z, carry):
        tb, tf = carry
        b = jnp.where(live, b0[z + 2], 0.0)
        f = jnp.where(live, f0[z + 1], 0.0)
        b0[z + 2] = b
        f0[z + 1] = f
        tb = tb + turn(jnp.where(mask_b, b, 0.0), 4 * z, 1)
        tf = tf + turn(jnp.where(mask_f, f, 0.0), 4 * z, 1)
        return tb, tf

    zero_tile = jnp.zeros((32, 128), F32)
    tb, tf = lax.fori_loop(0, 32, load_plane, (zero_tile, zero_tile))
    xs0[0] = tb
    xs0[1] = tf

    pl.semaphore_wait(barrier, (ns - 1) + (nb - 1) + 4)

    def x_copies(src, dst, base):
        made = []
        for side, there in ((0, right), (1, left)):
            for slot, level in ((0, up), (1, sub), (2, down)):
                n = base + side * 3 + slot
                made.append(
                    pltpu.make_async_remote_copy(
                        src_ref=src, dst_ref=dst.at[side, slot],
                        send_sem=send_sem.at[n], recv_sem=recv_sem.at[n],
                        device_id=(there, level), device_id_type=MESH,
                    )
                )
        return made

    def z_copies(ref, own, halo, base):
        made = []
        for n, (begin, to, level) in enumerate(
            ((own, 0, up), (halo, own + halo, down))
        ):
            made.append(
                pltpu.make_async_remote_copy(
                    src_ref=ref.at[pl.ds(begin, halo)], dst_ref=ref.at[pl.ds(to, halo)],
                    send_sem=send_sem.at[base + n], recv_sem=recv_sem.at[base + n],
                    device_id=(me, level), device_id_type=MESH,
                )
            )
        return made

    def start(copies):
        for copy in copies:
            copy.start()

    def wait(copies):
        for copy in copies:
            copy.wait()

    copies0 = x_copies(xs0, xr0, 0) + z_copies(b0, 32, 2, 6) + z_copies(f0, 32, 1, 8)
    start(copies0)

    def squeeze_level0():
        both = rs[:, pl.ds(0, 16, stride=2), :] + rs[:, pl.ds(1, 16, stride=2), :]
        return pick_right(both.reshape(256, 128), squeeze).reshape(16, 16, 128)

    def coarsen(x, scratch, step):
        planes, rows, _ = x.shape
        pairs = x.reshape(planes // 2, 2, rows, 128)
        scratch[...] = pairs[:, 0] + pairs[:, 1]
        y = (
            scratch[:, pl.ds(0, rows // 2, stride=2), :]
            + scratch[:, pl.ds(1, rows // 2, stride=2), :]
        )
        odd = (iota(y.shape, 2) // step) % 2 == 1
        return y + jnp.where(odd, turn(y, step, 2), turn(y, 128 - step, 2))

    def pack(x, tile_ref, group, reach):
        planes, rows, _ = x.shape
        at = iota((rows, 128), 1)
        keep = (at < reach) | ((at >= half - reach) & (at < half))
        total = jnp.zeros((rows, 128), F32)
        for z in range(planes):
            total = total + turn(jnp.where(keep, x[z], 0.0), group * z, 1)
        tile_ref[...] = total

    def to_slots(x):
        for z in range(4):
            t3[pl.ds(z, 4, stride=8), :] = x[z]
            t3[pl.ds(z + 4, 4, stride=8), :] = x[z]
        tiles = t3[...].reshape(4, 1, 8, 128)
        tiles = jnp.broadcast_to(tiles, (4, ns // 2, 8, 128)).reshape(lanes_n, 128)
        tx[...] = jnp.transpose(tiles)
        return tx[pl.ds(0, 16, stride=4), :]

    def sub_copy(k, which, slot):
        return pltpu.make_async_remote_copy(
            src_ref=xa.at[which], dst_ref=ga.at[which, slot],
            send_sem=zsend.at[which, k], recv_sem=zrecv.at[which, k],
            device_id=(me, lax.rem(sub + k, ns)), device_id_type=MESH,
        )

    def box_copy(k, which, slot):
        return pltpu.make_async_remote_copy(
            src_ref=xb.at[which], dst_ref=gb_all.at[which, slot],
            send_sem=bsend.at[which, k], recv_sem=brecv.at[which, k],
            device_id=(lax.rem(me + k, nb), sub), device_id_type=MESH,
        )

    def send_all(make, which, mine, count):
        def body(k, carry):
            make(k, which, mine).start()
            return carry
        lax.fori_loop(1, count, body, 0)

    def wait_all(make, which, mine, count):
        def body(k, carry):
            copy = make(k, which, lax.rem(mine - k + count, count))
            copy.wait_send()
            copy.wait_recv()
            return carry
        lax.fori_loop(1, count, body, 0)

    def gather_start(x, which):
        tile = to_slots(x)
        xa[which] = tile
        ga[which, sub] = tile
        send_all(sub_copy, which, sub, ns)

    def gather_turn(which):
        wait_all(sub_copy, which, sub, ns)
        at = (iota((16, lanes_n), 1) // 4) % ns
        tile = jnp.zeros((16, lanes_n), F32)
        for k in range(ns):
            tile = jnp.where(at == k, ga[which, k], tile)
        xb[which] = tile
        gb_all[which, me] = tile
        send_all(box_copy, which, me, nb)

    def gather_end(which):
        wait_all(box_copy, which, me, nb)
        rows = gb_all[which].reshape(nb * 16, lanes_n)
        return pick_left(onehot[...], rows).reshape(vn, 8, lanes_n)

    def pair_b(k, carry):
        rs[k] = b0[2 * k + 2] + b0[2 * k + 3]
        return carry

    lax.fori_loop(0, 16, pair_b, 0)
    own_b1 = 0.125 * squeeze_level0()
    b1[pl.ds(3, 16)] = own_b1
    pack(own_b1, xs1b, 8, 3)
    copies_b1 = x_copies(xs1b, xr1b, 10) + z_copies(b1, 16, 3, 16)
    start(copies_b1)
    own_b2 = 0.125 * coarsen(own_b1, y1, 1)
    b2[pl.ds(3, 8)] = own_b2
    pack(own_b2, xs2b, 16, 6)
    copies_b2 = x_copies(xs2b, xr2b, 18) + z_copies(b2, 8, 3, 24)
    start(copies_b2)
    gather_start(0.125 * coarsen(own_b2, y2, 2), 0)

    wait(copies0)

    @pl.when(floor)
    def _():
        b0[pl.ds(0, 2)] = jnp.zeros((2, 32, 128), F32)
        f0[pl.ds(0, 1)] = jnp.zeros((1, 32, 128), F32)

    @pl.when(roof)
    def _():
        b0[pl.ds(34, 2)] = jnp.zeros((2, 32, 128), F32)
        f0[pl.ds(33, 1)] = jnp.zeros((1, 32, 128), F32)

    quarter = lane % 4
    group = lane // 4
    q0, q3 = quarter == 0, quarter == 3
    turn_l1 = lax.rem(129 - width_left + 128, 128)
    turn_l2 = lax.rem(130 - width_left + 128, 128)

    def ghost(slot, which, near_by):
        from_left, from_right = xr0[0, slot, which], xr0[1, slot, which]
        shift_l = turn_l1 if near_by == 1 else turn_l2
        return jnp.where(
            q0, turn(from_left, shift_l, 1),
            jnp.where(q3, turn(from_right, lax.rem(width - near_by, 128), 1), 0.0),
        )

    ghost_b = ghost(1, 0, 1)
    ghost_b_low = jnp.where(floor, 0.0, ghost(0, 0, 1))
    ghost_b_high = jnp.where(roof, 0.0, ghost(2, 0, 1))
    ghost_b_far = ghost(1, 0, 2)
    ghost_f = ghost(1, 1, 1)
    own_edge = jnp.where(q0 | q3, tb, 0.0)
    turned = width // 4 - 1
    first_z = (q0 & (group == 0)) | (q3 & (group == turned))
    last_z = (q0 & (group == 31)) | (q3 & (group == lax.rem(31 + turned, 32)))
    ghost_sum = (
        ghost_b_far + own_edge + turn(ghost_b, 1, 0) + turn(ghost_b, 31, 0)
        + turn(jnp.where(first_z, ghost_b_high, ghost_b), 124, 1)
        + turn(jnp.where(last_z, ghost_b_low, ghost_b), 4, 1)
    )
    ghost_diag = 3.0 * ghost_b + 0.5 * ghost_sum
    ghost_u = OMEGA * ghost_f / jnp.maximum(ghost_diag, TINY)
    ghost_k = ghost_b + own_edge
    ghost_c = ghost_k * ghost_u

    def spread(v):
        return (
            turn(jnp.where(last_lane, 0.0, v), 1, 1) + turn(jnp.where(first_lane, 0.0, v), 127, 1)
            + turn(v, 1, 0) + turn(v, 31, 0)
        )

    def start_plane(e, tile, shift):
        b = b0[e + 1]
        f = f0[e]
        total = spread(b) + b0[e] + b0[e + 2] + jnp.where(edge, turn(tile, shift, 1), 0.0)
        w = OMEGA / jnp.maximum(3.0 * b + 0.5 * total, TINY)
        u = w * f
        w0[e] = w
        u0[e] = u
        v0[e] = b * u

    def start_own(z, carry):
        start_plane(z + 1, ghost_b, lax.rem(128 - 4 * z, 128))
        return carry

    lax.fori_loop(0, 32, start_own, 0)
    start_plane(0, ghost_b_low, 4)
    start_plane(33, ghost_b_high, 0)

    def pull(e):
        return b0[e + 1] * (spread(u0[e]) + u0[e - 1] + u0[e + 1]) + (
            spread(v0[e]) + v0[e - 1] + v0[e + 1]
        )

    def residual(z):
        gain = pull(z + 1) + jnp.where(edge, turn(ghost_c, lax.rem(128 - 4 * z, 128), 1), 0.0)
        return REST * f0[z + 1] + 0.5 * gain

    def pair_r(k, carry):
        rs[k] = residual(2 * k) + residual(2 * k + 1)
        return carry

    lax.fori_loop(0, 16, pair_r, 0)

    def join(ref, xr, own, halo, gr, reach):
        rows = ref.shape[1]
        at = iota((rows, 128), 1)
        inside = at < half
        keep = ((at >= half) & (at < half + reach)) | (at >= 128 - reach)
        sub_at = at % gr
        tiles = []
        for slot in range(3):
            from_left = turn(xr[0, slot], lax.rem(256 - half_left, 128), 1)
            from_right = turn(xr[1, slot], half, 1)
            tiles.append(
                jnp.where(
                    sub_at >= gr - reach, from_left, jnp.where(sub_at < reach, from_right, 0.0)
                )
            )
        for z in range(-halo, own + halo):
            slot = 0 if z < 0 else (2 if z >= own else 1)
            there = z % own
            plane = jnp.where(
                inside, ref[z + halo],
                jnp.where(keep, turn(tiles[slot], (128 - gr * there) % 128, 1), 0.0),
            )
            if z < 0:
                plane = jnp.where(floor, 0.0, plane)
            if z >= own:
                plane = jnp.where(roof, 0.0, plane)
            ref[z + halo] = plane

    def weights(b, step):
        n = b.shape[0]
        middle = b[1:n - 1]
        total = around(middle, step) + b[:n - 2] + b[2:]
        return OMEGA / jnp.maximum(3.0 * middle + 0.5 * total, TINY)

    def gain_of(b, u, v, step):
        n = u.shape[0]
        return b * (around(u[1:n - 1], step) + u[:n - 2] + u[2:]) + (
            around(v[1:n - 1], step) + v[:n - 2] + v[2:]
        )

    def begin_level(b_ref, f_ref, w_ref, u_ref, v_ref, own, step):
        w = w_ref[...]
        u = w * f_ref[...]
        u_ref[...] = u
        v = b_ref[pl.ds(1, own + 4)] * u
        v_ref[...] = v
        b = b_ref[pl.ds(3, own)]
        gain = gain_of(b, u[1:own + 3], v[1:own + 3], step)
        return REST * f_ref[pl.ds(2, own)] + 0.5 * gain

    def end_level(b_ref, f_ref, w_ref, u, own, step):
        v = b_ref[pl.ds(1, own + 4)] * u
        b = b_ref[pl.ds(2, own + 2)]
        gain = gain_of(b, u, v, step)
        e = REST * u[1:own + 3] + w_ref[pl.ds(1, own + 2)] * (
            f_ref[pl.ds(1, own + 2)] + 0.5 * gain
        )
        return jnp.concatenate([
            jnp.where(floor, 0.0, e[:1]), e[1:own + 1], jnp.where(roof, 0.0, e[own + 1:])
        ], 0)

    own_f1 = 0.5 * squeeze_level0()
    f1[pl.ds(2, 16)] = own_f1
    pack(own_f1, xs1f, 8, 2)
    copies_f1 = x_copies(xs1f, xr1f, 26) + z_copies(f1, 16, 2, 32)
    start(copies_f1)

    gather_turn(0)
    wait(copies_b1)
    join(b1, xr1b, 16, 3, 8, 3)
    w1[...] = weights(b1[...], 1)

    wait(copies_f1)
    join(f1, xr1f, 16, 2, 8, 2)
    r1 = begin_level(b1, f1, w1, u1, v1, 16, 1)
    own_f2 = 0.5 * coarsen(r1, y1, 1)
    own_f2 = jnp.where(iota(own_f2.shape, 2) < half, own_f2, 0.0)
    f2[pl.ds(2, 8)] = own_f2
    pack(own_f2, xs2f, 16, 4)
    copies_f2 = x_copies(xs2f, xr2f, 34) + z_copies(f2, 8, 2, 40)
    start(copies_f2)

    wait(copies_b2)
    join(b2, xr2b, 8, 3, 16, 6)
    w2[...] = weights(b2[...], 2)

    wait(copies_f2)
    join(f2, xr2f, 8, 2, 16, 4)
    r2 = begin_level(b2, f2, w2, u2, v2, 8, 2)
    gather_start(0.5 * coarsen(r2, y2, 2), 1)
    gather_turn(1)

    zz = iota((vn, 8, lanes_n), 2) % nz3
    not_top, not_bottom = zz < nz3 - 1, zz > 0

    def around3(p):
        return (
            jnp.concatenate([p[1:], turn(p[:1], 7, 1)], 0)
            + jnp.concatenate([turn(p[vn - 1:], 1, 1), p[:vn - 1]], 0)
            + turn(p, nz3, 2) + turn(p, lanes_n - nz3, 2)
            + jnp.where(not_top, turn(p, lanes_n - 1, 2), 0.0)
            + jnp.where(not_bottom, turn(p, 1, 2), 0.0)
        )

    def total3(x):
        tile = jnp.sum(x, axis=0)
        return jnp.sum(jnp.sum(tile, axis=0, keepdims=True), axis=1, keepdims=True)

    coarse_b = gather_end(0)
    b3[...] = coarse_b
    coarse_d = 3.0 * coarse_b + 0.5 * around3(coarse_b)
    d3[...] = coarse_d
    i3[...] = 1.0 / coarse_d

    coarse_f = gather_end(1)
    r3[...] = coarse_f
    first_p = coarse_f * i3[...]
    p3[...] = first_p
    s3[...] = jnp.zeros((vn, 8, lanes_n), F32)

    def iterate(n, rz):
        p = p3[...]
        b = b3[...]
        q = d3[...] * p - 0.5 * (b * around3(p) + around3(b * p))
        alpha = rz / total3(p * q)
        s3[...] = s3[...] + alpha * p
        r = r3[...] - alpha * q
        r3[...] = r
        scaled = r * i3[...]
        new = total3(r * scaled)
        p3[...] = scaled + (new / rz) * p
        return new

    lax.fori_loop(0, SWEEPS, iterate, total3(coarse_f * first_p))

    l_at, k_at = iota((128, 8 * vn), 0), iota((128, 8 * vn), 1)
    relative = jnp.where(l_at < 124, l_at // 4, -1)
    wanted = lax.rem(4 * my_start + relative + 8 * vn, 8 * vn)
    from_x = ones_where((k_at % 8) * vn + k_at // 8 == wanted)
    by_lane = pick_left(from_x, s3[...].reshape(8 * vn, lanes_n))
    q_at, r_at = iota((48, lanes_n), 0), iota((48, lanes_n), 1)
    z_at = 4 * sub + q_at // 8 - 1
    from_row = ones_where(
        (r_at == ((q_at % 8) // 2) * nz3 + z_at) & (z_at >= 0) & (z_at < nz3)
    )
    e3 = pick_left_t(from_row, by_lane).reshape(6, 1, 8, 128)
    e3 = jnp.broadcast_to(e3, (6, 2, 8, 128)).reshape(12, 8, 128)

    e2 = end_level(b2, f2, w2, u2[...] + e3, 8, 2)
    e1x[:, pl.ds(0, 8, stride=2), :] = e2
    e1x[:, pl.ds(1, 8, stride=2), :] = e2
    grown = jnp.broadcast_to(e1x[...].reshape(10, 1, 16, 128), (10, 2, 16, 128))
    e1 = end_level(b1, f1, w1, u1[...] + grown.reshape(20, 16, 128), 16, 1)

    si, sc = iota((128, 256), 0), iota((128, 256), 1)
    stretch = ones_where(
        ((sc < width) & (si == sc // 2))
        | ((sc == 128) & (si == 127))
        | ((sc == 128 + width - 1) & (si == half))
    )
    wide = pick_right(e1.reshape(288, 128), stretch)
    main = wide[:, :128].reshape(18, 16, 128)
    side = wide[:, 128:].reshape(18, 16, 128)
    e0m[:, pl.ds(0, 16, stride=2), :] = main
    e0m[:, pl.ds(1, 16, stride=2), :] = main
    e0g[:, pl.ds(0, 16, stride=2), :] = side
    e0g[:, pl.ds(1, 16, stride=2), :] = side

    def add_plane(e, carry):
        u = u0[e] + e0m[(e + 1) // 2]
        u0[e] = u
        v0[e] = b0[e + 1] * u
        return carry

    lax.fori_loop(0, 34, add_plane, 0)

    def finish(z, carry):
        shift = lax.rem(128 - 4 * z, 128)
        ends = jnp.where(edge, turn(ghost_c, shift, 1), 0.0)
        ends = ends + turn(ghost_k, shift, 1) * e0g[z // 2 + 1]
        gain = pull(z + 1) + ends
        u = REST * u0[z + 1] + w0[z + 1] * (f0[z + 1] + 0.5 * gain)
        out[z] = jnp.where(live, u, 0.0)
        return carry

    lax.fori_loop(0, 32, finish, 0)


def per_device(nb, ns, source, beta, counts):
    lanes_n = 16 * ns

    def vmem(*shape, dtype=F32):
        return pltpu.VMEM(shape, dtype)

    def coarse():
        return vmem(nb, 8, lanes_n)

    scratch = [
        vmem(36, 32, 128), vmem(34, 32, 128), vmem(34, 32, 128), vmem(34, 32, 128),
        vmem(34, 32, 128), vmem(16, 32, 128), vmem(2, 32, 128), vmem(2, 3, 2, 32, 128),
        vmem(18, 32, 128), vmem(18, 32, 128),
        vmem(22, 16, 128), vmem(20, 16, 128), vmem(20, 16, 128), vmem(20, 16, 128),
        vmem(20, 16, 128), vmem(16, 128), vmem(2, 3, 16, 128), vmem(16, 128), vmem(2, 3, 16, 128), vmem(8, 16, 128),
        vmem(10, 16, 128),
        vmem(14, 8, 128), vmem(12, 8, 128), vmem(12, 8, 128), vmem(12, 8, 128),
        vmem(12, 8, 128), vmem(8, 128), vmem(2, 3, 8, 128), vmem(8, 128), vmem(2, 3, 8, 128), vmem(4, 8, 128),
        vmem(32, 128), vmem(128, lanes_n), vmem(2, 16, lanes_n), vmem(2, ns, 16, lanes_n),
        vmem(2, 16, lanes_n), vmem(2, nb, 16, lanes_n), vmem(8 * nb, 16 * nb, dtype=BF16),
        coarse(), coarse(), coarse(), coarse(), coarse(), coarse(), coarse(),
        pltpu.SemaphoreType.DMA((2,)),
        pltpu.SemaphoreType.DMA((42,)), pltpu.SemaphoreType.DMA((42,)),
        pltpu.SemaphoreType.DMA((2, ns)), pltpu.SemaphoreType.DMA((2, ns)),
        pltpu.SemaphoreType.DMA((2, nb)), pltpu.SemaphoreType.DMA((2, nb)),
    ]
    return pl.pallas_call(
        functools.partial(kernel, nb, ns),
        out_shape=jax.ShapeDtypeStruct(source.shape, F32),
        in_specs=[
            pl.BlockSpec(memory_space=pltpu.SMEM),
            pl.BlockSpec(memory_space=pl.ANY),
            pl.BlockSpec(memory_space=pl.ANY),
        ],
        out_specs=pl.BlockSpec(memory_space=pltpu.VMEM),
        scratch_shapes=scratch,
        compiler_params=pltpu.CompilerParams(
            collective_id=0, has_side_effects=True, vmem_limit_bytes=32 * 1024 * 1024
        ),
    )(counts, source, beta)


def solution(mesh):
    in_specs = (P("sub", None, "box"), P("sub", None, "box"), P())
    out_specs = P("sub", None, "box")
    return jax.shard_map(
        functools.partial(per_device, mesh.shape["box"], mesh.shape["sub"]),
        mesh=mesh, in_specs=in_specs, out_specs=out_specs, check_vma=False,
    )
```

```python
import functools
import jax
import jax.numpy as jnp
from jax import lax
from jax.experimental import pallas as pl
from jax.experimental.pallas import tpu as pltpu
from jax.sharding import PartitionSpec as P

CAP = 4
SWEEPS = 8
OMEGA = 0.8
REST = 0.2
TINY = 1e-20
F32 = jnp.float32
BF16 = jnp.bfloat16
MESH = pl.DeviceIdType.MESH


def split(x):
    high = x.astype(BF16)
    rest = x - high.astype(F32)
    middle = rest.astype(BF16)
    low = (rest - middle.astype(F32)).astype(BF16)
    return (high, middle, low)


def pick_right(x, chosen):
    return sum(jnp.dot(part, chosen, preferred_element_type=F32) for part in split(x))


def pick_left(chosen, x):
    return sum(jnp.dot(chosen, part, preferred_element_type=F32) for part in split(x))


def pick_left_t(chosen, x):
    return sum(
        lax.dot_general(chosen, part, (((1,), (1,)), ((), ())), preferred_element_type=F32)
        for part in split(x)
    )


def ones_where(mask):
    return jnp.where(mask, 1.0, 0.0).astype(BF16)


def iota(shape, dim):
    return lax.broadcasted_iota(jnp.int32, shape, dim)


def turn(x, shift, axis):
    return pltpu.roll(x, shift, axis)


def around(x, step):
    rows = x.shape[-2]
    ax, ay = x.ndim - 1, x.ndim - 2
    return (
        turn(x, step, ax) + turn(x, 128 - step, ax) + turn(x, 1, ay) + turn(x, rows - 1, ay)
    )


def kernel(
    nb, ns,
    counts, source, beta, out,
    b0, f0, u0, w0, r0, kx, ky, rs, xs0, xr0, e0m, e0x, e0y, c0, cx, cy, cz,
    b1, f1, u1, v1, w1, xs1b, xr1b, xs1f, xr1f, y1, e1x,
    b2, f2, u2, v2, w2, xs2b, xr2b, xs2f, xr2f, y2,
    t3, tx, xa, ga, xb, gb_all, onehot, kx3, ky3, kz3, d3, i3, p3, r3, s3,
    in_sem, send_sem, recv_sem, zsend, zrecv, bsend, brecv,
):
    lanes_n = 16 * ns
    nz3 = 4 * ns
    vn = nb
    me, sub = lax.axis_index("box"), lax.axis_index("sub")
    left, right = lax.rem(me + nb - 1, nb), lax.rem(me + 1, nb)
    down, up = lax.rem(sub + ns - 1, ns), lax.rem(sub + 1, ns)
    floor, roof = sub == 0, sub == ns - 1

    get_b = pltpu.make_async_copy(beta, b0.at[pl.ds(2, 32)], in_sem.at[0])
    get_f = pltpu.make_async_copy(source, f0.at[pl.ds(1, 32)], in_sem.at[1])
    get_b.start()
    get_f.start()

    barrier = pltpu.get_barrier_semaphore()

    def greet_sub(k, carry):
        pl.semaphore_signal(
            barrier, inc=1, device_id=(me, lax.rem(sub + k, ns)), device_id_type=MESH
        )
        return carry

    def greet_box(k, carry):
        pl.semaphore_signal(
            barrier, inc=1, device_id=(lax.rem(me + k, nb), sub), device_id_type=MESH
        )
        return carry

    lax.fori_loop(1, ns, greet_sub, 0)
    lax.fori_loop(1, nb, greet_box, 0)
    for there in (left, right):
        for level in (down, up):
            pl.semaphore_signal(barrier, inc=1, device_id=(there, level), device_id_type=MESH)

    width = 32 * counts[me]
    width_left = 32 * counts[left]
    half = width // 2
    half_left = width_left // 2
    kk = iota((1, nb * 16), 1)
    kd, kj = kk // 16, kk % 16

    def place(d, carry):
        where_from, begin, mine = carry
        here = counts[d]
        value = jnp.where(kj < 4 * here, 4 * begin + kj, -1)
        where_from = jnp.where(kd == d, value, where_from)
        mine = jnp.where(d == me, begin, mine)
        return where_from, begin + here, mine

    where_from, _, my_start = lax.fori_loop(
        0, nb, place, (jnp.full((1, nb * 16), -1, jnp.int32), jnp.int32(0), jnp.int32(0))
    )
    row = iota((8 * vn, nb * 16), 0)
    onehot[...] = ones_where((row % 8) * vn + row // 8 == where_from)

    lane = iota((32, 128), 1)
    live = lane < width
    edge = (lane == 0) | (lane == width - 1)
    edge_two = (lane < 2) | ((lane >= width - 2) & live)
    inner = lane < width - 1

    ll = iota((128, 128), 0)
    lc = iota((128, 128), 1)
    squeeze = ones_where((ll // 2 == lc) & (ll < width))

    get_b.wait()
    get_f.wait()

    def each(count, first, last, act):
        def body(n, carry):
            for k in range(count):
                act(first + n * count + k)
            return carry
        lax.fori_loop(0, (last - first) // count, body, 0)

    def load_planes(n, carry):
        tb, tf = carry
        for k in range(4):
            z = 4 * n + k
            b = jnp.where(live, b0[z + 2], 0.0)
            f = jnp.where(live, f0[z + 1], 0.0)
            b0[z + 2] = b
            f0[z + 1] = f
            tb = tb + turn(jnp.where(edge_two, b, 0.0), 4 * z, 1)
            tf = tf + turn(jnp.where(edge, f, 0.0), 4 * z, 1)
        return tb, tf

    zero_tile = jnp.zeros((32, 128), F32)
    tb, tf = lax.fori_loop(0, 8, load_planes, (zero_tile, zero_tile))
    xs0[0] = tb
    xs0[1] = tf


    def squeeze_level0():
        both = rs[:, pl.ds(0, 16, stride=2), :] + rs[:, pl.ds(1, 16, stride=2), :]
        return pick_right(both.reshape(256, 128), squeeze).reshape(16, 16, 128)

    def coarsen(x, scratch, step):
        planes, rows, _ = x.shape
        pairs = x.reshape(planes // 2, 2, rows, 128)
        scratch[...] = pairs[:, 0] + pairs[:, 1]
        y = (
            scratch[:, pl.ds(0, rows // 2, stride=2), :]
            + scratch[:, pl.ds(1, rows // 2, stride=2), :]
        )
        odd = (iota(y.shape, 2) // step) % 2 == 1
        return y + jnp.where(odd, turn(y, step, 2), turn(y, 128 - step, 2))

    def pack(x, tile_ref, group, reach):
        planes, rows, _ = x.shape
        at = iota((rows, 128), 1)
        keep = (at < reach) | ((at >= half - reach) & (at < half))
        total = jnp.zeros((rows, 128), F32)
        for z in range(planes):
            total = total + turn(jnp.where(keep, x[z], 0.0), group * z, 1)
        tile_ref[...] = total

    def to_slots(x):
        for z in range(4):
            t3[pl.ds(z, 4, stride=8), :] = x[z]
            t3[pl.ds(z + 4, 4, stride=8), :] = x[z]
        tiles = t3[...].reshape(4, 1, 8, 128)
        tiles = jnp.broadcast_to(tiles, (4, ns // 2, 8, 128)).reshape(lanes_n, 128)
        tx[...] = jnp.transpose(tiles)
        return tx[pl.ds(0, 16, stride=4), :]

    def pair_b(k):
        rs[k] = b0[2 * k + 2] + b0[2 * k + 3]

    each(4, 0, 16, pair_b)
    own_b1 = 0.125 * squeeze_level0()
    b1[pl.ds(3, 16)] = own_b1
    pack(own_b1, xs1b, 8, 3)
    own_b2 = 0.125 * coarsen(own_b1, y1, 1)
    b2[pl.ds(3, 8)] = own_b2
    pack(own_b2, xs2b, 16, 6)

    def couple(e):
        b = b0[e + 1]
        px = jnp.where(inner, b + turn(b, 127, 1), 0.0)
        py = b + turn(b, 31, 0)
        kx[e] = px
        ky[e] = py
        return px + turn(px, 1, 1) + py + turn(py, 1, 0) + (b0[e] + b) + (b + b0[e + 2])

    def start_plane(e, more=0.0):
        w = (2.0 * OMEGA) / jnp.maximum(couple(e) + more, TINY)
        w0[e] = w
        u0[e] = w * f0[e]

    def pull(e):
        u, px, py, b = u0[e], kx[e], ky[e], b0[e + 1]
        return (
            px * turn(u, 127, 1) + turn(px * u, 1, 1) + py * turn(u, 31, 0) + turn(py * u, 1, 0)
            + (b0[e] + b) * u0[e - 1] + (b + b0[e + 2]) * u0[e + 1]
        )

    def residual(z):
        r = REST * f0[z + 1] + 0.5 * pull(z + 1)
        r0[z] = r
        return r

    def pair_r(k):
        rs[k] = residual(2 * k) + residual(2 * k + 1)

    each(5, 2, 32, start_plane)

    pl.semaphore_wait(barrier, (ns - 1) + (nb - 1) + 4)

    def x_copies(src, dst, base):
        made = []
        for side, there in ((0, right), (1, left)):
            for slot, level in ((0, up), (1, sub), (2, down)):
                n = base + side * 3 + slot
                made.append(
                    pltpu.make_async_remote_copy(
                        src_ref=src, dst_ref=dst.at[side, slot],
                        send_sem=send_sem.at[n], recv_sem=recv_sem.at[n],
                        device_id=(there, level), device_id_type=MESH,
                    )
                )
        return made

    def z_copies(ref, own, halo, base):
        made = []
        for n, (begin, to, level) in enumerate(
            ((own, 0, up), (halo, own + halo, down))
        ):
            made.append(
                pltpu.make_async_remote_copy(
                    src_ref=ref.at[pl.ds(begin, halo)], dst_ref=ref.at[pl.ds(to, halo)],
                    send_sem=send_sem.at[base + n], recv_sem=recv_sem.at[base + n],
                    device_id=(me, level), device_id_type=MESH,
                )
            )
        return made

    def start(copies):
        for copy in copies:
            copy.start()

    def wait(copies):
        for copy in copies:
            copy.wait()

    copies0 = x_copies(xs0, xr0, 0) + z_copies(b0, 32, 2, 6) + z_copies(f0, 32, 1, 8)
    start(copies0)

    def sub_copy(k, which, slot):
        return pltpu.make_async_remote_copy(
            src_ref=xa.at[which], dst_ref=ga.at[which, slot],
            send_sem=zsend.at[which, k], recv_sem=zrecv.at[which, k],
            device_id=(me, lax.rem(sub + k, ns)), device_id_type=MESH,
        )

    def box_copy(k, which, slot):
        return pltpu.make_async_remote_copy(
            src_ref=xb.at[which], dst_ref=gb_all.at[which, slot],
            send_sem=bsend.at[which, k], recv_sem=brecv.at[which, k],
            device_id=(lax.rem(me + k, nb), sub), device_id_type=MESH,
        )

    def send_all(make, which, mine, count):
        def body(k, carry):
            make(k, which, mine).start()
            return carry
        lax.fori_loop(1, count, body, 0)

    def wait_all(make, which, mine, count):
        def body(k, carry):
            copy = make(k, which, lax.rem(mine - k + count, count))
            copy.wait_send()
            copy.wait_recv()
            return carry
        lax.fori_loop(1, count, body, 0)

    def gather_start(x, which):
        tile = to_slots(x)
        xa[which] = tile
        ga[which, sub] = tile
        send_all(sub_copy, which, sub, ns)

    def gather_turn(which):
        wait_all(sub_copy, which, sub, ns)
        at = (iota((16, lanes_n), 1) // 4) % ns
        tile = jnp.zeros((16, lanes_n), F32)
        for k in range(ns):
            tile = jnp.where(at == k, ga[which, k], tile)
        xb[which] = tile
        gb_all[which, me] = tile
        send_all(box_copy, which, me, nb)

    def gather_end(which):
        wait_all(box_copy, which, me, nb)
        rows = gb_all[which].reshape(nb * 16, lanes_n)
        return pick_left(onehot[...], rows).reshape(vn, 8, lanes_n)

    copies_b1 = x_copies(xs1b, xr1b, 10) + z_copies(b1, 16, 3, 16)
    start(copies_b1)
    copies_b2 = x_copies(xs2b, xr2b, 18) + z_copies(b2, 8, 3, 24)
    start(copies_b2)
    gather_start(0.125 * coarsen(own_b2, y2, 2), 0)

    each(2, 1, 15, pair_r)
    wait(copies0)

    @pl.when(floor)
    def _():
        b0[pl.ds(0, 2)] = jnp.zeros((2, 32, 128), F32)
        f0[pl.ds(0, 1)] = jnp.zeros((1, 32, 128), F32)

    @pl.when(roof)
    def _():
        b0[pl.ds(34, 2)] = jnp.zeros((2, 32, 128), F32)
        f0[pl.ds(33, 1)] = jnp.zeros((1, 32, 128), F32)

    quarter = lane % 4
    group = lane // 4
    q0, q3 = quarter == 0, quarter == 3
    turn_l1 = lax.rem(129 - width_left + 128, 128)
    turn_l2 = lax.rem(130 - width_left + 128, 128)

    def ghost(slot, which, near_by):
        from_left, from_right = xr0[0, slot, which], xr0[1, slot, which]
        shift_l = turn_l1 if near_by == 1 else turn_l2
        return jnp.where(
            q0, turn(from_left, shift_l, 1),
            jnp.where(q3, turn(from_right, lax.rem(width - near_by, 128), 1), 0.0),
        )

    ghost_b = ghost(1, 0, 1)
    ghost_b_low = jnp.where(floor, 0.0, ghost(0, 0, 1))
    ghost_b_high = jnp.where(roof, 0.0, ghost(2, 0, 1))
    ghost_b_far = ghost(1, 0, 2)
    ghost_f = ghost(1, 1, 1)
    own_edge = jnp.where(q0 | q3, tb, 0.0)
    turned = width // 4 - 1
    first_z = (q0 & (group == 0)) | (q3 & (group == turned))
    last_z = (q0 & (group == 31)) | (q3 & (group == lax.rem(31 + turned, 32)))

    def beside(tile, low, high):
        return (
            turn(tile, 1, 0) + turn(tile, 31, 0)
            + turn(jnp.where(first_z, high, tile), 124, 1)
            + turn(jnp.where(last_z, low, tile), 4, 1)
        )

    ghost_k = ghost_b + own_edge
    ghost_sum = 6.0 * ghost_b + ghost_b_far + own_edge
    ghost_sum = ghost_sum + beside(ghost_b, ghost_b_low, ghost_b_high)
    ghost_u = (2.0 * OMEGA) * ghost_f / jnp.maximum(ghost_sum, TINY)

    below = turn(jnp.where(edge, b0[1], 0.0), 124, 1)
    above = jnp.where(edge, b0[34], 0.0)
    edge_part = 6.0 * own_edge + beside(own_edge, below, above)
    edge_part = edge_part + jnp.where(q0, turn(tb, 127, 1), turn(tb, 1, 1))
    without = (edge_part - own_edge)
    edge_w = (2.0 * OMEGA) / jnp.maximum(without + ghost_k, TINY)
    edge_w = jnp.where(q0 | q3, edge_w, 0.0)
    drift = edge_w * tf - jnp.where(
        q0 | q3, (2.0 * OMEGA) * tf / jnp.maximum(without, TINY), 0.0
    )
    drift_v = own_edge * drift
    gap = own_edge * beside(drift, 0.0, 0.0) + beside(drift_v, 0.0, 0.0) + ghost_k * ghost_u
    gap = jnp.where(
        q0 | q3, gap,
        jnp.where(
            quarter == 1, (tb + turn(own_edge, 1, 1)) * turn(drift, 1, 1),
            (tb + turn(own_edge, 127, 1)) * turn(drift, 127, 1),
        ),
    )
    gap = 0.5 * gap
    gap_pair = gap + turn(gap, 124, 1)

    def back(tile, z):
        return turn(tile, lax.rem(128 - 4 * z, 128), 1)

    start_plane(0, jnp.where(edge, turn(ghost_b_low + below, 4, 1), 0.0))
    start_plane(1)
    start_plane(32)
    start_plane(33, jnp.where(edge, ghost_b_high + above, 0.0))
    pair_r(0)
    pair_r(15)

    def mend(k):
        rs[k] = rs[k] + jnp.where(edge_two, back(gap_pair, 2 * k), 0.0)

    each(4, 0, 16, mend)

    def join(ref, xr, own, halo, gr, reach):
        rows = ref.shape[1]
        at = iota((rows, 128), 1)
        inside = at < half
        keep = ((at >= half) & (at < half + reach)) | (at >= 128 - reach)
        sub_at = at % gr
        tiles = []
        for slot in range(3):
            from_left = turn(xr[0, slot], lax.rem(256 - half_left, 128), 1)
            from_right = turn(xr[1, slot], half, 1)
            tiles.append(
                jnp.where(
                    sub_at >= gr - reach, from_left, jnp.where(sub_at < reach, from_right, 0.0)
                )
            )
        for z in range(-halo, own + halo):
            slot = 0 if z < 0 else (2 if z >= own else 1)
            there = z % own
            plane = jnp.where(
                inside, ref[z + halo],
                jnp.where(keep, turn(tiles[slot], (128 - gr * there) % 128, 1), 0.0),
            )
            if z < 0:
                plane = jnp.where(floor, 0.0, plane)
            if z >= own:
                plane = jnp.where(roof, 0.0, plane)
            ref[z + halo] = plane

    def weights(b, step):
        n = b.shape[0]
        middle = b[1:n - 1]
        total = around(middle, step) + b[:n - 2] + b[2:]
        return OMEGA / jnp.maximum(3.0 * middle + 0.5 * total, TINY)

    def gain_of(b, u, v, step):
        n = u.shape[0]
        return b * (around(u[1:n - 1], step) + u[:n - 2] + u[2:]) + (
            around(v[1:n - 1], step) + v[:n - 2] + v[2:]
        )

    def begin_level(b_ref, f_ref, w_ref, u_ref, v_ref, own, step):
        w = w_ref[...]
        u = w * f_ref[...]
        u_ref[...] = u
        v = b_ref[pl.ds(1, own + 4)] * u
        v_ref[...] = v
        b = b_ref[pl.ds(3, own)]
        gain = gain_of(b, u[1:own + 3], v[1:own + 3], step)
        return REST * f_ref[pl.ds(2, own)] + 0.5 * gain

    def end_level(b_ref, f_ref, w_ref, u, own, step):
        v = b_ref[pl.ds(1, own + 4)] * u
        b = b_ref[pl.ds(2, own + 2)]
        gain = gain_of(b, u, v, step)
        e = REST * u[1:own + 3] + w_ref[pl.ds(1, own + 2)] * (
            f_ref[pl.ds(1, own + 2)] + 0.5 * gain
        )
        return jnp.concatenate([
            jnp.where(floor, 0.0, e[:1]), e[1:own + 1], jnp.where(roof, 0.0, e[own + 1:])
        ], 0)

    own_f1 = 0.5 * squeeze_level0()
    f1[pl.ds(2, 16)] = own_f1
    pack(own_f1, xs1f, 8, 2)
    copies_f1 = x_copies(xs1f, xr1f, 26) + z_copies(f1, 16, 2, 32)
    start(copies_f1)

    def prepare(z, odd):
        e = z + 1
        w = jnp.where(edge, back(edge_w, z), w0[e])
        r = r0[z] + jnp.where(edge_two, back(gap, z), 0.0)
        out[z] = jnp.where(live, w * (f0[e] + r), 0.0)
        px, py, b = kx[e], ky[e], b0[e + 1]
        px_low, py_low = turn(px, 1, 1), turn(py, 1, 0)
        pz_low, pz = b0[e] + b, b + b0[e + 2]
        even_x, even_y = lane % 2 == 0, iota((32, 128), 0) % 2 == 0
        rim = jnp.where(edge, back(ghost_k, z), 0.0)
        same = jnp.where(even_x, px, px_low) + jnp.where(even_y, py, py_low)
        same = same + (pz_low if odd else pz)
        w = jnp.where(live, 0.5 * w, 0.0)
        c0[z] = REST + w * same
        cx[z] = w * (jnp.where(even_x, px_low, px) + rim)
        cy[z] = w * jnp.where(even_y, py_low, py)
        cz[z] = w * (pz if odd else pz_low)

    def prepare_pair(k):
        prepare(2 * k, False)
        prepare(2 * k + 1, True)

    gather_turn(0)
    each(1, 0, 8, prepare_pair)
    wait(copies_b1)
    join(b1, xr1b, 16, 3, 8, 3)
    w1[...] = weights(b1[...], 1)

    wait(copies_f1)
    join(f1, xr1f, 16, 2, 8, 2)
    r1 = begin_level(b1, f1, w1, u1, v1, 16, 1)
    own_f2 = 0.5 * coarsen(r1, y1, 1)
    own_f2 = jnp.where(iota(own_f2.shape, 2) < half, own_f2, 0.0)
    f2[pl.ds(2, 8)] = own_f2
    pack(own_f2, xs2f, 16, 4)
    copies_f2 = x_copies(xs2f, xr2f, 34) + z_copies(f2, 8, 2, 40)
    start(copies_f2)

    each(1, 8, 16, prepare_pair)
    wait(copies_b2)
    join(b2, xr2b, 8, 3, 16, 6)
    w2[...] = weights(b2[...], 2)

    wait(copies_f2)
    join(f2, xr2f, 8, 2, 16, 4)
    r2 = begin_level(b2, f2, w2, u2, v2, 8, 2)
    gather_start(0.5 * coarsen(r2, y2, 2), 1)
    gather_turn(1)

    not_top = iota((vn, 8, lanes_n), 2) % nz3 < nz3 - 1

    def next_x(p):
        return jnp.concatenate([p[1:], turn(p[:1], 7, 1)], 0)

    def last_x(p):
        return jnp.concatenate([turn(p[vn - 1:], 1, 1), p[:vn - 1]], 0)

    def total3(x):
        tile = jnp.sum(x, axis=0)
        return jnp.sum(jnp.sum(tile, axis=0, keepdims=True), axis=1, keepdims=True)

    coarse_b = gather_end(0)
    px = 0.5 * (coarse_b + next_x(coarse_b))
    py = 0.5 * (coarse_b + turn(coarse_b, lanes_n - nz3, 2))
    pz = jnp.where(not_top, 0.5 * (coarse_b + turn(coarse_b, lanes_n - 1, 2)), 0.0)
    ends = jnp.where(
        not_top, 0.0, 0.5 * coarse_b
    ) + jnp.where(iota((vn, 8, lanes_n), 2) % nz3 == 0, 0.5 * coarse_b, 0.0)
    kx3[...] = px
    ky3[...] = py
    kz3[...] = pz
    coarse_d = px + last_x(px) + py + turn(py, nz3, 2) + pz + turn(pz, 1, 2) + ends
    d3[...] = coarse_d
    i3[...] = 1.0 / coarse_d

    coarse_f = gather_end(1)
    r3[...] = coarse_f
    first_p = coarse_f * i3[...]
    p3[...] = first_p
    s3[...] = jnp.zeros((vn, 8, lanes_n), F32)

    def image(p):
        px, py, pz = kx3[...], ky3[...], kz3[...]
        return d3[...] * p - (
            px * next_x(p) + last_x(px * p)
            + py * turn(p, lanes_n - nz3, 2) + turn(py * p, nz3, 2)
            + pz * turn(p, lanes_n - 1, 2) + turn(pz * p, 1, 2)
        )

    def iterate(n, rz):
        p = p3[...]
        q = image(p)
        alpha = rz / total3(p * q)
        s3[...] = s3[...] + alpha * p
        r = r3[...] - alpha * q
        r3[...] = r
        scaled = r * i3[...]
        new = total3(r * scaled)
        p3[...] = scaled + (new / rz) * p
        return new

    rz = lax.fori_loop(0, SWEEPS - 1, iterate, total3(coarse_f * first_p))
    last_p = p3[...]
    solved = s3[...] + (rz / total3(last_p * image(last_p))) * last_p

    l_at, k_at = iota((128, 8 * vn), 0), iota((128, 8 * vn), 1)
    relative = jnp.where(l_at < 124, l_at // 4, -1)
    wanted = lax.rem(4 * my_start + relative + 8 * vn, 8 * vn)
    from_x = ones_where((k_at % 8) * vn + k_at // 8 == wanted)
    by_lane = pick_left(from_x, solved.reshape(8 * vn, lanes_n))
    q_at, r_at = iota((48, lanes_n), 0), iota((48, lanes_n), 1)
    z_at = 4 * sub + q_at // 8 - 1
    from_row = ones_where(
        (r_at == ((q_at % 8) // 2) * nz3 + z_at) & (z_at >= 0) & (z_at < nz3)
    )
    e3 = pick_left_t(from_row, by_lane).reshape(6, 1, 8, 128)
    e3 = jnp.broadcast_to(e3, (6, 2, 8, 128)).reshape(12, 8, 128)

    e2 = end_level(b2, f2, w2, u2[...] + e3, 8, 2)
    e1x[:, pl.ds(0, 8, stride=2), :] = e2
    e1x[:, pl.ds(1, 8, stride=2), :] = e2
    grown = jnp.broadcast_to(e1x[...].reshape(10, 1, 16, 128), (10, 2, 16, 128))
    e1 = end_level(b1, f1, w1, u1[...] + grown.reshape(20, 16, 128), 16, 1)

    si, sc = iota((128, 256), 0), iota((128, 256), 1)
    sx = sc - 128
    step = jnp.where(sx % 2 == 0, sx // 2 - 1, sx // 2 + 1)
    step = jnp.where(step < 0, 127, step)
    stretch = ones_where(
        ((sc < width) & (si == sc // 2)) | ((sx >= 0) & (sx < width) & (si == step))
    )
    wide = pick_right(e1.reshape(288, 128), stretch)
    main = wide[:, :128].reshape(18, 16, 128)
    side = wide[:, 128:].reshape(18, 16, 128)
    e0m[:, pl.ds(0, 16, stride=2), :] = main
    e0m[:, pl.ds(1, 16, stride=2), :] = main
    e0x[:, pl.ds(0, 16, stride=2), :] = side
    e0x[:, pl.ds(1, 16, stride=2), :] = side
    e0y[:, pl.ds(0, 16, stride=2), :] = turn(main, 1, 1)
    e0y[:, pl.ds(1, 16, stride=2), :] = turn(main, 15, 1)

    def finish_pair(k):
        e, ex, ey = e0m[k + 1], e0x[k + 1], e0y[k + 1]
        for z, ez in ((2 * k, e0m[k]), (2 * k + 1, e0m[k + 2])):
            out[z] = out[z] + c0[z] * e + cx[z] * ex + cy[z] * ey + cz[z] * ez

    each(2, 0, 16, finish_pair)


def per_device(nb, ns, source, beta, counts):
    lanes_n = 16 * ns

    def vmem(*shape, dtype=F32):
        return pltpu.VMEM(shape, dtype)

    def coarse():
        return vmem(nb, 8, lanes_n)

    scratch = [
        vmem(36, 32, 128), vmem(34, 32, 128), vmem(34, 32, 128), vmem(34, 32, 128),
        vmem(32, 32, 128), vmem(34, 32, 128), vmem(34, 32, 128),
        vmem(16, 32, 128), vmem(2, 32, 128), vmem(2, 3, 2, 32, 128),
        vmem(18, 32, 128), vmem(18, 32, 128), vmem(18, 32, 128),
        vmem(32, 32, 128), vmem(32, 32, 128), vmem(32, 32, 128), vmem(32, 32, 128),
        vmem(22, 16, 128), vmem(20, 16, 128), vmem(20, 16, 128), vmem(20, 16, 128),
        vmem(20, 16, 128), vmem(16, 128), vmem(2, 3, 16, 128), vmem(16, 128), vmem(2, 3, 16, 128), vmem(8, 16, 128),
        vmem(10, 16, 128),
        vmem(14, 8, 128), vmem(12, 8, 128), vmem(12, 8, 128), vmem(12, 8, 128),
        vmem(12, 8, 128), vmem(8, 128), vmem(2, 3, 8, 128), vmem(8, 128), vmem(2, 3, 8, 128), vmem(4, 8, 128),
        vmem(32, 128), vmem(128, lanes_n), vmem(2, 16, lanes_n), vmem(2, ns, 16, lanes_n),
        vmem(2, 16, lanes_n), vmem(2, nb, 16, lanes_n), vmem(8 * nb, 16 * nb, dtype=BF16),
        coarse(), coarse(), coarse(), coarse(), coarse(), coarse(), coarse(), coarse(),
        pltpu.SemaphoreType.DMA((2,)),
        pltpu.SemaphoreType.DMA((42,)), pltpu.SemaphoreType.DMA((42,)),
        pltpu.SemaphoreType.DMA((2, ns)), pltpu.SemaphoreType.DMA((2, ns)),
        pltpu.SemaphoreType.DMA((2, nb)), pltpu.SemaphoreType.DMA((2, nb)),
    ]
    return pl.pallas_call(
        functools.partial(kernel, nb, ns),
        out_shape=jax.ShapeDtypeStruct(source.shape, F32),
        in_specs=[
            pl.BlockSpec(memory_space=pltpu.SMEM),
            pl.BlockSpec(memory_space=pl.ANY),
            pl.BlockSpec(memory_space=pl.ANY),
        ],
        out_specs=pl.BlockSpec(memory_space=pltpu.VMEM),
        scratch_shapes=scratch,
        compiler_params=pltpu.CompilerParams(
            collective_id=0, has_side_effects=True, vmem_limit_bytes=62 * 1024 * 1024
        ),
    )(counts, source, beta)


def solution(mesh):
    in_specs = (P("sub", None, "box"), P("sub", None, "box"), P())
    out_specs = P("sub", None, "box")
    return jax.shard_map(
        functools.partial(per_device, mesh.shape["box"], mesh.shape["sub"]),
        mesh=mesh, in_specs=in_specs, out_specs=out_specs, check_vma=False,
    )
```

```python
import functools
import jax
import jax.numpy as jnp
from jax import lax
from jax.experimental import pallas as pl
from jax.experimental.pallas import tpu as pltpu
from jax.sharding import PartitionSpec as P

CAP = 4
SWEEPS = 8
OMEGA = 0.8
REST = 0.2
TINY = 1e-20
F32 = jnp.float32
BF16 = jnp.bfloat16
MESH = pl.DeviceIdType.MESH


def split(x):
    high = x.astype(BF16)
    rest = x - high.astype(F32)
    middle = rest.astype(BF16)
    low = (rest - middle.astype(F32)).astype(BF16)
    return (high, middle, low)


def pick_right(x, chosen):
    return sum(jnp.dot(part, chosen, preferred_element_type=F32) for part in split(x))


def pick_left(chosen, x):
    return sum(jnp.dot(chosen, part, preferred_element_type=F32) for part in split(x))


def pick_left_t(chosen, x):
    return sum(
        lax.dot_general(chosen, part, (((1,), (1,)), ((), ())), preferred_element_type=F32)
        for part in split(x)
    )


def ones_where(mask):
    return jnp.where(mask, 1.0, 0.0).astype(BF16)


def iota(shape, dim):
    return lax.broadcasted_iota(jnp.int32, shape, dim)


def turn(x, shift, axis):
    return pltpu.roll(x, shift, axis)


def around(x, step):
    rows = x.shape[-2]
    ax, ay = x.ndim - 1, x.ndim - 2
    return (
        turn(x, step, ax) + turn(x, 128 - step, ax) + turn(x, 1, ay) + turn(x, rows - 1, ay)
    )


def kernel(
    nb, ns,
    counts, source, beta, out,
    b0, f0, u0, w0, r0, kx, ky, rs, xs0, xr0, xc0, e0m, e0x, e0y, c0, cx, cy, cz,
    b1, f1, u1, w1, xs1b, xr1b, xc1b, xs1f, xr1f, xc1f, y1, e1x,
    b2, f2, u2, w2, y2,
    t3, tx, xa, ga, xb, gb_all, onehot, kx3, ky3, kz3, d3, i3, p3, r3, s3,
    in_sem, send_sem, recv_sem, zsend, zrecv, bsend, brecv,
):
    lanes_n = 16 * ns
    nz3 = 4 * ns
    vn = nb
    me, sub = lax.axis_index("box"), lax.axis_index("sub")
    left, right = lax.rem(me + nb - 1, nb), lax.rem(me + 1, nb)
    down, up = lax.rem(sub + ns - 1, ns), lax.rem(sub + 1, ns)
    floor, roof = sub == 0, sub == ns - 1

    get_b = pltpu.make_async_copy(beta, b0.at[pl.ds(2, 32)], in_sem.at[0])
    get_f = pltpu.make_async_copy(source, f0.at[pl.ds(1, 32)], in_sem.at[1])
    get_b.start()
    get_f.start()

    core, chip, chips = lax.rem(me, 2), me // 2, nb // 2

    def stack_peer(k):
        return 2 * chip + lax.rem(core + k, 2), lax.rem(sub + k // 2, ns)

    def chip_peer(k):
        return 2 * lax.rem(chip + k, chips) + core, sub

    barrier = pltpu.get_barrier_semaphore()

    def greet(peer):
        def body(k, carry):
            pl.semaphore_signal(barrier, inc=1, device_id=peer(k), device_id_type=MESH)
            return carry
        return body

    for there in (left, right):
        for level in (down, sub, up):
            pl.semaphore_signal(barrier, inc=1, device_id=(there, level), device_id_type=MESH)
    lax.fori_loop(1, 2 * ns, greet(stack_peer), 0)
    lax.fori_loop(1, chips, greet(chip_peer), 0)

    width = 32 * counts[me]
    width_left = 32 * counts[left]
    half = width // 2
    half_left = width_left // 2
    kk = iota((1, nb * 16), 1)
    kd, kj = kk // 16, kk % 16

    def place(d, carry):
        where_from, begin, mine = carry
        here = counts[d]
        value = jnp.where(kj < 4 * here, 4 * begin + kj, -1)
        where_from = jnp.where(kd == d, value, where_from)
        mine = jnp.where(d == me, begin, mine)
        return where_from, begin + here, mine

    where_from, _, my_start = lax.fori_loop(
        0, nb, place, (jnp.full((1, nb * 16), -1, jnp.int32), jnp.int32(0), jnp.int32(0))
    )
    row = iota((8 * vn, nb * 16), 0)
    onehot[...] = ones_where((row % 8) * vn + row // 8 == where_from)

    lane = iota((32, 128), 1)
    live = lane < width
    edge = (lane == 0) | (lane == width - 1)
    edge_two = (lane < 2) | ((lane >= width - 2) & live)
    inner = lane < width - 1

    ll = iota((128, 128), 0)
    lc = iota((128, 128), 1)
    squeeze = ones_where((ll // 2 == lc) & (ll < width))

    get_b.wait()
    get_f.wait()

    def each(count, first, last, act):
        def body(n, carry):
            for k in range(count):
                act(first + n * count + k)
            return carry
        lax.fori_loop(0, (last - first) // count, body, 0)

    def load_planes(n, carry):
        tb, tf = carry
        for k in range(4):
            z = 4 * n + k
            b = jnp.where(live, b0[z + 2], 0.0)
            f = jnp.where(live, f0[z + 1], 0.0)
            b0[z + 2] = b
            f0[z + 1] = f
            tb = tb + turn(jnp.where(edge_two, b, 0.0), 4 * z, 1)
            tf = tf + turn(jnp.where(edge, f, 0.0), 4 * z, 1)
        return tb, tf

    zero_tile = jnp.zeros((32, 128), F32)
    tb, tf = lax.fori_loop(0, 8, load_planes, (zero_tile, zero_tile))
    xs0[0] = tb
    xs0[1] = tf


    def squeeze_level0():
        both = rs[:, pl.ds(0, 16, stride=2), :] + rs[:, pl.ds(1, 16, stride=2), :]
        return pick_right(both.reshape(256, 128), squeeze).reshape(16, 16, 128)

    def coarsen(x, scratch, step):
        planes, rows, _ = x.shape
        n = planes // 2
        pairs = x.reshape(n, 2, rows, 128)
        scratch[pl.ds(0, n)] = pairs[:, 0] + pairs[:, 1]
        y = (
            scratch[pl.ds(0, n), pl.ds(0, rows // 2, stride=2), :]
            + scratch[pl.ds(0, n), pl.ds(1, rows // 2, stride=2), :]
        )
        odd = (iota(y.shape, 2) // step) % 2 == 1
        return y + jnp.where(odd, turn(y, step, 2), turn(y, 128 - step, 2))

    def pack(x, tile_ref, reach):
        at = iota((16, 128), 1)
        keep = (at < reach) | ((at >= half - reach) & (at < half))
        for n in range(2):
            total = jnp.zeros((16, 128), F32)
            for z in range(8):
                total = total + turn(jnp.where(keep, x[8 * n + z], 0.0), 16 * z, 1)
            tile_ref[n] = total

    def to_slots(x):
        for z in range(4):
            t3[pl.ds(z, 4, stride=8), :] = x[z]
            t3[pl.ds(z + 4, 4, stride=8), :] = x[z]
        tiles = t3[...].reshape(4, 1, 8, 128)
        tiles = jnp.broadcast_to(tiles, (4, ns // 2, 8, 128)).reshape(lanes_n, 128)
        tx[...] = jnp.transpose(tiles)
        return tx[pl.ds(0, 16, stride=4), :]

    def pair_b(k):
        rs[k] = b0[2 * k + 2] + b0[2 * k + 3]

    each(4, 0, 16, pair_b)
    own_b1 = 0.125 * squeeze_level0()
    b1[pl.ds(6, 16)] = own_b1
    pack(own_b1, xs1b, 6)
    own_b2 = 0.125 * coarsen(own_b1, y1, 1)

    def couple(e):
        b = b0[e + 1]
        px = jnp.where(inner, b + turn(b, 127, 1), 0.0)
        py = b + turn(b, 31, 0)
        kx[e] = px
        ky[e] = py
        return px + turn(px, 1, 1) + py + turn(py, 1, 0) + (b0[e] + b) + (b + b0[e + 2])

    def start_plane(e, more=0.0):
        w = (2.0 * OMEGA) / jnp.maximum(couple(e) + more, TINY)
        w0[e] = w
        u0[e] = w * f0[e]

    def pull(e):
        u, px, py, b = u0[e], kx[e], ky[e], b0[e + 1]
        return (
            px * turn(u, 127, 1) + turn(px * u, 1, 1) + py * turn(u, 31, 0) + turn(py * u, 1, 0)
            + (b0[e] + b) * u0[e - 1] + (b + b0[e + 2]) * u0[e + 1]
        )

    def residual(z):
        r = REST * f0[z + 1] + 0.5 * pull(z + 1)
        r0[z] = r
        return r

    def pair_r(k):
        rs[k] = residual(2 * k) + residual(2 * k + 1)

    each(5, 2, 32, start_plane)

    pl.semaphore_wait(barrier, 6 + (2 * ns - 1) + (chips - 1))

    def x_copies(src, dst, for_up, for_down, corner, base):
        made = []
        for side, there in ((0, right), (1, left)):
            for n, (begin, end, level) in enumerate((
                (src, dst.at[side], sub),
                (for_up, corner.at[side, 0], up),
                (for_down, corner.at[side, 1], down),
            )):
                at = base + side * 3 + n
                made.append(
                    pltpu.make_async_remote_copy(
                        src_ref=begin, dst_ref=end,
                        send_sem=send_sem.at[at], recv_sem=recv_sem.at[at],
                        device_id=(there, level), device_id_type=MESH,
                    )
                )
        return made

    def z_copies(ref, own, halo, base):
        made = []
        for n, (begin, to, level) in enumerate(
            ((own, 0, up), (halo, own + halo, down))
        ):
            made.append(
                pltpu.make_async_remote_copy(
                    src_ref=ref.at[pl.ds(begin, halo)], dst_ref=ref.at[pl.ds(to, halo)],
                    send_sem=send_sem.at[base + n], recv_sem=recv_sem.at[base + n],
                    device_id=(me, level), device_id_type=MESH,
                )
            )
        return made

    def start(copies):
        for copy in copies:
            copy.start()

    def wait(copies):
        for copy in copies:
            copy.wait()

    copies0 = x_copies(xs0, xr0, xs0.at[0], xs0.at[0], xc0, 0) + z_copies(b0, 32, 2, 6) + z_copies(f0, 32, 1, 8)
    start(copies0)

    def stack_copy(k, which, slot):
        return pltpu.make_async_remote_copy(
            src_ref=xa.at[which], dst_ref=ga.at[which, slot[0], slot[1]],
            send_sem=zsend.at[which, k], recv_sem=zrecv.at[which, k],
            device_id=stack_peer(k), device_id_type=MESH,
        )

    def chip_copy(k, which, slot):
        return pltpu.make_async_remote_copy(
            src_ref=xb.at[which], dst_ref=gb_all.at[which, pl.ds(2 * slot, 2)],
            send_sem=bsend.at[which, k], recv_sem=brecv.at[which, k],
            device_id=chip_peer(k), device_id_type=MESH,
        )

    def stack_from(k):
        return lax.rem(core + k, 2), lax.rem(sub - k // 2 + ns, ns)

    def chip_from(k):
        return lax.rem(chip - k + chips, chips)

    def send_all(make, which, mine, count):
        def body(k, carry):
            make(k, which, mine).start()
            return carry
        lax.fori_loop(1, count, body, 0)

    def wait_all(make, which, source, count):
        def body(k, carry):
            copy = make(k, which, source(k))
            copy.wait_send()
            copy.wait_recv()
            return carry
        lax.fori_loop(1, count, body, 0)

    def gather_start(x, which):
        tile = to_slots(x)
        xa[which] = tile
        ga[which, core, sub] = tile
        send_all(stack_copy, which, (core, sub), 2 * ns)

    def gather_turn(which):
        wait_all(stack_copy, which, stack_from, 2 * ns)
        at = (iota((16, lanes_n), 1) // 4) % ns
        for c in range(2):
            tile = jnp.zeros((16, lanes_n), F32)
            for k in range(ns):
                tile = jnp.where(at == k, ga[which, c, k], tile)
            xb[which, c] = tile
            gb_all[which, 2 * chip + c] = tile
        send_all(chip_copy, which, chip, chips)

    def gather_end(which):
        wait_all(chip_copy, which, chip_from, chips)
        rows = gb_all[which].reshape(nb * 16, lanes_n)
        return pick_left(onehot[...], rows).reshape(vn, 8, lanes_n)

    copies_b1 = x_copies(xs1b, xr1b, xs1b.at[1], xs1b.at[0], xc1b, 10)
    copies_b1 = copies_b1 + z_copies(b1, 16, 6, 16)
    start(copies_b1)
    gather_start(0.125 * coarsen(own_b2, y2, 2), 0)

    each(2, 1, 15, pair_r)
    wait(copies0)

    @pl.when(floor)
    def _():
        b0[pl.ds(0, 2)] = jnp.zeros((2, 32, 128), F32)
        f0[pl.ds(0, 1)] = jnp.zeros((1, 32, 128), F32)

    @pl.when(roof)
    def _():
        b0[pl.ds(34, 2)] = jnp.zeros((2, 32, 128), F32)
        f0[pl.ds(33, 1)] = jnp.zeros((1, 32, 128), F32)

    quarter = lane % 4
    group = lane // 4
    q0, q3 = quarter == 0, quarter == 3
    turn_l1 = lax.rem(129 - width_left + 128, 128)
    turn_l2 = lax.rem(130 - width_left + 128, 128)

    def ghost(from_left, from_right, near_by):
        shift_l = turn_l1 if near_by == 1 else turn_l2
        return jnp.where(
            q0, turn(from_left, shift_l, 1),
            jnp.where(q3, turn(from_right, lax.rem(width - near_by, 128), 1), 0.0),
        )

    ghost_b = ghost(xr0[0, 0], xr0[1, 0], 1)
    ghost_b_low = jnp.where(floor, 0.0, ghost(xc0[0, 0], xc0[1, 0], 1))
    ghost_b_high = jnp.where(roof, 0.0, ghost(xc0[0, 1], xc0[1, 1], 1))
    ghost_b_far = ghost(xr0[0, 0], xr0[1, 0], 2)
    ghost_f = ghost(xr0[0, 1], xr0[1, 1], 1)
    own_edge = jnp.where(q0 | q3, tb, 0.0)
    turned = width // 4 - 1
    first_z = (q0 & (group == 0)) | (q3 & (group == turned))
    last_z = (q0 & (group == 31)) | (q3 & (group == lax.rem(31 + turned, 32)))

    def beside(tile, low, high):
        return (
            turn(tile, 1, 0) + turn(tile, 31, 0)
            + turn(jnp.where(first_z, high, tile), 124, 1)
            + turn(jnp.where(last_z, low, tile), 4, 1)
        )

    ghost_k = ghost_b + own_edge
    ghost_sum = 6.0 * ghost_b + ghost_b_far + own_edge
    ghost_sum = ghost_sum + beside(ghost_b, ghost_b_low, ghost_b_high)
    ghost_u = (2.0 * OMEGA) * ghost_f / jnp.maximum(ghost_sum, TINY)

    below = turn(jnp.where(edge, b0[1], 0.0), 124, 1)
    above = jnp.where(edge, b0[34], 0.0)
    edge_part = 6.0 * own_edge + beside(own_edge, below, above)
    edge_part = edge_part + jnp.where(q0, turn(tb, 127, 1), turn(tb, 1, 1))
    without = (edge_part - own_edge)
    edge_w = (2.0 * OMEGA) / jnp.maximum(without + ghost_k, TINY)
    edge_w = jnp.where(q0 | q3, edge_w, 0.0)
    drift = edge_w * tf - jnp.where(
        q0 | q3, (2.0 * OMEGA) * tf / jnp.maximum(without, TINY), 0.0
    )
    drift_v = own_edge * drift
    gap = own_edge * beside(drift, 0.0, 0.0) + beside(drift_v, 0.0, 0.0) + ghost_k * ghost_u
    gap = jnp.where(
        q0 | q3, gap,
        jnp.where(
            quarter == 1, (tb + turn(own_edge, 1, 1)) * turn(drift, 1, 1),
            (tb + turn(own_edge, 127, 1)) * turn(drift, 127, 1),
        ),
    )
    gap = 0.5 * gap
    gap_pair = gap + turn(gap, 124, 1)

    def back(tile, z):
        return turn(tile, lax.rem(128 - 4 * z, 128), 1)

    start_plane(0, jnp.where(edge, turn(ghost_b_low + below, 4, 1), 0.0))
    start_plane(1)
    start_plane(32)
    start_plane(33, jnp.where(edge, ghost_b_high + above, 0.0))
    pair_r(0)
    pair_r(15)

    def mend(k):
        rs[k] = rs[k] + jnp.where(edge_two, back(gap_pair, 2 * k), 0.0)

    each(4, 0, 16, mend)

    def join(ref, xr, xc, halo):
        at = iota((16, 128), 1)
        inside = at < half
        keep = ((at >= half) & (at < half + halo)) | (at >= 128 - halo)
        sub_at = at % 16

        def beside_own(from_left, from_right):
            from_left = turn(from_left, lax.rem(256 - half_left, 128), 1)
            from_right = turn(from_right, half, 1)
            return jnp.where(
                sub_at >= 16 - halo, from_left, jnp.where(sub_at < halo, from_right, 0.0)
            )

        tiles = [beside_own(xr[0, n], xr[1, n]) for n in range(2)]
        low = beside_own(xc[0, 0], xc[1, 0])
        high = beside_own(xc[0, 1], xc[1, 1])
        for z in range(-halo, 16 + halo):
            tile = low if z < 0 else (high if z >= 16 else tiles[z // 8])
            plane = jnp.where(
                inside, ref[z + halo],
                jnp.where(keep, turn(tile, (128 - 16 * (z % 8)) % 128, 1), 0.0),
            )
            if z < 0:
                plane = jnp.where(floor, 0.0, plane)
            if z >= 16:
                plane = jnp.where(roof, 0.0, plane)
            ref[z + halo] = plane

    def only_inside(x, out):
        n = x.shape[0]
        return jnp.concatenate([
            jnp.where(floor, 0.0, x[:out]), x[out:n - out], jnp.where(roof, 0.0, x[n - out:])
        ], 0)

    def weights(b, step):
        n = b.shape[0]
        middle = b[1:n - 1]
        total = around(middle, step) + b[:n - 2] + b[2:]
        return OMEGA / jnp.maximum(3.0 * middle + 0.5 * total, TINY)

    def gain_of(b, u, v, step):
        n = u.shape[0]
        return b * (around(u[1:n - 1], step) + u[:n - 2] + u[2:]) + (
            around(v[1:n - 1], step) + v[:n - 2] + v[2:]
        )

    def begin_level(b_ref, f_ref, w_ref, u_ref, step):
        n = f_ref.shape[0]
        f = f_ref[...]
        u = w_ref[...] * f
        u_ref[...] = u
        v = b_ref[pl.ds(1, n)] * u
        gain = gain_of(b_ref[pl.ds(2, n - 2)], u, v, step)
        return REST * f[1:n - 1] + 0.5 * gain

    def end_level(b_ref, f_ref, w_ref, u, step):
        n = u.shape[0]
        skip = (f_ref.shape[0] - n) // 2 + 1
        v = b_ref[pl.ds(skip, n)] * u
        b = b_ref[pl.ds(skip + 1, n - 2)]
        gain = gain_of(b, u, v, step)
        return only_inside(REST * u[1:n - 1] + w_ref[pl.ds(skip, n - 2)] * (
            f_ref[pl.ds(skip, n - 2)] + 0.5 * gain
        ), 1)

    own_f1 = 0.5 * squeeze_level0()
    f1[pl.ds(5, 16)] = own_f1
    pack(own_f1, xs1f, 5)
    copies_f1 = x_copies(xs1f, xr1f, xs1f.at[1], xs1f.at[0], xc1f, 18)
    copies_f1 = copies_f1 + z_copies(f1, 16, 5, 24)
    start(copies_f1)

    def prepare(z, odd):
        e = z + 1
        w = jnp.where(edge, back(edge_w, z), w0[e])
        r = r0[z] + jnp.where(edge_two, back(gap, z), 0.0)
        out[z] = jnp.where(live, w * (f0[e] + r), 0.0)
        px, py, b = kx[e], ky[e], b0[e + 1]
        px_low, py_low = turn(px, 1, 1), turn(py, 1, 0)
        pz_low, pz = b0[e] + b, b + b0[e + 2]
        even_x, even_y = lane % 2 == 0, iota((32, 128), 0) % 2 == 0
        rim = jnp.where(edge, back(ghost_k, z), 0.0)
        same = jnp.where(even_x, px, px_low) + jnp.where(even_y, py, py_low)
        same = same + (pz_low if odd else pz)
        w = jnp.where(live, 0.5 * w, 0.0)
        c0[z] = REST + w * same
        cx[z] = w * (jnp.where(even_x, px_low, px) + rim)
        cy[z] = w * jnp.where(even_y, py_low, py)
        cz[z] = w * (pz if odd else pz_low)

    def prepare_pair(k):
        prepare(2 * k, False)
        prepare(2 * k + 1, True)

    gather_turn(0)
    wait(copies_b1)
    join(b1, xr1b, xc1b, 6)
    w1[...] = weights(b1[...], 1)
    b2[...] = 0.125 * coarsen(b1[...], y1, 1)
    w2[...] = weights(b2[...], 2)

    wait(copies_f1)
    join(f1, xr1f, xc1f, 5)
    r1 = begin_level(b1, f1, w1, u1, 1)
    f2[...] = only_inside(0.5 * coarsen(r1, y1, 1), 2)
    r2 = begin_level(b2, f2, w2, u2, 2)
    gather_start(0.5 * coarsen(r2[1:9], y2, 2), 1)
    each(1, 0, 8, prepare_pair)
    gather_turn(1)
    each(1, 8, 16, prepare_pair)

    not_top = iota((vn, 8, lanes_n), 2) % nz3 < nz3 - 1

    def next_x(p):
        return jnp.concatenate([p[1:], turn(p[:1], 7, 1)], 0)

    def last_x(p):
        return jnp.concatenate([turn(p[vn - 1:], 1, 1), p[:vn - 1]], 0)

    def total3(x):
        tile = jnp.sum(x, axis=0)
        return jnp.sum(jnp.sum(tile, axis=0, keepdims=True), axis=1, keepdims=True)

    coarse_b = gather_end(0)
    px = 0.5 * (coarse_b + next_x(coarse_b))
    py = 0.5 * (coarse_b + turn(coarse_b, lanes_n - nz3, 2))
    pz = jnp.where(not_top, 0.5 * (coarse_b + turn(coarse_b, lanes_n - 1, 2)), 0.0)
    ends = jnp.where(
        not_top, 0.0, 0.5 * coarse_b
    ) + jnp.where(iota((vn, 8, lanes_n), 2) % nz3 == 0, 0.5 * coarse_b, 0.0)
    kx3[...] = px
    ky3[...] = py
    kz3[...] = pz
    coarse_d = px + last_x(px) + py + turn(py, nz3, 2) + pz + turn(pz, 1, 2) + ends
    d3[...] = coarse_d
    i3[...] = 1.0 / coarse_d

    coarse_f = gather_end(1)
    r3[...] = coarse_f
    first_p = coarse_f * i3[...]
    p3[...] = first_p
    s3[...] = jnp.zeros((vn, 8, lanes_n), F32)

    def image(p):
        px, py, pz = kx3[...], ky3[...], kz3[...]
        return d3[...] * p - (
            px * next_x(p) + last_x(px * p)
            + py * turn(p, lanes_n - nz3, 2) + turn(py * p, nz3, 2)
            + pz * turn(p, lanes_n - 1, 2) + turn(pz * p, 1, 2)
        )

    def iterate(n, rz):
        p = p3[...]
        q = image(p)
        alpha = rz / total3(p * q)
        s3[...] = s3[...] + alpha * p
        r = r3[...] - alpha * q
        r3[...] = r
        scaled = r * i3[...]
        new = total3(r * scaled)
        p3[...] = scaled + (new / rz) * p
        return new

    rz = lax.fori_loop(0, SWEEPS - 1, iterate, total3(coarse_f * first_p))
    last_p = p3[...]
    solved = s3[...] + (rz / total3(last_p * image(last_p))) * last_p

    l_at, k_at = iota((128, 8 * vn), 0), iota((128, 8 * vn), 1)
    relative = jnp.where(l_at < 124, l_at // 4, -1)
    wanted = lax.rem(4 * my_start + relative + 8 * vn, 8 * vn)
    from_x = ones_where((k_at % 8) * vn + k_at // 8 == wanted)
    by_lane = pick_left(from_x, solved.reshape(8 * vn, lanes_n))
    q_at, r_at = iota((48, lanes_n), 0), iota((48, lanes_n), 1)
    z_at = 4 * sub + q_at // 8 - 1
    from_row = ones_where(
        (r_at == ((q_at % 8) // 2) * nz3 + z_at) & (z_at >= 0) & (z_at < nz3)
    )
    e3 = pick_left_t(from_row, by_lane).reshape(6, 1, 8, 128)
    e3 = jnp.broadcast_to(e3, (6, 2, 8, 128)).reshape(12, 8, 128)

    e2 = end_level(b2, f2, w2, u2[...] + e3, 2)
    e1x[:, pl.ds(0, 8, stride=2), :] = e2
    e1x[:, pl.ds(1, 8, stride=2), :] = e2
    grown = jnp.broadcast_to(e1x[...].reshape(10, 1, 16, 128), (10, 2, 16, 128))
    e1 = end_level(b1, f1, w1, u1[pl.ds(3, 20)] + grown.reshape(20, 16, 128), 1)

    si, sc = iota((128, 256), 0), iota((128, 256), 1)
    sx = sc - 128
    step = jnp.where(sx % 2 == 0, sx // 2 - 1, sx // 2 + 1)
    step = jnp.where(step < 0, 127, step)
    stretch = ones_where(
        ((sc < width) & (si == sc // 2)) | ((sx >= 0) & (sx < width) & (si == step))
    )
    wide = pick_right(e1.reshape(288, 128), stretch)
    main = wide[:, :128].reshape(18, 16, 128)
    side = wide[:, 128:].reshape(18, 16, 128)
    e0m[:, pl.ds(0, 16, stride=2), :] = main
    e0m[:, pl.ds(1, 16, stride=2), :] = main
    e0x[:, pl.ds(0, 16, stride=2), :] = side
    e0x[:, pl.ds(1, 16, stride=2), :] = side
    e0y[:, pl.ds(0, 16, stride=2), :] = turn(main, 1, 1)
    e0y[:, pl.ds(1, 16, stride=2), :] = turn(main, 15, 1)

    def finish_pair(k):
        e, ex, ey = e0m[k + 1], e0x[k + 1], e0y[k + 1]
        for z, ez in ((2 * k, e0m[k]), (2 * k + 1, e0m[k + 2])):
            out[z] = out[z] + c0[z] * e + cx[z] * ex + cy[z] * ey + cz[z] * ez

    each(2, 0, 16, finish_pair)


def per_device(nb, ns, source, beta, counts):
    lanes_n = 16 * ns

    def vmem(*shape, dtype=F32):
        return pltpu.VMEM(shape, dtype)

    def coarse():
        return vmem(nb, 8, lanes_n)

    scratch = [
        vmem(36, 32, 128), vmem(34, 32, 128), vmem(34, 32, 128), vmem(34, 32, 128),
        vmem(32, 32, 128), vmem(34, 32, 128), vmem(34, 32, 128),
        vmem(16, 32, 128), vmem(2, 32, 128), vmem(2, 2, 32, 128), vmem(2, 2, 32, 128),
        vmem(18, 32, 128), vmem(18, 32, 128), vmem(18, 32, 128),
        vmem(32, 32, 128), vmem(32, 32, 128), vmem(32, 32, 128), vmem(32, 32, 128),
        vmem(28, 16, 128), vmem(26, 16, 128), vmem(26, 16, 128), vmem(26, 16, 128),
        vmem(2, 16, 128), vmem(2, 2, 16, 128), vmem(2, 2, 16, 128),
        vmem(2, 16, 128), vmem(2, 2, 16, 128), vmem(2, 2, 16, 128),
        vmem(14, 16, 128), vmem(10, 16, 128),
        vmem(14, 8, 128), vmem(12, 8, 128), vmem(12, 8, 128), vmem(12, 8, 128), vmem(4, 8, 128),
        vmem(32, 128), vmem(128, lanes_n), vmem(2, 16, lanes_n), vmem(2, 2, ns, 16, lanes_n),
        vmem(2, 2, 16, lanes_n), vmem(2, nb, 16, lanes_n), vmem(8 * nb, 16 * nb, dtype=BF16),
        coarse(), coarse(), coarse(), coarse(), coarse(), coarse(), coarse(), coarse(),
        pltpu.SemaphoreType.DMA((2,)),
        pltpu.SemaphoreType.DMA((26,)), pltpu.SemaphoreType.DMA((26,)),
        pltpu.SemaphoreType.DMA((2, 2 * ns)), pltpu.SemaphoreType.DMA((2, 2 * ns)),
        pltpu.SemaphoreType.DMA((2, nb // 2)), pltpu.SemaphoreType.DMA((2, nb // 2)),
    ]
    return pl.pallas_call(
        functools.partial(kernel, nb, ns),
        out_shape=jax.ShapeDtypeStruct(source.shape, F32),
        in_specs=[
            pl.BlockSpec(memory_space=pltpu.SMEM),
            pl.BlockSpec(memory_space=pl.ANY),
            pl.BlockSpec(memory_space=pl.ANY),
        ],
        out_specs=pl.BlockSpec(memory_space=pltpu.VMEM),
        scratch_shapes=scratch,
        compiler_params=pltpu.CompilerParams(
            collective_id=0, has_side_effects=True, vmem_limit_bytes=62 * 1024 * 1024
        ),
    )(counts, source, beta)


def solution(mesh):
    in_specs = (P("sub", None, "box"), P("sub", None, "box"), P())
    out_specs = P("sub", None, "box")
    return jax.shard_map(
        functools.partial(per_device, mesh.shape["box"], mesh.shape["sub"]),
        mesh=mesh, in_specs=in_specs, out_specs=out_specs, check_vma=False,
    )
```

```python
import functools
import jax
import jax.numpy as jnp
from jax import lax
from jax.experimental import pallas as pl
from jax.experimental.pallas import tpu as pltpu
from jax.sharding import PartitionSpec as P

CAP = 4
SWEEPS = 8
OMEGA = 0.8
REST = 0.2
TINY = 1e-20
F32 = jnp.float32
BF16 = jnp.bfloat16
MESH = pl.DeviceIdType.MESH


def split(x):
    high = x.astype(BF16)
    rest = x - high.astype(F32)
    middle = rest.astype(BF16)
    low = (rest - middle.astype(F32)).astype(BF16)
    return (high, middle, low)


def pick_right(x, chosen):
    return sum(jnp.dot(part, chosen, preferred_element_type=F32) for part in split(x))


def pick_left(chosen, x):
    return sum(jnp.dot(chosen, part, preferred_element_type=F32) for part in split(x))


def pick_left_t(chosen, x):
    return sum(
        lax.dot_general(chosen, part, (((1,), (1,)), ((), ())), preferred_element_type=F32)
        for part in split(x)
    )


def ones_where(mask):
    return jnp.where(mask, 1.0, 0.0).astype(BF16)


def iota(shape, dim):
    return lax.broadcasted_iota(jnp.int32, shape, dim)


def turn(x, shift, axis):
    return pltpu.roll(x, shift, axis)


def around(x, step):
    rows = x.shape[-2]
    ax, ay = x.ndim - 1, x.ndim - 2
    return (
        turn(x, step, ax) + turn(x, 128 - step, ax) + turn(x, 1, ay) + turn(x, rows - 1, ay)
    )


def kernel(
    nb, ns,
    counts, source, beta, out,
    b0, f0, u0, w0, r0, kx, ky, rs, xs0, xr0, xd0, xc0, e0m, e0x, e0y, c0, cx, cy, cz,
    b1, f1, u1, w1, xs1b, xr1b, xc1b, xs1f, xr1f, xc1f, y1, e1x,
    b2, f2, u2, w2, y2,
    t3, tx, xa, ga, xb, gb_all, onehot, kx3, ky3, kz3, d3, i3, p3, m3, r3, s3,
    in_sem, send_sem, recv_sem, zsend, zrecv, bsend, brecv,
):
    lanes_n = 16 * ns
    nz3 = 4 * ns
    vn = nb
    me, sub = lax.axis_index("box"), lax.axis_index("sub")
    left, right = lax.rem(me + nb - 1, nb), lax.rem(me + 1, nb)
    down, up = lax.rem(sub + ns - 1, ns), lax.rem(sub + 1, ns)
    floor, roof = sub == 0, sub == ns - 1

    get_b = pltpu.make_async_copy(beta, b0.at[pl.ds(2, 32)], in_sem.at[0])
    get_f = pltpu.make_async_copy(source, f0.at[pl.ds(1, 32)], in_sem.at[1])
    get_b.start()
    get_f.start()

    core, chip, chips = lax.rem(me, 2), me // 2, nb // 2

    def stack_peer(k):
        return 2 * chip + lax.rem(core + k, 2), lax.rem(sub + k // 2, ns)

    def chip_peer(k):
        return 2 * lax.rem(chip + k, chips) + core, sub

    barrier = pltpu.get_barrier_semaphore()

    def greet(peer):
        def body(k, carry):
            pl.semaphore_signal(barrier, inc=1, device_id=peer(k), device_id_type=MESH)
            return carry
        return body

    for there in (left, right):
        for level in (down, sub, up):
            pl.semaphore_signal(barrier, inc=1, device_id=(there, level), device_id_type=MESH)
    lax.fori_loop(1, 2 * ns, greet(stack_peer), 0)
    lax.fori_loop(1, chips, greet(chip_peer), 0)

    width = 32 * counts[me]
    width_left = 32 * counts[left]
    half = width // 2
    half_left = width_left // 2
    kk = iota((1, nb * 16), 1)
    kd, kj = kk // 16, (kk % 16) // ns * ns + ns - 1 - kk % ns

    def place(d, carry):
        where_from, begin, mine = carry
        here = counts[d]
        value = jnp.where(kj < 4 * here, 4 * begin + kj, -1)
        where_from = jnp.where(kd == d, value, where_from)
        mine = jnp.where(d == me, begin, mine)
        return where_from, begin + here, mine

    where_from, _, my_start = lax.fori_loop(
        0, nb, place, (jnp.full((1, nb * 16), -1, jnp.int32), jnp.int32(0), jnp.int32(0))
    )
    row = iota((8 * vn, nb * 16), 0)
    onehot[...] = ones_where((row % 8) * vn + row // 8 == where_from)

    lane = iota((32, 128), 1)
    live = lane < width
    edge = (lane == 0) | (lane == width - 1)
    edge_two = (lane < 2) | ((lane >= width - 2) & live)
    inner = lane < width - 1

    ll = iota((128, 128), 0)
    lc = iota((128, 128), 1)
    squeeze = ones_where((ll // 2 == lc) & (ll < width))

    get_b.wait()
    get_f.wait()

    def each(count, first, last, act):
        def body(n, carry):
            for k in range(count):
                act(first + n * count + k)
            return carry
        lax.fori_loop(0, (last - first) // count, body, 0)

    def load_planes(n, carry):
        tb, tf = carry
        for k in range(4):
            z = 4 * n + k
            b = jnp.where(live, b0[z + 2], 0.0)
            f = jnp.where(live, f0[z + 1], 0.0)
            b0[z + 2] = b
            f0[z + 1] = f
            tb = tb + turn(jnp.where(edge_two, b, 0.0), 4 * z, 1)
            tf = tf + turn(jnp.where(edge, f, 0.0), 4 * z, 1)
        return tb, tf

    zero_tile = jnp.zeros((32, 128), F32)
    tb, tf = lax.fori_loop(0, 8, load_planes, (zero_tile, zero_tile))
    xs0[0] = tb
    xs0[1] = tf
    for n, z in ((0, 0), (1, 31)):
        corner = jnp.zeros((8, 128), F32)
        for m, shift in ((0, (128 - 4 * z) % 128), (4, lax.rem(389 - 4 * z - width, 128))):
            column = jnp.where(lane == m, turn(tb, shift, 1), 0.0)
            for q in range(4):
                corner = corner + turn(column[8 * q:8 * q + 8], q, 1)
        xd0[n] = corner


    def squeeze_level0():
        both = rs[:, pl.ds(0, 16, stride=2), :] + rs[:, pl.ds(1, 16, stride=2), :]
        return pick_right(both.reshape(256, 128), squeeze).reshape(16, 16, 128)

    def coarsen(x, scratch, step):
        planes, rows, _ = x.shape
        n = planes // 2
        pairs = x.reshape(n, 2, rows, 128)
        scratch[pl.ds(0, n)] = pairs[:, 0] + pairs[:, 1]
        y = (
            scratch[pl.ds(0, n), pl.ds(0, rows // 2, stride=2), :]
            + scratch[pl.ds(0, n), pl.ds(1, rows // 2, stride=2), :]
        )
        odd = (iota(y.shape, 2) // step) % 2 == 1
        return y + jnp.where(odd, turn(y, step, 2), turn(y, 128 - step, 2))

    def pack(x, tile_ref, reach):
        at = iota((16, 128), 1)
        keep = (at < reach) | ((at >= half - reach) & (at < half))
        for n in range(2):
            total = jnp.zeros((16, 128), F32)
            for z in range(8):
                total = total + turn(jnp.where(keep, x[8 * n + z], 0.0), 16 * z, 1)
            tile_ref[n] = total

    def to_slots(x):
        for z in range(4):
            t3[pl.ds(z, 4, stride=8), :] = x[z]
            t3[pl.ds(z + 4, 4, stride=8), :] = x[z]
        tiles = t3[...].reshape(4, 1, 8, 128)
        tiles = jnp.broadcast_to(tiles, (4, ns // 2, 8, 128)).reshape(lanes_n, 128)
        tx[...] = jnp.transpose(tiles)
        return tx[pl.ds(0, 16, stride=4), :]

    def pair_b(k):
        rs[k] = b0[2 * k + 2] + b0[2 * k + 3]

    each(4, 0, 16, pair_b)
    own_b1 = 0.125 * squeeze_level0()
    b1[pl.ds(6, 16)] = own_b1
    pack(own_b1, xs1b, 6)
    own_b2 = 0.125 * coarsen(own_b1, y1, 1)

    def couple(e):
        b = b0[e + 1]
        px = jnp.where(inner, b + turn(b, 127, 1), 0.0)
        py = b + turn(b, 31, 0)
        kx[e] = px
        ky[e] = py
        return px + turn(px, 1, 1) + py + turn(py, 1, 0) + (b0[e] + b) + (b + b0[e + 2])

    def start_plane(e, more=0.0):
        w = (2.0 * OMEGA) / jnp.maximum(couple(e) + more, TINY)
        w0[e] = w
        u0[e] = w * f0[e]

    def pull(e):
        u, px, py, b = u0[e], kx[e], ky[e], b0[e + 1]
        return (
            px * turn(u, 127, 1) + turn(px * u, 1, 1) + py * turn(u, 31, 0) + turn(py * u, 1, 0)
            + (b0[e] + b) * u0[e - 1] + (b + b0[e + 2]) * u0[e + 1]
        )

    def residual(z):
        r = REST * f0[z + 1] + 0.5 * pull(z + 1)
        r0[z] = r
        return r

    def pair_r(k):
        rs[k] = residual(2 * k) + residual(2 * k + 1)

    each(5, 2, 32, start_plane)

    pl.semaphore_wait(barrier, 6 + (2 * ns - 1) + (chips - 1))

    def x_copies(src, dst, for_up, for_down, corner, base):
        made = []
        for side, there in ((0, right), (1, left)):
            for n, (begin, end, level) in enumerate((
                (src, dst.at[side], sub),
                (for_up, corner.at[side, 0], up),
                (for_down, corner.at[side, 1], down),
            )):
                at = base + side * 3 + n
                made.append(
                    pltpu.make_async_remote_copy(
                        src_ref=begin, dst_ref=end,
                        send_sem=send_sem.at[at], recv_sem=recv_sem.at[at],
                        device_id=(there, level), device_id_type=MESH,
                    )
                )
        return made

    def z_copies(ref, own, halo, base):
        made = []
        for n, (begin, to, level) in enumerate(
            ((own, 0, up), (halo, own + halo, down))
        ):
            made.append(
                pltpu.make_async_remote_copy(
                    src_ref=ref.at[pl.ds(begin, halo)], dst_ref=ref.at[pl.ds(to, halo)],
                    send_sem=send_sem.at[base + n], recv_sem=recv_sem.at[base + n],
                    device_id=(me, level), device_id_type=MESH,
                )
            )
        return made

    def start(copies):
        for copy in copies:
            copy.start()

    def wait(copies):
        for copy in copies:
            copy.wait()

    copies0 = x_copies(xs0, xr0, xd0.at[1], xd0.at[0], xc0, 0) + z_copies(b0, 32, 2, 6) + z_copies(f0, 32, 1, 8)
    start(copies0)

    def stack_copy(k, which, slot):
        return pltpu.make_async_remote_copy(
            src_ref=xa.at[which], dst_ref=ga.at[which, slot[0], slot[1]],
            send_sem=zsend.at[which, k], recv_sem=zrecv.at[which, k],
            device_id=stack_peer(k), device_id_type=MESH,
        )

    def chip_copy(k, which, slot):
        return pltpu.make_async_remote_copy(
            src_ref=xb.at[which], dst_ref=gb_all.at[which, pl.ds(2 * slot, 2)],
            send_sem=bsend.at[which, k], recv_sem=brecv.at[which, k],
            device_id=chip_peer(k), device_id_type=MESH,
        )

    def stack_from(k):
        return lax.rem(core + k, 2), lax.rem(sub - k // 2 + ns, ns)

    def chip_from(k):
        return lax.rem(chip - k + chips, chips)

    def send_all(make, which, mine, count):
        def body(k, carry):
            make(k, which, mine).start()
            return carry
        lax.fori_loop(1, count, body, 0)

    def wait_all(make, which, source, count):
        def body(k, carry):
            copy = make(k, which, source(k))
            copy.wait_send()
            copy.wait_recv()
            return carry
        lax.fori_loop(1, count, body, 0)

    slot_at = (iota((ns, lanes_n), 1) // 4) % ns
    row_at = iota((ns, lanes_n), 0)

    def gather_start(x, which):
        tile = to_slots(x)
        for h in range(16 // ns):
            part = jnp.where(row_at == slot_at, tile[h * ns:(h + 1) * ns], 0.0)
            part = jnp.sum(part, axis=0, keepdims=True)
            xa[which, pl.ds(h, 1)] = part
            ga[which, core, sub, pl.ds(h, 1)] = part
        send_all(stack_copy, which, (core, sub), 2 * ns)

    def gather_turn(which):
        wait_all(stack_copy, which, stack_from, 2 * ns)
        for c in range(2):
            for h in range(16 // ns):
                tile = jnp.zeros((ns, lanes_n), F32)
                for k in range(ns):
                    part = jnp.broadcast_to(ga[which, c, k, pl.ds(h, 1)], (ns, lanes_n))
                    part = pltpu.roll(part, 0, 1, stride=4, stride_axis=0)
                    part = turn(part, (4 * (k - ns + 1)) % lanes_n, 1)
                    tile = jnp.where(slot_at == k, part, tile)
                xb[which, c, pl.ds(h * ns, ns)] = tile
                gb_all[which, 2 * chip + c, pl.ds(h * ns, ns)] = tile
        send_all(chip_copy, which, chip, chips)

    def gather_end(which):
        wait_all(chip_copy, which, chip_from, chips)
        rows = gb_all[which].reshape(nb * 16, lanes_n)
        return pick_left(onehot[...], rows).reshape(vn, 8, lanes_n)

    copies_b1 = x_copies(xs1b, xr1b, xs1b.at[1], xs1b.at[0], xc1b, 10)
    copies_b1 = copies_b1 + z_copies(b1, 16, 6, 16)
    start(copies_b1)
    gather_start(0.125 * coarsen(own_b2, y2, 2), 0)

    each(2, 1, 15, pair_r)
    wait(copies0)

    @pl.when(floor)
    def _():
        b0[pl.ds(0, 2)] = jnp.zeros((2, 32, 128), F32)
        f0[pl.ds(0, 1)] = jnp.zeros((1, 32, 128), F32)

    @pl.when(roof)
    def _():
        b0[pl.ds(34, 2)] = jnp.zeros((2, 32, 128), F32)
        f0[pl.ds(33, 1)] = jnp.zeros((1, 32, 128), F32)

    quarter = lane % 4
    group = lane // 4
    q0, q3 = quarter == 0, quarter == 3
    turn_l1 = lax.rem(129 - width_left + 128, 128)
    turn_l2 = lax.rem(130 - width_left + 128, 128)

    def ghost(from_left, from_right, near_by):
        shift_l = turn_l1 if near_by == 1 else turn_l2
        return jnp.where(
            q0, turn(from_left, shift_l, 1),
            jnp.where(q3, turn(from_right, lax.rem(width - near_by, 128), 1), 0.0),
        )

    ghost_b = ghost(xr0[0, 0], xr0[1, 0], 1)

    def ghost_corner(n, z, outside):
        from_left, from_right = xc0[0, n], xc0[1, n]
        rows = []
        for q in range(4):
            at_left = turn(from_left, (128 + 4 * z - 4 - q) % 128, 1)
            at_right = turn(from_right, lax.rem(4 * z + width + 127 - q, 128), 1)
            rows.append(jnp.where(
                lane[:8] == 4 * z, at_left,
                jnp.where(lane[:8] == lax.rem(4 * z + width - 1, 128), at_right, 0.0),
            ))
        return jnp.where(outside, 0.0, jnp.concatenate(rows, 0))

    ghost_b_low = ghost_corner(0, 31, floor)
    ghost_b_high = ghost_corner(1, 0, roof)
    ghost_b_far = ghost(xr0[0, 0], xr0[1, 0], 2)
    ghost_f = ghost(xr0[0, 1], xr0[1, 1], 1)
    own_edge = jnp.where(q0 | q3, tb, 0.0)
    turned = width // 4 - 1
    first_z = (q0 & (group == 0)) | (q3 & (group == turned))
    last_z = (q0 & (group == 31)) | (q3 & (group == lax.rem(31 + turned, 32)))

    def beside(tile, low, high):
        return (
            turn(tile, 1, 0) + turn(tile, 31, 0)
            + turn(jnp.where(first_z, high, tile), 124, 1)
            + turn(jnp.where(last_z, low, tile), 4, 1)
        )

    ghost_k = ghost_b + own_edge
    ghost_sum = 6.0 * ghost_b + ghost_b_far + own_edge
    ghost_sum = ghost_sum + beside(ghost_b, ghost_b_low, ghost_b_high)
    ghost_u = (2.0 * OMEGA) * ghost_f / jnp.maximum(ghost_sum, TINY)

    below = turn(jnp.where(edge, b0[1], 0.0), 124, 1)
    above = jnp.where(edge, b0[34], 0.0)
    edge_part = 6.0 * own_edge + beside(own_edge, below, above)
    edge_part = edge_part + jnp.where(q0, turn(tb, 127, 1), turn(tb, 1, 1))
    without = (edge_part - own_edge)
    edge_w = (2.0 * OMEGA) / jnp.maximum(without + ghost_k, TINY)
    edge_w = jnp.where(q0 | q3, edge_w, 0.0)
    drift = edge_w * tf - jnp.where(
        q0 | q3, (2.0 * OMEGA) * tf / jnp.maximum(without, TINY), 0.0
    )
    drift_v = own_edge * drift
    gap = own_edge * beside(drift, 0.0, 0.0) + beside(drift_v, 0.0, 0.0) + ghost_k * ghost_u
    gap = jnp.where(
        q0 | q3, gap,
        jnp.where(
            quarter == 1, (tb + turn(own_edge, 1, 1)) * turn(drift, 1, 1),
            (tb + turn(own_edge, 127, 1)) * turn(drift, 127, 1),
        ),
    )
    gap = 0.5 * gap
    gap_pair = gap + turn(gap, 124, 1)

    def back(tile, z):
        return turn(tile, lax.rem(128 - 4 * z, 128), 1)

    start_plane(0, jnp.where(edge, turn(ghost_b_low + below, 4, 1), 0.0))
    start_plane(1)
    start_plane(32)
    start_plane(33, jnp.where(edge, ghost_b_high + above, 0.0))
    pair_r(0)
    pair_r(15)

    def mend(k):
        rs[k] = rs[k] + jnp.where(edge_two, back(gap_pair, 2 * k), 0.0)

    each(4, 0, 16, mend)

    def join(ref, xr, xc, halo):
        at = iota((16, 128), 1)
        inside = at < half
        keep = ((at >= half) & (at < half + halo)) | (at >= 128 - halo)
        sub_at = at % 16

        def beside_own(from_left, from_right):
            from_left = turn(from_left, lax.rem(256 - half_left, 128), 1)
            from_right = turn(from_right, half, 1)
            return jnp.where(
                sub_at >= 16 - halo, from_left, jnp.where(sub_at < halo, from_right, 0.0)
            )

        tiles = [beside_own(xr[0, n], xr[1, n]) for n in range(2)]
        low = beside_own(xc[0, 0], xc[1, 0])
        high = beside_own(xc[0, 1], xc[1, 1])
        for z in range(-halo, 16 + halo):
            tile = low if z < 0 else (high if z >= 16 else tiles[z // 8])
            plane = jnp.where(
                inside, ref[z + halo],
                jnp.where(keep, turn(tile, (128 - 16 * (z % 8)) % 128, 1), 0.0),
            )
            if z < 0:
                plane = jnp.where(floor, 0.0, plane)
            if z >= 16:
                plane = jnp.where(roof, 0.0, plane)
            ref[z + halo] = plane

    def only_inside(x, out):
        n = x.shape[0]
        return jnp.concatenate([
            jnp.where(floor, 0.0, x[:out]), x[out:n - out], jnp.where(roof, 0.0, x[n - out:])
        ], 0)

    def weights(b, step):
        n = b.shape[0]
        middle = b[1:n - 1]
        total = around(middle, step) + b[:n - 2] + b[2:]
        return OMEGA / jnp.maximum(3.0 * middle + 0.5 * total, TINY)

    def gain_of(b, u, v, step):
        n = u.shape[0]
        return b * (around(u[1:n - 1], step) + u[:n - 2] + u[2:]) + (
            around(v[1:n - 1], step) + v[:n - 2] + v[2:]
        )

    def begin_level(b_ref, f_ref, w_ref, u_ref, step):
        n = f_ref.shape[0]
        f = f_ref[...]
        u = w_ref[...] * f
        u_ref[...] = u
        v = b_ref[pl.ds(1, n)] * u
        gain = gain_of(b_ref[pl.ds(2, n - 2)], u, v, step)
        return REST * f[1:n - 1] + 0.5 * gain

    def end_level(b_ref, f_ref, w_ref, u, step):
        n = u.shape[0]
        skip = (f_ref.shape[0] - n) // 2 + 1
        v = b_ref[pl.ds(skip, n)] * u
        b = b_ref[pl.ds(skip + 1, n - 2)]
        gain = gain_of(b, u, v, step)
        return only_inside(REST * u[1:n - 1] + w_ref[pl.ds(skip, n - 2)] * (
            f_ref[pl.ds(skip, n - 2)] + 0.5 * gain
        ), 1)

    own_f1 = 0.5 * squeeze_level0()
    f1[pl.ds(5, 16)] = own_f1
    pack(own_f1, xs1f, 5)
    copies_f1 = x_copies(xs1f, xr1f, xs1f.at[1], xs1f.at[0], xc1f, 18)
    copies_f1 = copies_f1 + z_copies(f1, 16, 5, 24)
    start(copies_f1)

    def prepare(z, odd):
        e = z + 1
        w = jnp.where(edge, back(edge_w, z), w0[e])
        r = r0[z] + jnp.where(edge_two, back(gap, z), 0.0)
        out[z] = jnp.where(live, w * (f0[e] + r), 0.0)
        px, py, b = kx[e], ky[e], b0[e + 1]
        px_low, py_low = turn(px, 1, 1), turn(py, 1, 0)
        pz_low, pz = b0[e] + b, b + b0[e + 2]
        even_x, even_y = lane % 2 == 0, iota((32, 128), 0) % 2 == 0
        rim = jnp.where(edge, back(ghost_k, z), 0.0)
        same = jnp.where(even_x, px, px_low) + jnp.where(even_y, py, py_low)
        same = same + (pz_low if odd else pz)
        w = jnp.where(live, 0.5 * w, 0.0)
        c0[z] = REST + w * same
        cx[z] = w * (jnp.where(even_x, px_low, px) + rim)
        cy[z] = w * jnp.where(even_y, py_low, py)
        cz[z] = w * (pz if odd else pz_low)

    def prepare_pair(k):
        prepare(2 * k, False)
        prepare(2 * k + 1, True)

    gather_turn(0)
    wait(copies_b1)
    join(b1, xr1b, xc1b, 6)
    w1[...] = weights(b1[...], 1)
    b2[...] = 0.125 * coarsen(b1[...], y1, 1)
    w2[...] = weights(b2[...], 2)

    wait(copies_f1)
    join(f1, xr1f, xc1f, 5)
    r1 = begin_level(b1, f1, w1, u1, 1)
    f2[...] = only_inside(0.5 * coarsen(r1, y1, 1), 2)
    r2 = begin_level(b2, f2, w2, u2, 2)
    gather_start(0.5 * coarsen(r2[1:9], y2, 2), 1)
    each(1, 0, 8, prepare_pair)
    gather_turn(1)
    each(1, 8, 16, prepare_pair)

    not_top = iota((vn, 8, lanes_n), 2) % nz3 < nz3 - 1

    def next_x(p):
        return jnp.concatenate([p[1:], turn(p[:1], 7, 1)], 0)

    def last_x(p):
        return jnp.concatenate([turn(p[vn - 1:], 1, 1), p[:vn - 1]], 0)

    def total3(x):
        tile = jnp.sum(x, axis=0)
        return jnp.sum(jnp.sum(tile, axis=0, keepdims=True), axis=1, keepdims=True)

    coarse_b = gather_end(0)
    px = 0.5 * (coarse_b + next_x(coarse_b))
    py = 0.5 * (coarse_b + turn(coarse_b, lanes_n - nz3, 2))
    pz = jnp.where(not_top, 0.5 * (coarse_b + turn(coarse_b, lanes_n - 1, 2)), 0.0)
    ends = jnp.where(
        not_top, 0.0, 0.5 * coarse_b
    ) + jnp.where(iota((vn, 8, lanes_n), 2) % nz3 == 0, 0.5 * coarse_b, 0.0)
    kx3[...] = px
    ky3[...] = py
    kz3[...] = pz
    coarse_d = px + last_x(px) + py + turn(py, nz3, 2) + pz + turn(pz, 1, 2) + ends
    d3[...] = coarse_d
    i3[...] = 1.0 / coarse_d

    coarse_f = gather_end(1)
    r3[...] = coarse_f
    s3[...] = jnp.zeros((vn, 8, lanes_n), F32)
    p3[...] = jnp.zeros((vn, 8, lanes_n), F32)
    m3[...] = jnp.zeros((vn, 8, lanes_n), F32)

    def image(p):
        px, py, pz = kx3[...], ky3[...], kz3[...]
        return d3[...] * p - (
            px * next_x(p) + last_x(px * p)
            + py * turn(p, lanes_n - nz3, 2) + turn(py * p, nz3, 2)
            + pz * turn(p, lanes_n - 1, 2) + turn(pz * p, 1, 2)
        )

    def iterate(n, carry):
        gamma_old, alpha_old = carry
        r = r3[...]
        z = r * i3[...]
        az = image(z)
        gamma, delta = total3(r * z), total3(z * az)
        beta = jnp.where(n == 0, 0.0, gamma / gamma_old)
        alpha = gamma / (delta - beta * gamma / alpha_old)
        p = z + beta * p3[...]
        q = az + beta * m3[...]
        p3[...] = p
        m3[...] = q
        s3[...] = s3[...] + alpha * p
        r3[...] = r - alpha * q
        return gamma, alpha

    one = jnp.ones((1, 1), F32)
    lax.fori_loop(0, SWEEPS, iterate, (one, one))
    solved = s3[...]

    l_at, k_at = iota((128, 8 * vn), 0), iota((128, 8 * vn), 1)
    relative = jnp.where(l_at < 124, l_at // 4, -1)
    wanted = lax.rem(4 * my_start + relative + 8 * vn, 8 * vn)
    from_x = ones_where((k_at % 8) * vn + k_at // 8 == wanted)
    by_lane = pick_left(from_x, solved.reshape(8 * vn, lanes_n))
    q_at, r_at = iota((48, lanes_n), 0), iota((48, lanes_n), 1)
    z_at = 4 * sub + q_at // 8 - 1
    from_row = ones_where(
        (r_at == ((q_at % 8) // 2) * nz3 + z_at) & (z_at >= 0) & (z_at < nz3)
    )
    e3 = pick_left_t(from_row, by_lane).reshape(6, 1, 8, 128)
    e3 = jnp.broadcast_to(e3, (6, 2, 8, 128)).reshape(12, 8, 128)

    e2 = end_level(b2, f2, w2, u2[...] + e3, 2)
    e1x[:, pl.ds(0, 8, stride=2), :] = e2
    e1x[:, pl.ds(1, 8, stride=2), :] = e2
    grown = jnp.broadcast_to(e1x[...].reshape(10, 1, 16, 128), (10, 2, 16, 128))
    e1 = end_level(b1, f1, w1, u1[pl.ds(3, 20)] + grown.reshape(20, 16, 128), 1)

    si, sc = iota((128, 256), 0), iota((128, 256), 1)
    sx = sc - 128
    step = jnp.where(sx % 2 == 0, sx // 2 - 1, sx // 2 + 1)
    step = jnp.where(step < 0, 127, step)
    stretch = ones_where(
        ((sc < width) & (si == sc // 2)) | ((sx >= 0) & (sx < width) & (si == step))
    )
    wide = pick_right(e1.reshape(288, 128), stretch)
    main = wide[:, :128].reshape(18, 16, 128)
    side = wide[:, 128:].reshape(18, 16, 128)
    e0m[:, pl.ds(0, 16, stride=2), :] = main
    e0m[:, pl.ds(1, 16, stride=2), :] = main
    e0x[:, pl.ds(0, 16, stride=2), :] = side
    e0x[:, pl.ds(1, 16, stride=2), :] = side
    e0y[:, pl.ds(0, 16, stride=2), :] = turn(main, 1, 1)
    e0y[:, pl.ds(1, 16, stride=2), :] = turn(main, 15, 1)

    def finish_pair(k):
        e, ex, ey = e0m[k + 1], e0x[k + 1], e0y[k + 1]
        for z, ez in ((2 * k, e0m[k]), (2 * k + 1, e0m[k + 2])):
            out[z] = out[z] + c0[z] * e + cx[z] * ex + cy[z] * ey + cz[z] * ez

    each(2, 0, 16, finish_pair)


def per_device(nb, ns, source, beta, counts):
    lanes_n = 16 * ns

    def vmem(*shape, dtype=F32):
        return pltpu.VMEM(shape, dtype)

    def coarse():
        return vmem(nb, 8, lanes_n)

    scratch = [
        vmem(36, 32, 128), vmem(34, 32, 128), vmem(34, 32, 128), vmem(34, 32, 128),
        vmem(32, 32, 128), vmem(34, 32, 128), vmem(34, 32, 128),
        vmem(16, 32, 128), vmem(2, 32, 128), vmem(2, 2, 32, 128), vmem(2, 8, 128), vmem(2, 2, 8, 128),
        vmem(18, 32, 128), vmem(18, 32, 128), vmem(18, 32, 128),
        vmem(32, 32, 128), vmem(32, 32, 128), vmem(32, 32, 128), vmem(32, 32, 128),
        vmem(28, 16, 128), vmem(26, 16, 128), vmem(26, 16, 128), vmem(26, 16, 128),
        vmem(2, 16, 128), vmem(2, 2, 16, 128), vmem(2, 2, 16, 128),
        vmem(2, 16, 128), vmem(2, 2, 16, 128), vmem(2, 2, 16, 128),
        vmem(14, 16, 128), vmem(10, 16, 128),
        vmem(14, 8, 128), vmem(12, 8, 128), vmem(12, 8, 128), vmem(12, 8, 128), vmem(4, 8, 128),
        vmem(32, 128), vmem(128, lanes_n), vmem(2, 16 // ns, lanes_n), vmem(2, 2, ns, 16 // ns, lanes_n),
        vmem(2, 2, 16, lanes_n), vmem(2, nb, 16, lanes_n), vmem(8 * nb, 16 * nb, dtype=BF16),
        coarse(), coarse(), coarse(), coarse(), coarse(), coarse(), coarse(), coarse(), coarse(),
        pltpu.SemaphoreType.DMA((2,)),
        pltpu.SemaphoreType.DMA((26,)), pltpu.SemaphoreType.DMA((26,)),
        pltpu.SemaphoreType.DMA((2, 2 * ns)), pltpu.SemaphoreType.DMA((2, 2 * ns)),
        pltpu.SemaphoreType.DMA((2, nb // 2)), pltpu.SemaphoreType.DMA((2, nb // 2)),
    ]
    return pl.pallas_call(
        functools.partial(kernel, nb, ns),
        out_shape=jax.ShapeDtypeStruct(source.shape, F32),
        in_specs=[
            pl.BlockSpec(memory_space=pltpu.SMEM),
            pl.BlockSpec(memory_space=pl.ANY),
            pl.BlockSpec(memory_space=pl.ANY),
        ],
        out_specs=pl.BlockSpec(memory_space=pltpu.VMEM),
        scratch_shapes=scratch,
        compiler_params=pltpu.CompilerParams(
            collective_id=0, has_side_effects=True, vmem_limit_bytes=62 * 1024 * 1024
        ),
    )(counts, source, beta)


def solution(mesh):
    in_specs = (P("sub", None, "box"), P("sub", None, "box"), P())
    out_specs = P("sub", None, "box")
    return jax.shard_map(
        functools.partial(per_device, mesh.shape["box"], mesh.shape["sub"]),
        mesh=mesh, in_specs=in_specs, out_specs=out_specs, check_vma=False,
    )
```

```python
import functools
import jax
import jax.numpy as jnp
from jax import lax
from jax.experimental import pallas as pl
from jax.experimental.pallas import tpu as pltpu
from jax.sharding import PartitionSpec as P

CAP = 4
SWEEPS = 8
OMEGA = 0.8
REST = 0.2
TINY = 1e-20
F32 = jnp.float32
BF16 = jnp.bfloat16
MESH = pl.DeviceIdType.MESH


def split(x):
    high = x.astype(BF16)
    middle = (x - high.astype(F32)).astype(BF16)
    return (high, middle)


def pick_right(x, chosen):
    return sum(jnp.dot(part, chosen, preferred_element_type=F32) for part in split(x))


def pick_left(chosen, x):
    return sum(jnp.dot(chosen, part, preferred_element_type=F32) for part in split(x))


def pick_left_t(chosen, x):
    return sum(
        lax.dot_general(chosen, part, (((1,), (1,)), ((), ())), preferred_element_type=F32)
        for part in split(x)
    )


def ones_where(mask):
    return jnp.where(mask, 1.0, 0.0).astype(BF16)


def iota(shape, dim):
    return lax.broadcasted_iota(jnp.int32, shape, dim)


def turn(x, shift, axis):
    return pltpu.roll(x, shift, axis)


def around(x, step):
    rows = x.shape[-2]
    ax, ay = x.ndim - 1, x.ndim - 2
    return (
        turn(x, step, ax) + turn(x, 128 - step, ax) + turn(x, 1, ay) + turn(x, rows - 1, ay)
    )


def kernel(
    nb, ns,
    counts, source, beta, out,
    b0, f0, u0, w0, r0, kx, ky, rs, xs0, xr0, xd0, xc0, e0m, e0x, e0y, c0, cx, cy, cz,
    b1, f1, u1, w1, xs1b, xr1b, xc1b, xs1f, xr1f, xc1f, y1, e1x,
    b2, f2, u2, w2, y2,
    t3, tx, xa, ga, xb, gb_all, onehot, kx3, ky3, kz3, d3, i3, p3, m3, r3, s3,
    in_sem, send_sem, recv_sem, zsend, zrecv, bsend, brecv,
):
    lanes_n = 16 * ns
    nz3 = 4 * ns
    vn = nb
    me, sub = lax.axis_index("box"), lax.axis_index("sub")
    left, right = lax.rem(me + nb - 1, nb), lax.rem(me + 1, nb)
    down, up = lax.rem(sub + ns - 1, ns), lax.rem(sub + 1, ns)
    floor, roof = sub == 0, sub == ns - 1

    get_b = pltpu.make_async_copy(beta, b0.at[pl.ds(2, 32)], in_sem.at[0])
    get_f = pltpu.make_async_copy(source, f0.at[pl.ds(1, 32)], in_sem.at[1])
    get_b.start()
    get_f.start()

    core, chip, chips = lax.rem(me, 2), me // 2, nb // 2

    def stack_peer(k):
        return 2 * chip + lax.rem(core + k, 2), lax.rem(sub + k // 2, ns)

    def chip_peer(k):
        return 2 * lax.rem(chip + k, chips) + core, sub

    barrier = pltpu.get_barrier_semaphore()

    def greet(peer):
        def body(k, carry):
            pl.semaphore_signal(barrier, inc=1, device_id=peer(k), device_id_type=MESH)
            return carry
        return body

    for there in (left, right):
        for level in (down, sub, up):
            pl.semaphore_signal(barrier, inc=1, device_id=(there, level), device_id_type=MESH)
    lax.fori_loop(1, 2 * ns, greet(stack_peer), 0)
    lax.fori_loop(1, chips, greet(chip_peer), 0)

    width = 32 * counts[me]
    width_left = 32 * counts[left]
    half = width // 2
    half_left = width_left // 2
    kk = iota((1, nb * 16), 1)
    kd, kj = kk // 16, (kk % 16) // ns * ns + ns - 1 - kk % ns

    def place(d, carry):
        where_from, begin, mine = carry
        here = counts[d]
        value = jnp.where(kj < 4 * here, 4 * begin + kj, -1)
        where_from = jnp.where(kd == d, value, where_from)
        mine = jnp.where(d == me, begin, mine)
        return where_from, begin + here, mine

    where_from, _, my_start = lax.fori_loop(
        0, nb, place, (jnp.full((1, nb * 16), -1, jnp.int32), jnp.int32(0), jnp.int32(0))
    )
    row = iota((8 * vn, nb * 16), 0)
    onehot[...] = ones_where((row % 8) * vn + row // 8 == where_from)

    lane = iota((32, 128), 1)
    live = lane < width
    edge = (lane == 0) | (lane == width - 1)
    edge_two = (lane < 2) | ((lane >= width - 2) & live)
    inner = lane < width - 1

    ll = iota((128, 128), 0)
    lc = iota((128, 128), 1)
    squeeze = ones_where((ll // 2 == lc) & (ll < width))

    get_b.wait()
    get_f.wait()

    def each(count, first, last, act):
        def body(n, carry):
            for k in range(count):
                act(first + n * count + k)
            return carry
        lax.fori_loop(0, (last - first) // count, body, 0)

    def load_planes(n, carry):
        tb, tf = carry
        for k in range(4):
            z = 4 * n + k
            b = jnp.where(live, b0[z + 2], 0.0)
            f = jnp.where(live, f0[z + 1], 0.0)
            b0[z + 2] = b
            f0[z + 1] = f
            tb = tb + turn(jnp.where(edge_two, b, 0.0), 4 * z, 1)
            tf = tf + turn(jnp.where(edge, f, 0.0), 4 * z, 1)
        return tb, tf

    zero_tile = jnp.zeros((32, 128), F32)
    tb, tf = lax.fori_loop(0, 8, load_planes, (zero_tile, zero_tile))
    xs0[0] = tb
    xs0[1] = tf
    for n, z in ((0, 0), (1, 31)):
        corner = jnp.zeros((8, 128), F32)
        for m, shift in ((0, (128 - 4 * z) % 128), (4, lax.rem(389 - 4 * z - width, 128))):
            column = jnp.where(lane == m, turn(tb, shift, 1), 0.0)
            for q in range(4):
                corner = corner + turn(column[8 * q:8 * q + 8], q, 1)
        xd0[n] = corner


    def squeeze_level0():
        both = rs[:, pl.ds(0, 16, stride=2), :] + rs[:, pl.ds(1, 16, stride=2), :]
        return pick_right(both.reshape(256, 128), squeeze).reshape(16, 16, 128)

    def coarsen(x, scratch, step):
        planes, rows, _ = x.shape
        n = planes // 2
        pairs = x.reshape(n, 2, rows, 128)
        scratch[pl.ds(0, n)] = pairs[:, 0] + pairs[:, 1]
        y = (
            scratch[pl.ds(0, n), pl.ds(0, rows // 2, stride=2), :]
            + scratch[pl.ds(0, n), pl.ds(1, rows // 2, stride=2), :]
        )
        odd = (iota(y.shape, 2) // step) % 2 == 1
        return y + jnp.where(odd, turn(y, step, 2), turn(y, 128 - step, 2))

    def pack(x, tile_ref, reach):
        at = iota((16, 128), 1)
        keep = (at < reach) | ((at >= half - reach) & (at < half))
        for n in range(2):
            total = jnp.zeros((16, 128), F32)
            for z in range(8):
                total = total + turn(jnp.where(keep, x[8 * n + z], 0.0), 16 * z, 1)
            tile_ref[n] = total

    def to_slots(x):
        for z in range(4):
            t3[pl.ds(z, 4, stride=8), :] = x[z]
            t3[pl.ds(z + 4, 4, stride=8), :] = x[z]
        tiles = t3[...].reshape(4, 1, 8, 128)
        tiles = jnp.broadcast_to(tiles, (4, ns // 2, 8, 128)).reshape(lanes_n, 128)
        tx[...] = jnp.transpose(tiles)
        return tx[pl.ds(0, 16, stride=4), :]

    def pair_b(k):
        rs[k] = b0[2 * k + 2] + b0[2 * k + 3]

    each(4, 0, 16, pair_b)
    own_b1 = 0.125 * squeeze_level0()
    b1[pl.ds(6, 16)] = own_b1
    pack(own_b1, xs1b, 6)
    own_b2 = 0.125 * coarsen(own_b1, y1, 1)

    def couple(e):
        b = b0[e + 1]
        px = jnp.where(inner, b + turn(b, 127, 1), 0.0)
        py = b + turn(b, 31, 0)
        kx[e] = px
        ky[e] = py
        return px + turn(px, 1, 1) + py + turn(py, 1, 0) + (b0[e] + b) + (b + b0[e + 2])

    def start_plane(e, more=0.0):
        w = (2.0 * OMEGA) / jnp.maximum(couple(e) + more, TINY)
        w0[e] = w
        u0[e] = w * f0[e]

    def pull(e):
        u, px, py, b = u0[e], kx[e], ky[e], b0[e + 1]
        return (
            px * turn(u, 127, 1) + turn(px * u, 1, 1) + py * turn(u, 31, 0) + turn(py * u, 1, 0)
            + (b0[e] + b) * u0[e - 1] + (b + b0[e + 2]) * u0[e + 1]
        )

    def residual(z):
        r = REST * f0[z + 1] + 0.5 * pull(z + 1)
        r0[z] = r
        return r

    def pair_r(k):
        rs[k] = residual(2 * k) + residual(2 * k + 1)


    pl.semaphore_wait(barrier, 6 + (2 * ns - 1) + (chips - 1))

    def x_copies(src, dst, for_up, for_down, corner, base):
        made = []
        for side, there in ((0, right), (1, left)):
            for n, (begin, end, level) in enumerate((
                (src, dst.at[side], sub),
                (for_up, corner.at[side, 0], up),
                (for_down, corner.at[side, 1], down),
            )):
                at = base + side * 3 + n
                made.append(
                    pltpu.make_async_remote_copy(
                        src_ref=begin, dst_ref=end,
                        send_sem=send_sem.at[at], recv_sem=recv_sem.at[at],
                        device_id=(there, level), device_id_type=MESH,
                    )
                )
        return made

    def z_copies(ref, own, halo, base):
        made = []
        for n, (begin, to, level) in enumerate(
            ((own, 0, up), (halo, own + halo, down))
        ):
            made.append(
                pltpu.make_async_remote_copy(
                    src_ref=ref.at[pl.ds(begin, halo)], dst_ref=ref.at[pl.ds(to, halo)],
                    send_sem=send_sem.at[base + n], recv_sem=recv_sem.at[base + n],
                    device_id=(me, level), device_id_type=MESH,
                )
            )
        return made

    def start(copies):
        for copy in copies:
            copy.start()

    def wait(copies):
        for copy in copies:
            copy.wait()

    copies0 = x_copies(xs0, xr0, xd0.at[1], xd0.at[0], xc0, 0) + z_copies(b0, 32, 2, 6) + z_copies(f0, 32, 1, 8)
    start(copies0)

    def stack_copy(k, which, slot):
        return pltpu.make_async_remote_copy(
            src_ref=xa.at[which], dst_ref=ga.at[which, slot[0], slot[1]],
            send_sem=zsend.at[which, k], recv_sem=zrecv.at[which, k],
            device_id=stack_peer(k), device_id_type=MESH,
        )

    def chip_copy(k, which, slot):
        return pltpu.make_async_remote_copy(
            src_ref=xb.at[which], dst_ref=gb_all.at[which, pl.ds(2 * slot, 2)],
            send_sem=bsend.at[which, k], recv_sem=brecv.at[which, k],
            device_id=chip_peer(k), device_id_type=MESH,
        )

    def stack_from(k):
        return lax.rem(core + k, 2), lax.rem(sub - k // 2 + ns, ns)

    def chip_from(k):
        return lax.rem(chip - k + chips, chips)

    def send_all(make, which, mine, count):
        def body(k, carry):
            make(k, which, mine).start()
            return carry
        lax.fori_loop(1, count, body, 0)

    def wait_all(make, which, source, count):
        def body(k, carry):
            copy = make(k, which, source(k))
            copy.wait_send()
            copy.wait_recv()
            return carry
        lax.fori_loop(1, count, body, 0)

    slot_at = (iota((ns, lanes_n), 1) // 4) % ns
    row_at = iota((ns, lanes_n), 0)

    def gather_start(x, which):
        tile = to_slots(x)
        for h in range(16 // ns):
            part = jnp.where(row_at == slot_at, tile[h * ns:(h + 1) * ns], 0.0)
            part = jnp.sum(part, axis=0, keepdims=True)
            xa[which, pl.ds(h, 1)] = part
            ga[which, core, sub, pl.ds(h, 1)] = part
        send_all(stack_copy, which, (core, sub), 2 * ns)

    def gather_turn(which):
        wait_all(stack_copy, which, stack_from, 2 * ns)
        for c in range(2):
            for h in range(16 // ns):
                tile = jnp.zeros((ns, lanes_n), F32)
                for k in range(ns):
                    part = jnp.broadcast_to(ga[which, c, k, pl.ds(h, 1)], (ns, lanes_n))
                    part = pltpu.roll(part, 0, 1, stride=4, stride_axis=0)
                    part = turn(part, (4 * (k - ns + 1)) % lanes_n, 1)
                    tile = jnp.where(slot_at == k, part, tile)
                xb[which, c, pl.ds(h * ns, ns)] = tile
                gb_all[which, 2 * chip + c, pl.ds(h * ns, ns)] = tile
        send_all(chip_copy, which, chip, chips)

    def gather_end(which):
        wait_all(chip_copy, which, chip_from, chips)
        rows = gb_all[which].reshape(nb * 16, lanes_n)
        return pick_left(onehot[...], rows).reshape(vn, 8, lanes_n)

    copies_b1 = x_copies(xs1b, xr1b, xs1b.at[1], xs1b.at[0], xc1b, 10)
    copies_b1 = copies_b1 + z_copies(b1, 16, 6, 16)
    start(copies_b1)

    each(5, 2, 32, start_plane)
    each(2, 1, 15, pair_r)
    wait(copies0)

    @pl.when(floor)
    def _():
        b0[pl.ds(0, 2)] = jnp.zeros((2, 32, 128), F32)
        f0[pl.ds(0, 1)] = jnp.zeros((1, 32, 128), F32)

    @pl.when(roof)
    def _():
        b0[pl.ds(34, 2)] = jnp.zeros((2, 32, 128), F32)
        f0[pl.ds(33, 1)] = jnp.zeros((1, 32, 128), F32)

    quarter = lane % 4
    group = lane // 4
    q0, q3 = quarter == 0, quarter == 3
    turn_l1 = lax.rem(129 - width_left + 128, 128)
    turn_l2 = lax.rem(130 - width_left + 128, 128)

    def ghost(from_left, from_right, near_by):
        shift_l = turn_l1 if near_by == 1 else turn_l2
        return jnp.where(
            q0, turn(from_left, shift_l, 1),
            jnp.where(q3, turn(from_right, lax.rem(width - near_by, 128), 1), 0.0),
        )

    ghost_b = ghost(xr0[0, 0], xr0[1, 0], 1)

    def ghost_corner(n, z, outside):
        from_left, from_right = xc0[0, n], xc0[1, n]
        rows = []
        for q in range(4):
            at_left = turn(from_left, (128 + 4 * z - 4 - q) % 128, 1)
            at_right = turn(from_right, lax.rem(4 * z + width + 127 - q, 128), 1)
            rows.append(jnp.where(
                lane[:8] == 4 * z, at_left,
                jnp.where(lane[:8] == lax.rem(4 * z + width - 1, 128), at_right, 0.0),
            ))
        return jnp.where(outside, 0.0, jnp.concatenate(rows, 0))

    ghost_b_low = ghost_corner(0, 31, floor)
    ghost_b_high = ghost_corner(1, 0, roof)
    ghost_b_far = ghost(xr0[0, 0], xr0[1, 0], 2)
    ghost_f = ghost(xr0[0, 1], xr0[1, 1], 1)
    own_edge = jnp.where(q0 | q3, tb, 0.0)
    turned = width // 4 - 1
    first_z = (q0 & (group == 0)) | (q3 & (group == turned))
    last_z = (q0 & (group == 31)) | (q3 & (group == lax.rem(31 + turned, 32)))

    def beside(tile, low, high):
        return (
            turn(tile, 1, 0) + turn(tile, 31, 0)
            + turn(jnp.where(first_z, high, tile), 124, 1)
            + turn(jnp.where(last_z, low, tile), 4, 1)
        )

    ghost_k = ghost_b + own_edge
    ghost_sum = 6.0 * ghost_b + ghost_b_far + own_edge
    ghost_sum = ghost_sum + beside(ghost_b, ghost_b_low, ghost_b_high)
    ghost_u = (2.0 * OMEGA) * ghost_f / jnp.maximum(ghost_sum, TINY)

    below = turn(jnp.where(edge, b0[1], 0.0), 124, 1)
    above = jnp.where(edge, b0[34], 0.0)
    edge_part = 6.0 * own_edge + beside(own_edge, below, above)
    edge_part = edge_part + jnp.where(q0, turn(tb, 127, 1), turn(tb, 1, 1))
    without = (edge_part - own_edge)
    edge_w = (2.0 * OMEGA) / jnp.maximum(without + ghost_k, TINY)
    edge_w = jnp.where(q0 | q3, edge_w, 0.0)
    drift = edge_w * tf - jnp.where(
        q0 | q3, (2.0 * OMEGA) * tf / jnp.maximum(without, TINY), 0.0
    )
    drift_v = own_edge * drift
    gap = own_edge * beside(drift, 0.0, 0.0) + beside(drift_v, 0.0, 0.0) + ghost_k * ghost_u
    gap = jnp.where(
        q0 | q3, gap,
        jnp.where(
            quarter == 1, (tb + turn(own_edge, 1, 1)) * turn(drift, 1, 1),
            (tb + turn(own_edge, 127, 1)) * turn(drift, 127, 1),
        ),
    )
    gap = 0.5 * gap
    gap_pair = gap + turn(gap, 124, 1)

    def back(tile, z):
        return turn(tile, lax.rem(128 - 4 * z, 128), 1)

    start_plane(0, jnp.where(edge, turn(ghost_b_low + below, 4, 1), 0.0))
    start_plane(1)
    start_plane(32)
    start_plane(33, jnp.where(edge, ghost_b_high + above, 0.0))
    pair_r(0)
    pair_r(15)

    def mend(k):
        rs[k] = rs[k] + jnp.where(edge_two, back(gap_pair, 2 * k), 0.0)

    each(4, 0, 16, mend)

    def join(ref, xr, xc, halo):
        at = iota((16, 128), 1)
        inside = at < half
        keep = ((at >= half) & (at < half + halo)) | (at >= 128 - halo)
        sub_at = at % 16

        def beside_own(from_left, from_right):
            from_left = turn(from_left, lax.rem(256 - half_left, 128), 1)
            from_right = turn(from_right, half, 1)
            return jnp.where(
                sub_at >= 16 - halo, from_left, jnp.where(sub_at < halo, from_right, 0.0)
            )

        tiles = [beside_own(xr[0, n], xr[1, n]) for n in range(2)]
        low = beside_own(xc[0, 0], xc[1, 0])
        high = beside_own(xc[0, 1], xc[1, 1])
        for z in range(-halo, 16 + halo):
            tile = low if z < 0 else (high if z >= 16 else tiles[z // 8])
            plane = jnp.where(
                inside, ref[z + halo],
                jnp.where(keep, turn(tile, (128 - 16 * (z % 8)) % 128, 1), 0.0),
            )
            if z < 0:
                plane = jnp.where(floor, 0.0, plane)
            if z >= 16:
                plane = jnp.where(roof, 0.0, plane)
            ref[z + halo] = plane

    def only_inside(x, out):
        n = x.shape[0]
        return jnp.concatenate([
            jnp.where(floor, 0.0, x[:out]), x[out:n - out], jnp.where(roof, 0.0, x[n - out:])
        ], 0)

    def weights(b, step):
        n = b.shape[0]
        middle = b[1:n - 1]
        total = around(middle, step) + b[:n - 2] + b[2:]
        return OMEGA / jnp.maximum(3.0 * middle + 0.5 * total, TINY)

    def gain_of(b, u, v, step):
        n = u.shape[0]
        return b * (around(u[1:n - 1], step) + u[:n - 2] + u[2:]) + (
            around(v[1:n - 1], step) + v[:n - 2] + v[2:]
        )

    def begin_level(b_ref, f_ref, w_ref, u_ref, step):
        n = f_ref.shape[0]
        f = f_ref[...]
        u = w_ref[...] * f
        u_ref[...] = u
        v = b_ref[pl.ds(1, n)] * u
        gain = gain_of(b_ref[pl.ds(2, n - 2)], u, v, step)
        return REST * f[1:n - 1] + 0.5 * gain

    def end_level(b_ref, f_ref, w_ref, u, step):
        n = u.shape[0]
        skip = (f_ref.shape[0] - n) // 2 + 1
        v = b_ref[pl.ds(skip, n)] * u
        b = b_ref[pl.ds(skip + 1, n - 2)]
        gain = gain_of(b, u, v, step)
        return only_inside(REST * u[1:n - 1] + w_ref[pl.ds(skip, n - 2)] * (
            f_ref[pl.ds(skip, n - 2)] + 0.5 * gain
        ), 1)

    own_f1 = 0.5 * squeeze_level0()
    f1[pl.ds(5, 16)] = own_f1
    pack(own_f1, xs1f, 5)
    copies_f1 = x_copies(xs1f, xr1f, xs1f.at[1], xs1f.at[0], xc1f, 18)
    copies_f1 = copies_f1 + z_copies(f1, 16, 5, 24)
    start(copies_f1)
    gather_start(0.125 * coarsen(own_b2, y2, 2), 0)

    def prepare(z, odd):
        e = z + 1
        w = jnp.where(edge, back(edge_w, z), w0[e])
        r = r0[z] + jnp.where(edge_two, back(gap, z), 0.0)
        out[z] = jnp.where(live, w * (f0[e] + r), 0.0)
        px, py, b = kx[e], ky[e], b0[e + 1]
        px_low, py_low = turn(px, 1, 1), turn(py, 1, 0)
        pz_low, pz = b0[e] + b, b + b0[e + 2]
        even_x, even_y = lane % 2 == 0, iota((32, 128), 0) % 2 == 0
        rim = jnp.where(edge, back(ghost_k, z), 0.0)
        same = jnp.where(even_x, px, px_low) + jnp.where(even_y, py, py_low)
        same = same + (pz_low if odd else pz)
        w = jnp.where(live, 0.5 * w, 0.0)
        c0[z] = REST + w * same
        cx[z] = w * (jnp.where(even_x, px_low, px) + rim)
        cy[z] = w * jnp.where(even_y, py_low, py)
        cz[z] = w * (pz if odd else pz_low)

    def prepare_pair(k):
        prepare(2 * k, False)
        prepare(2 * k + 1, True)

    wait(copies_b1)
    join(b1, xr1b, xc1b, 6)
    w1[...] = weights(b1[...], 1)
    b2[...] = 0.125 * coarsen(b1[...], y1, 1)
    w2[...] = weights(b2[...], 2)

    wait(copies_f1)
    join(f1, xr1f, xc1f, 5)
    r1 = begin_level(b1, f1, w1, u1, 1)
    f2[...] = only_inside(0.5 * coarsen(r1, y1, 1), 2)
    r2 = begin_level(b2, f2, w2, u2, 2)
    gather_start(0.5 * coarsen(r2[1:9], y2, 2), 1)
    gather_turn(0)
    each(1, 0, 8, prepare_pair)
    gather_turn(1)
    each(1, 8, 16, prepare_pair)

    not_top = iota((vn, 8, lanes_n), 2) % nz3 < nz3 - 1

    def next_x(p):
        return jnp.concatenate([p[1:], turn(p[:1], 7, 1)], 0)

    def last_x(p):
        return jnp.concatenate([turn(p[vn - 1:], 1, 1), p[:vn - 1]], 0)

    def total3(x):
        tile = jnp.sum(x, axis=0)
        return jnp.sum(jnp.sum(tile, axis=0, keepdims=True), axis=1, keepdims=True)

    coarse_b = gather_end(0)
    px = 0.5 * (coarse_b + next_x(coarse_b))
    py = 0.5 * (coarse_b + turn(coarse_b, lanes_n - nz3, 2))
    pz = jnp.where(not_top, 0.5 * (coarse_b + turn(coarse_b, lanes_n - 1, 2)), 0.0)
    ends = jnp.where(
        not_top, 0.0, 0.5 * coarse_b
    ) + jnp.where(iota((vn, 8, lanes_n), 2) % nz3 == 0, 0.5 * coarse_b, 0.0)
    kx3[...] = px
    ky3[...] = py
    kz3[...] = pz
    coarse_d = px + last_x(px) + py + turn(py, nz3, 2) + pz + turn(pz, 1, 2) + ends
    d3[...] = coarse_d
    i3[...] = 1.0 / coarse_d

    coarse_f = gather_end(1)
    r3[...] = coarse_f
    s3[...] = jnp.zeros((vn, 8, lanes_n), F32)
    p3[...] = jnp.zeros((vn, 8, lanes_n), F32)
    m3[...] = jnp.zeros((vn, 8, lanes_n), F32)

    def image(p):
        px, py, pz = kx3[...], ky3[...], kz3[...]
        return d3[...] * p - (
            px * next_x(p) + last_x(px * p)
            + py * turn(p, lanes_n - nz3, 2) + turn(py * p, nz3, 2)
            + pz * turn(p, lanes_n - 1, 2) + turn(pz * p, 1, 2)
        )

    def iterate(n, carry):
        gamma_old, alpha_old = carry
        r = r3[...]
        z = r * i3[...]
        az = image(z)
        gamma, delta = total3(r * z), total3(z * az)
        beta = 0.0 if n == 0 else gamma / gamma_old
        alpha = gamma / (delta - beta * gamma / alpha_old)
        p = z + beta * p3[...]
        q = az + beta * m3[...]
        p3[...] = p
        m3[...] = q
        s3[...] = s3[...] + alpha * p
        r3[...] = r - alpha * q
        return gamma, alpha

    one = jnp.ones((1, 1), F32)
    carry = (one, one)
    for n in range(SWEEPS):
        carry = iterate(n, carry)
    solved = s3[...]

    l_at, k_at = iota((128, 8 * vn), 0), iota((128, 8 * vn), 1)
    relative = jnp.where(l_at < 124, l_at // 4, -1)
    wanted = lax.rem(4 * my_start + relative + 8 * vn, 8 * vn)
    from_x = ones_where((k_at % 8) * vn + k_at // 8 == wanted)
    by_lane = pick_left(from_x, solved.reshape(8 * vn, lanes_n))
    q_at, r_at = iota((48, lanes_n), 0), iota((48, lanes_n), 1)
    z_at = 4 * sub + q_at // 8 - 1
    from_row = ones_where(
        (r_at == ((q_at % 8) // 2) * nz3 + z_at) & (z_at >= 0) & (z_at < nz3)
    )
    e3 = pick_left_t(from_row, by_lane).reshape(6, 1, 8, 128)
    e3 = jnp.broadcast_to(e3, (6, 2, 8, 128)).reshape(12, 8, 128)

    e2 = end_level(b2, f2, w2, u2[...] + e3, 2)
    e1x[:, pl.ds(0, 8, stride=2), :] = e2
    e1x[:, pl.ds(1, 8, stride=2), :] = e2
    grown = jnp.broadcast_to(e1x[...].reshape(10, 1, 16, 128), (10, 2, 16, 128))
    e1 = end_level(b1, f1, w1, u1[pl.ds(3, 20)] + grown.reshape(20, 16, 128), 1)

    si, sc = iota((128, 256), 0), iota((128, 256), 1)
    sx = sc - 128
    step = jnp.where(sx % 2 == 0, sx // 2 - 1, sx // 2 + 1)
    step = jnp.where(step < 0, 127, step)
    stretch = ones_where(
        ((sc < width) & (si == sc // 2)) | ((sx >= 0) & (sx < width) & (si == step))
    )
    wide = pick_right(e1.reshape(288, 128), stretch)
    main = wide[:, :128].reshape(18, 16, 128)
    side = wide[:, 128:].reshape(18, 16, 128)
    e0m[:, pl.ds(0, 16, stride=2), :] = main
    e0m[:, pl.ds(1, 16, stride=2), :] = main
    e0x[:, pl.ds(0, 16, stride=2), :] = side
    e0x[:, pl.ds(1, 16, stride=2), :] = side
    e0y[:, pl.ds(0, 16, stride=2), :] = turn(main, 1, 1)
    e0y[:, pl.ds(1, 16, stride=2), :] = turn(main, 15, 1)

    def finish_pair(k):
        e, ex, ey = e0m[k + 1], e0x[k + 1], e0y[k + 1]
        for z, ez in ((2 * k, e0m[k]), (2 * k + 1, e0m[k + 2])):
            out[z] = out[z] + c0[z] * e + cx[z] * ex + cy[z] * ey + cz[z] * ez

    each(2, 0, 16, finish_pair)


def per_device(nb, ns, source, beta, counts):
    lanes_n = 16 * ns

    def vmem(*shape, dtype=F32):
        return pltpu.VMEM(shape, dtype)

    def coarse():
        return vmem(nb, 8, lanes_n)

    scratch = [
        vmem(36, 32, 128), vmem(34, 32, 128), vmem(34, 32, 128), vmem(34, 32, 128),
        vmem(32, 32, 128), vmem(34, 32, 128), vmem(34, 32, 128),
        vmem(16, 32, 128), vmem(2, 32, 128), vmem(2, 2, 32, 128), vmem(2, 8, 128), vmem(2, 2, 8, 128),
        vmem(18, 32, 128), vmem(18, 32, 128), vmem(18, 32, 128),
        vmem(32, 32, 128), vmem(32, 32, 128), vmem(32, 32, 128), vmem(32, 32, 128),
        vmem(28, 16, 128), vmem(26, 16, 128), vmem(26, 16, 128), vmem(26, 16, 128),
        vmem(2, 16, 128), vmem(2, 2, 16, 128), vmem(2, 2, 16, 128),
        vmem(2, 16, 128), vmem(2, 2, 16, 128), vmem(2, 2, 16, 128),
        vmem(14, 16, 128), vmem(10, 16, 128),
        vmem(14, 8, 128), vmem(12, 8, 128), vmem(12, 8, 128), vmem(12, 8, 128), vmem(4, 8, 128),
        vmem(32, 128), vmem(128, lanes_n), vmem(2, 16 // ns, lanes_n), vmem(2, 2, ns, 16 // ns, lanes_n),
        vmem(2, 2, 16, lanes_n), vmem(2, nb, 16, lanes_n), vmem(8 * nb, 16 * nb, dtype=BF16),
        coarse(), coarse(), coarse(), coarse(), coarse(), coarse(), coarse(), coarse(), coarse(),
        pltpu.SemaphoreType.DMA((2,)),
        pltpu.SemaphoreType.DMA((26,)), pltpu.SemaphoreType.DMA((26,)),
        pltpu.SemaphoreType.DMA((2, 2 * ns)), pltpu.SemaphoreType.DMA((2, 2 * ns)),
        pltpu.SemaphoreType.DMA((2, nb // 2)), pltpu.SemaphoreType.DMA((2, nb // 2)),
    ]
    return pl.pallas_call(
        functools.partial(kernel, nb, ns),
        out_shape=jax.ShapeDtypeStruct(source.shape, F32),
        in_specs=[
            pl.BlockSpec(memory_space=pltpu.SMEM),
            pl.BlockSpec(memory_space=pl.ANY),
            pl.BlockSpec(memory_space=pl.ANY),
        ],
        out_specs=pl.BlockSpec(memory_space=pltpu.VMEM),
        scratch_shapes=scratch,
        compiler_params=pltpu.CompilerParams(
            collective_id=0, has_side_effects=True, vmem_limit_bytes=62 * 1024 * 1024
        ),
    )(counts, source, beta)


def solution(mesh):
    in_specs = (P("sub", None, "box"), P("sub", None, "box"), P())
    out_specs = P("sub", None, "box")
    return jax.shard_map(
        functools.partial(per_device, mesh.shape["box"], mesh.shape["sub"]),
        mesh=mesh, in_specs=in_specs, out_specs=out_specs, check_vma=False,
    )
```

```python
import functools
import jax
import jax.numpy as jnp
from jax import lax
from jax.experimental import pallas as pl
from jax.experimental.pallas import tpu as pltpu
from jax.sharding import PartitionSpec as P

CAP = 4
SWEEPS = 8
OMEGA = 0.8
REST = 0.2
TINY = 1e-20
F32 = jnp.float32
BF16 = jnp.bfloat16
MESH = pl.DeviceIdType.MESH


def split(x):
    high = x.astype(BF16)
    middle = (x - high.astype(F32)).astype(BF16)
    return (high, middle)


def pick_right(x, chosen):
    return sum(jnp.dot(part, chosen, preferred_element_type=F32) for part in split(x))


def pick_left(chosen, x):
    return sum(jnp.dot(chosen, part, preferred_element_type=F32) for part in split(x))


def pick_left_t(chosen, x):
    return sum(
        lax.dot_general(chosen, part, (((1,), (1,)), ((), ())), preferred_element_type=F32)
        for part in split(x)
    )


def ones_where(mask):
    return jnp.where(mask, 1.0, 0.0).astype(BF16)


def iota(shape, dim):
    return lax.broadcasted_iota(jnp.int32, shape, dim)


def turn(x, shift, axis):
    return pltpu.roll(x, shift, axis)


def around(x, step):
    rows = x.shape[-2]
    ax, ay = x.ndim - 1, x.ndim - 2
    return (
        turn(x, step, ax) + turn(x, 128 - step, ax) + turn(x, 1, ay) + turn(x, rows - 1, ay)
    )


def kernel(
    nb, ns,
    counts, source, beta, out,
    b0, f0, u0, w0, r0, kx, ky, rs, xs0, xr0, xd0, xc0, e0m, e0x, e0y, c0, cx, cy, cz,
    b1, f1, u1, w1, xs1b, xr1b, xc1b, xs1f, xr1f, xc1f, y1, e1x,
    b2, f2, u2, w2, y2,
    t3, tx, xa, ga, xb, gb_all, onehot, kx3, ky3, kz3, d3, i3, p3, m3, r3, s3,
    in_sem, send_sem, recv_sem, zsend, zrecv, bsend, brecv,
):
    lanes_n = 16 * ns
    nz3 = 4 * ns
    vn = nb
    me, sub = lax.axis_index("box"), lax.axis_index("sub")
    left, right = lax.rem(me + nb - 1, nb), lax.rem(me + 1, nb)
    down, up = lax.rem(sub + ns - 1, ns), lax.rem(sub + 1, ns)
    floor, roof = sub == 0, sub == ns - 1

    get_b = pltpu.make_async_copy(beta, b0.at[pl.ds(2, 32)], in_sem.at[0])
    get_f = pltpu.make_async_copy(source, f0.at[pl.ds(1, 32)], in_sem.at[1])
    get_b.start()
    get_f.start()

    core, chip, chips = lax.rem(me, 2), me // 2, nb // 2

    def stack_peer(k):
        return 2 * chip + lax.rem(core + k, 2), lax.rem(sub + k // 2, ns)

    def chip_peer(k):
        return 2 * lax.rem(chip + k, chips) + core, sub

    barrier = pltpu.get_barrier_semaphore()

    def greet(peer):
        def body(k, carry):
            pl.semaphore_signal(barrier, inc=1, device_id=peer(k), device_id_type=MESH)
            return carry
        return body

    for there in (left, right):
        for level in (down, sub, up):
            pl.semaphore_signal(barrier, inc=1, device_id=(there, level), device_id_type=MESH)
    lax.fori_loop(1, 2 * ns, greet(stack_peer), 0)
    lax.fori_loop(1, chips, greet(chip_peer), 0)

    width = 32 * counts[me]
    width_left = 32 * counts[left]
    half = width // 2
    half_left = width_left // 2
    kk = iota((1, nb * 16), 1)
    kd, kj = kk // 16, (kk % 16) // ns * ns + ns - 1 - kk % ns

    def place(d, carry):
        where_from, begin, mine = carry
        here = counts[d]
        value = jnp.where(kj < 4 * here, 4 * begin + kj, -1)
        where_from = jnp.where(kd == d, value, where_from)
        mine = jnp.where(d == me, begin, mine)
        return where_from, begin + here, mine

    where_from, _, my_start = lax.fori_loop(
        0, nb, place, (jnp.full((1, nb * 16), -1, jnp.int32), jnp.int32(0), jnp.int32(0))
    )
    row = iota((8 * vn, nb * 16), 0)
    onehot[...] = ones_where((row % 8) * vn + row // 8 == where_from)

    lane = iota((32, 128), 1)
    live = lane < width
    edge = (lane == 0) | (lane == width - 1)
    edge_two = (lane < 2) | ((lane >= width - 2) & live)
    inner = lane < width - 1

    ll = iota((128, 128), 0)
    lc = iota((128, 128), 1)
    squeeze = ones_where((ll // 2 == lc) & (ll < width))

    get_b.wait()
    get_f.wait()

    def each(count, first, last, act):
        def body(n, carry):
            for k in range(count):
                act(first + n * count + k)
            return carry
        lax.fori_loop(0, (last - first) // count, body, 0)

    def load_planes(n, carry):
        tb, tf = carry
        for k in range(4):
            z = 4 * n + k
            b = jnp.where(live, b0[z + 2], 0.0)
            f = jnp.where(live, f0[z + 1], 0.0)
            b0[z + 2] = b
            f0[z + 1] = f
            tb = tb + turn(jnp.where(edge_two, b, 0.0), 4 * z, 1)
            tf = tf + turn(jnp.where(edge, f, 0.0), 4 * z, 1)
        return tb, tf

    zero_tile = jnp.zeros((32, 128), F32)
    tb, tf = lax.fori_loop(0, 8, load_planes, (zero_tile, zero_tile))
    xs0[0] = tb
    xs0[1] = tf
    for n, z in ((0, 0), (1, 31)):
        corner = jnp.zeros((8, 128), F32)
        for m, shift in ((0, (128 - 4 * z) % 128), (4, lax.rem(389 - 4 * z - width, 128))):
            column = jnp.where(lane == m, turn(tb, shift, 1), 0.0)
            for q in range(4):
                corner = corner + turn(column[8 * q:8 * q + 8], q, 1)
        xd0[n] = corner


    def squeeze_level0():
        both = rs[:, pl.ds(0, 16, stride=2), :] + rs[:, pl.ds(1, 16, stride=2), :]
        return pick_right(both.reshape(256, 128), squeeze).reshape(16, 16, 128)

    def coarsen(x, scratch, step):
        planes, rows, _ = x.shape
        n = planes // 2
        pairs = x.reshape(n, 2, rows, 128)
        scratch[pl.ds(0, n)] = pairs[:, 0] + pairs[:, 1]
        y = (
            scratch[pl.ds(0, n), pl.ds(0, rows // 2, stride=2), :]
            + scratch[pl.ds(0, n), pl.ds(1, rows // 2, stride=2), :]
        )
        odd = (iota(y.shape, 2) // step) % 2 == 1
        return y + jnp.where(odd, turn(y, step, 2), turn(y, 128 - step, 2))

    def pack(x, tile_ref, reach):
        at = iota((16, 128), 1)
        keep = (at < reach) | ((at >= half - reach) & (at < half))
        for n in range(2):
            total = jnp.zeros((16, 128), F32)
            for z in range(8):
                total = total + turn(jnp.where(keep, x[8 * n + z], 0.0), 16 * z, 1)
            tile_ref[n] = total

    def to_slots(x):
        for z in range(4):
            t3[pl.ds(z, 4, stride=8), :] = x[z]
            t3[pl.ds(z + 4, 4, stride=8), :] = x[z]
        tiles = t3[pl.ds(0, 32)].reshape(4, 1, 8, 128)
        tiles = jnp.broadcast_to(tiles, (4, ns // 2, 8, 128)).reshape(lanes_n, 128)
        tx[...] = jnp.transpose(tiles)
        return tx[pl.ds(0, 16, stride=4), :]

    def pair_b(k):
        rs[k] = b0[2 * k + 2] + b0[2 * k + 3]

    each(4, 0, 16, pair_b)
    own_b1 = 0.125 * squeeze_level0()
    b1[pl.ds(6, 16)] = own_b1
    pack(own_b1, xs1b, 6)
    own_b2 = 0.125 * coarsen(own_b1, y1, 1)

    def couple(e):
        b = b0[e + 1]
        px = jnp.where(inner, b + turn(b, 127, 1), 0.0)
        py = b + turn(b, 31, 0)
        kx[e] = px
        ky[e] = py
        return px + turn(px, 1, 1) + py + turn(py, 1, 0) + (b0[e] + b) + (b + b0[e + 2])

    def start_plane(e, more=0.0):
        w = (2.0 * OMEGA) / jnp.maximum(couple(e) + more, TINY)
        w0[e] = w
        u0[e] = w * f0[e]

    def pull(e):
        u, px, py, b = u0[e], kx[e], ky[e], b0[e + 1]
        return (
            px * turn(u, 127, 1) + turn(px * u, 1, 1) + py * turn(u, 31, 0) + turn(py * u, 1, 0)
            + (b0[e] + b) * u0[e - 1] + (b + b0[e + 2]) * u0[e + 1]
        )

    def residual(z):
        r = REST * f0[z + 1] + 0.5 * pull(z + 1)
        r0[z] = r
        return r

    def pair_r(k):
        rs[k] = residual(2 * k) + residual(2 * k + 1)


    pl.semaphore_wait(barrier, 6 + (2 * ns - 1) + (chips - 1))

    def x_copies(src, dst, for_up, for_down, corner, base):
        made = []
        for side, there in ((0, right), (1, left)):
            for n, (begin, end, level) in enumerate((
                (src, dst.at[side], sub),
                (for_up, corner.at[side, 0], up),
                (for_down, corner.at[side, 1], down),
            )):
                at = base + side * 3 + n
                made.append(
                    pltpu.make_async_remote_copy(
                        src_ref=begin, dst_ref=end,
                        send_sem=send_sem.at[at], recv_sem=recv_sem.at[at],
                        device_id=(there, level), device_id_type=MESH,
                    )
                )
        return made

    def z_copies(ref, own, halo, base):
        made = []
        for n, (begin, to, level) in enumerate(
            ((own, 0, up), (halo, own + halo, down))
        ):
            made.append(
                pltpu.make_async_remote_copy(
                    src_ref=ref.at[pl.ds(begin, halo)], dst_ref=ref.at[pl.ds(to, halo)],
                    send_sem=send_sem.at[base + n], recv_sem=recv_sem.at[base + n],
                    device_id=(me, level), device_id_type=MESH,
                )
            )
        return made

    def start(copies):
        for copy in copies:
            copy.start()

    def wait(copies):
        for copy in copies:
            copy.wait()

    copies0 = x_copies(xs0, xr0, xd0.at[1], xd0.at[0], xc0, 0) + z_copies(b0, 32, 2, 6) + z_copies(f0, 32, 1, 8)
    start(copies0)

    def stack_copy(k, which, slot):
        return pltpu.make_async_remote_copy(
            src_ref=xa.at[which], dst_ref=ga.at[which, slot[0], slot[1]],
            send_sem=zsend.at[which, k], recv_sem=zrecv.at[which, k],
            device_id=stack_peer(k), device_id_type=MESH,
        )

    def chip_copy(k, which, slot):
        return pltpu.make_async_remote_copy(
            src_ref=xb.at[which], dst_ref=gb_all.at[which, pl.ds(2 * slot, 2)],
            send_sem=bsend.at[which, k], recv_sem=brecv.at[which, k],
            device_id=chip_peer(k), device_id_type=MESH,
        )

    def stack_from(k):
        return lax.rem(core + k, 2), lax.rem(sub - k // 2 + ns, ns)

    def chip_from(k):
        return lax.rem(chip - k + chips, chips)

    def send_all(make, which, mine, count):
        def body(k, carry):
            make(k, which, mine).start()
            return carry
        lax.fori_loop(1, count, body, 0)

    def wait_all(make, which, source, count):
        def body(k, carry):
            copy = make(k, which, source(k))
            copy.wait_send()
            copy.wait_recv()
            return carry
        lax.fori_loop(1, count, body, 0)

    slot_at = (iota((ns, lanes_n), 1) // 4) % ns
    row_at = iota((ns, lanes_n), 0)

    def gather_start(x, which):
        tile = to_slots(x)
        for h in range(16 // ns):
            part = jnp.where(row_at == slot_at, tile[h * ns:(h + 1) * ns], 0.0)
            part = jnp.sum(part, axis=0, keepdims=True)
            xa[which, pl.ds(h, 1)] = part
            ga[which, core, sub, pl.ds(h, 1)] = part
        send_all(stack_copy, which, (core, sub), 2 * ns)

    def gather_turn(which):
        wait_all(stack_copy, which, stack_from, 2 * ns)
        for c in range(2):
            for h in range(16 // ns):
                tile = jnp.zeros((ns, lanes_n), F32)
                for k in range(ns):
                    part = jnp.broadcast_to(ga[which, c, k, pl.ds(h, 1)], (ns, lanes_n))
                    part = pltpu.roll(part, 0, 1, stride=4, stride_axis=0)
                    part = turn(part, (4 * (k - ns + 1)) % lanes_n, 1)
                    tile = jnp.where(slot_at == k, part, tile)
                xb[which, c, pl.ds(h * ns, ns)] = tile
                gb_all[which, 2 * chip + c, pl.ds(h * ns, ns)] = tile
        send_all(chip_copy, which, chip, chips)

    def gather_end(which):
        wait_all(chip_copy, which, chip_from, chips)
        rows = gb_all[which].reshape(nb * 16, lanes_n)
        return pick_left(onehot[...], rows).reshape(vn, 8, lanes_n)

    copies_b1 = x_copies(xs1b, xr1b, xs1b.at[1], xs1b.at[0], xc1b, 10)
    copies_b1 = copies_b1 + z_copies(b1, 16, 6, 16)
    start(copies_b1)

    each(5, 2, 32, start_plane)
    each(2, 1, 15, pair_r)
    wait(copies0)

    @pl.when(floor)
    def _():
        b0[pl.ds(0, 2)] = jnp.zeros((2, 32, 128), F32)
        f0[pl.ds(0, 1)] = jnp.zeros((1, 32, 128), F32)

    @pl.when(roof)
    def _():
        b0[pl.ds(34, 2)] = jnp.zeros((2, 32, 128), F32)
        f0[pl.ds(33, 1)] = jnp.zeros((1, 32, 128), F32)

    quarter = lane % 4
    group = lane // 4
    q0, q3 = quarter == 0, quarter == 3
    turn_l1 = lax.rem(129 - width_left + 128, 128)
    turn_l2 = lax.rem(130 - width_left + 128, 128)

    def ghost(from_left, from_right, near_by):
        shift_l = turn_l1 if near_by == 1 else turn_l2
        return jnp.where(
            q0, turn(from_left, shift_l, 1),
            jnp.where(q3, turn(from_right, lax.rem(width - near_by, 128), 1), 0.0),
        )

    ghost_b = ghost(xr0[0, 0], xr0[1, 0], 1)

    def ghost_corner(n, z, outside):
        from_left, from_right = xc0[0, n], xc0[1, n]
        rows = []
        for q in range(4):
            at_left = turn(from_left, (128 + 4 * z - 4 - q) % 128, 1)
            at_right = turn(from_right, lax.rem(4 * z + width + 127 - q, 128), 1)
            rows.append(jnp.where(
                lane[:8] == 4 * z, at_left,
                jnp.where(lane[:8] == lax.rem(4 * z + width - 1, 128), at_right, 0.0),
            ))
        return jnp.where(outside, 0.0, jnp.concatenate(rows, 0))

    ghost_b_low = ghost_corner(0, 31, floor)
    ghost_b_high = ghost_corner(1, 0, roof)
    ghost_b_far = ghost(xr0[0, 0], xr0[1, 0], 2)
    ghost_f = ghost(xr0[0, 1], xr0[1, 1], 1)
    own_edge = jnp.where(q0 | q3, tb, 0.0)
    turned = width // 4 - 1
    first_z = (q0 & (group == 0)) | (q3 & (group == turned))
    last_z = (q0 & (group == 31)) | (q3 & (group == lax.rem(31 + turned, 32)))

    def beside(tile, low, high):
        return (
            turn(tile, 1, 0) + turn(tile, 31, 0)
            + turn(jnp.where(first_z, high, tile), 124, 1)
            + turn(jnp.where(last_z, low, tile), 4, 1)
        )

    ghost_k = ghost_b + own_edge
    ghost_sum = 6.0 * ghost_b + ghost_b_far + own_edge
    ghost_sum = ghost_sum + beside(ghost_b, ghost_b_low, ghost_b_high)
    ghost_u = (2.0 * OMEGA) * ghost_f / jnp.maximum(ghost_sum, TINY)

    below = turn(jnp.where(edge, b0[1], 0.0), 124, 1)
    above = jnp.where(edge, b0[34], 0.0)
    edge_part = 6.0 * own_edge + beside(own_edge, below, above)
    edge_part = edge_part + jnp.where(q0, turn(tb, 127, 1), turn(tb, 1, 1))
    without = (edge_part - own_edge)
    edge_w = (2.0 * OMEGA) / jnp.maximum(without + ghost_k, TINY)
    edge_w = jnp.where(q0 | q3, edge_w, 0.0)
    drift = edge_w * tf - jnp.where(
        q0 | q3, (2.0 * OMEGA) * tf / jnp.maximum(without, TINY), 0.0
    )
    drift_v = own_edge * drift
    gap = own_edge * beside(drift, 0.0, 0.0) + beside(drift_v, 0.0, 0.0) + ghost_k * ghost_u
    gap = jnp.where(
        q0 | q3, gap,
        jnp.where(
            quarter == 1, (tb + turn(own_edge, 1, 1)) * turn(drift, 1, 1),
            (tb + turn(own_edge, 127, 1)) * turn(drift, 127, 1),
        ),
    )
    gap = 0.5 * gap
    gap_pair = gap + turn(gap, 124, 1)

    def back(tile, z):
        return turn(tile, lax.rem(128 - 4 * z, 128), 1)

    start_plane(0, jnp.where(edge, turn(ghost_b_low + below, 4, 1), 0.0))
    start_plane(1)
    start_plane(32)
    start_plane(33, jnp.where(edge, ghost_b_high + above, 0.0))
    pair_r(0)
    pair_r(15)

    def mend(k):
        rs[k] = rs[k] + jnp.where(edge_two, back(gap_pair, 2 * k), 0.0)

    each(4, 0, 16, mend)

    def join(ref, xr, xc, halo):
        at = iota((16, 128), 1)
        inside = at < half
        keep = ((at >= half) & (at < half + halo)) | (at >= 128 - halo)
        sub_at = at % 16

        def beside_own(from_left, from_right):
            from_left = turn(from_left, lax.rem(256 - half_left, 128), 1)
            from_right = turn(from_right, half, 1)
            return jnp.where(
                sub_at >= 16 - halo, from_left, jnp.where(sub_at < halo, from_right, 0.0)
            )

        tiles = [beside_own(xr[0, n], xr[1, n]) for n in range(2)]
        low = beside_own(xc[0, 0], xc[1, 0])
        high = beside_own(xc[0, 1], xc[1, 1])
        for z in range(-halo, 16 + halo):
            tile = low if z < 0 else (high if z >= 16 else tiles[z // 8])
            plane = jnp.where(
                inside, ref[z + halo],
                jnp.where(keep, turn(tile, (128 - 16 * (z % 8)) % 128, 1), 0.0),
            )
            if z < 0:
                plane = jnp.where(floor, 0.0, plane)
            if z >= 16:
                plane = jnp.where(roof, 0.0, plane)
            ref[z + halo] = plane

    def only_inside(x, out):
        n = x.shape[0]
        return jnp.concatenate([
            jnp.where(floor, 0.0, x[:out]), x[out:n - out], jnp.where(roof, 0.0, x[n - out:])
        ], 0)

    def weights(b, step):
        n = b.shape[0]
        middle = b[1:n - 1]
        total = around(middle, step) + b[:n - 2] + b[2:]
        return OMEGA / jnp.maximum(3.0 * middle + 0.5 * total, TINY)

    def gain_of(b, u, v, step):
        n = u.shape[0]
        return b * (around(u[1:n - 1], step) + u[:n - 2] + u[2:]) + (
            around(v[1:n - 1], step) + v[:n - 2] + v[2:]
        )

    def begin_level(b_ref, f_ref, w_ref, u_ref, step):
        n = f_ref.shape[0]
        f = f_ref[...]
        u = w_ref[...] * f
        u_ref[...] = u
        v = b_ref[pl.ds(1, n)] * u
        gain = gain_of(b_ref[pl.ds(2, n - 2)], u, v, step)
        return REST * f[1:n - 1] + 0.5 * gain

    def end_level(b_ref, f_ref, w_ref, u, step):
        n = u.shape[0]
        skip = (f_ref.shape[0] - n) // 2 + 1
        v = b_ref[pl.ds(skip, n)] * u
        b = b_ref[pl.ds(skip + 1, n - 2)]
        gain = gain_of(b, u, v, step)
        return only_inside(REST * u[1:n - 1] + w_ref[pl.ds(skip, n - 2)] * (
            f_ref[pl.ds(skip, n - 2)] + 0.5 * gain
        ), 1)

    own_f1 = 0.5 * squeeze_level0()
    f1[pl.ds(5, 16)] = own_f1
    pack(own_f1, xs1f, 5)
    copies_f1 = x_copies(xs1f, xr1f, xs1f.at[1], xs1f.at[0], xc1f, 18)
    copies_f1 = copies_f1 + z_copies(f1, 16, 5, 24)
    start(copies_f1)
    gather_start(0.125 * coarsen(own_b2, y2, 2), 0)

    def prepare(z, odd):
        e = z + 1
        w = jnp.where(edge, back(edge_w, z), w0[e])
        r = r0[z] + jnp.where(edge_two, back(gap, z), 0.0)
        out[z] = jnp.where(live, w * (f0[e] + r), 0.0)
        px, py, b = kx[e], ky[e], b0[e + 1]
        px_low, py_low = turn(px, 1, 1), turn(py, 1, 0)
        pz_low, pz = b0[e] + b, b + b0[e + 2]
        even_x, even_y = lane % 2 == 0, iota((32, 128), 0) % 2 == 0
        rim = jnp.where(edge, back(ghost_k, z), 0.0)
        same = jnp.where(even_x, px, px_low) + jnp.where(even_y, py, py_low)
        same = same + (pz_low if odd else pz)
        w = jnp.where(live, 0.5 * w, 0.0)
        c0[z] = REST + w * same
        cx[z] = w * (jnp.where(even_x, px_low, px) + rim)
        cy[z] = w * jnp.where(even_y, py_low, py)
        cz[z] = w * (pz if odd else pz_low)

    def prepare_pair(k):
        prepare(2 * k, False)
        prepare(2 * k + 1, True)

    wait(copies_b1)
    join(b1, xr1b, xc1b, 6)
    w1[...] = weights(b1[...], 1)
    b2[...] = 0.125 * coarsen(b1[...], y1, 1)
    w2[...] = weights(b2[...], 2)

    wait(copies_f1)
    join(f1, xr1f, xc1f, 5)
    r1 = begin_level(b1, f1, w1, u1, 1)
    f2[...] = only_inside(0.5 * coarsen(r1, y1, 1), 2)
    r2 = begin_level(b2, f2, w2, u2, 2)
    gather_start(0.5 * coarsen(r2[1:9], y2, 2), 1)
    gather_turn(0)
    each(1, 0, 8, prepare_pair)
    gather_turn(1)
    each(1, 8, 16, prepare_pair)

    not_top = iota((vn, 8, lanes_n), 2) % nz3 < nz3 - 1

    def next_x(p):
        return jnp.concatenate([p[1:], turn(p[:1], 7, 1)], 0)

    def last_x(p):
        return jnp.concatenate([turn(p[vn - 1:], 1, 1), p[:vn - 1]], 0)

    def total3(x):
        tile = jnp.sum(x, axis=0)
        return jnp.sum(jnp.sum(tile, axis=0, keepdims=True), axis=1, keepdims=True)

    coarse_b = gather_end(0)
    px = 0.5 * (coarse_b + next_x(coarse_b))
    py = 0.5 * (coarse_b + turn(coarse_b, lanes_n - nz3, 2))
    pz = jnp.where(not_top, 0.5 * (coarse_b + turn(coarse_b, lanes_n - 1, 2)), 0.0)
    ends = jnp.where(
        not_top, 0.0, 0.5 * coarse_b
    ) + jnp.where(iota((vn, 8, lanes_n), 2) % nz3 == 0, 0.5 * coarse_b, 0.0)
    kx3[...] = px
    ky3[...] = py
    kz3[...] = pz
    coarse_d = px + last_x(px) + py + turn(py, nz3, 2) + pz + turn(pz, 1, 2) + ends
    d3[...] = coarse_d
    i3[...] = 1.0 / coarse_d

    coarse_f = gather_end(1)
    r3[...] = coarse_f
    s3[...] = jnp.zeros((vn, 8, lanes_n), F32)
    p3[...] = jnp.zeros((vn, 8, lanes_n), F32)
    m3[...] = jnp.zeros((vn, 8, lanes_n), F32)

    def image(p):
        px, py, pz = kx3[...], ky3[...], kz3[...]
        return d3[...] * p - (
            px * next_x(p) + last_x(px * p)
            + py * turn(p, lanes_n - nz3, 2) + turn(py * p, nz3, 2)
            + pz * turn(p, lanes_n - 1, 2) + turn(pz * p, 1, 2)
        )

    def iterate(n, carry):
        gamma_old, alpha_old = carry
        r = r3[...]
        z = r * i3[...]
        az = image(z)
        gamma, delta = total3(r * z), total3(z * az)
        beta = 0.0 if n == 0 else gamma / gamma_old
        alpha = gamma / (delta - beta * gamma / alpha_old)
        p = z + beta * p3[...]
        q = az + beta * m3[...]
        p3[...] = p
        m3[...] = q
        s3[...] = s3[...] + alpha * p
        r3[...] = r - alpha * q
        return gamma, alpha

    one = jnp.ones((1, 1), F32)
    carry = (one, one)
    for n in range(SWEEPS):
        carry = iterate(n, carry)
    solved = s3[...]

    l_at, k_at = iota((128, 8 * vn), 0), iota((128, 8 * vn), 1)
    relative = jnp.where(l_at < 124, l_at // 4, -1)
    wanted = lax.rem(4 * my_start + relative + 8 * vn, 8 * vn)
    from_x = ones_where((k_at % 8) * vn + k_at // 8 == wanted)
    by_lane = pick_left(from_x, solved.reshape(8 * vn, lanes_n))
    q_at, r_at = iota((48, lanes_n), 0), iota((48, lanes_n), 1)
    z_at = 4 * sub + q_at // 8 - 1
    from_row = ones_where(
        (r_at == ((q_at % 8) // 2) * nz3 + z_at) & (z_at >= 0) & (z_at < nz3)
    )
    e3 = pick_left_t(from_row, by_lane).reshape(6, 1, 8, 128)
    e3 = jnp.broadcast_to(e3, (6, 2, 8, 128)).reshape(12, 8, 128)

    e2 = end_level(b2, f2, w2, u2[...] + e3, 2)
    e1x[:, pl.ds(0, 8, stride=2), :] = e2
    e1x[:, pl.ds(1, 8, stride=2), :] = e2
    grown = jnp.broadcast_to(e1x[...].reshape(10, 1, 16, 128), (10, 2, 16, 128))
    e1 = end_level(b1, f1, w1, u1[pl.ds(3, 20)] + grown.reshape(20, 16, 128), 1)

    si, sc = iota((128, 256), 0), iota((128, 256), 1)
    sx = sc - 128
    step = jnp.where(sx % 2 == 0, sx // 2 - 1, sx // 2 + 1)
    step = jnp.where(step < 0, 127, step)
    stretch = ones_where(
        ((sc < width) & (si == sc // 2)) | ((sx >= 0) & (sx < width) & (si == step))
    )
    wide = pick_right(e1.reshape(288, 128), stretch)
    main = wide[:, :128].reshape(18, 16, 128)
    side = wide[:, 128:].reshape(18, 16, 128)
    e0m[:, pl.ds(0, 16, stride=2), :] = main
    e0m[:, pl.ds(1, 16, stride=2), :] = main
    e0x[:, pl.ds(0, 16, stride=2), :] = side
    e0x[:, pl.ds(1, 16, stride=2), :] = side
    e0y[:, pl.ds(0, 16, stride=2), :] = turn(main, 1, 1)
    e0y[:, pl.ds(1, 16, stride=2), :] = turn(main, 15, 1)

    def finish_pair(k):
        e, ex, ey = e0m[k + 1], e0x[k + 1], e0y[k + 1]
        for z, ez in ((2 * k, e0m[k]), (2 * k + 1, e0m[k + 2])):
            out[z] = out[z] + c0[z] * e + cx[z] * ex + cy[z] * ey + cz[z] * ez

    each(2, 0, 16, finish_pair)


def per_device(nb, ns, source, beta, counts):
    lanes_n = 16 * ns

    def vmem(*shape, dtype=F32):
        return pltpu.VMEM(shape, dtype)

    def coarse():
        return vmem(nb, 8, lanes_n)

    scratch = [
        vmem(36, 32, 128), vmem(34, 32, 128), vmem(34, 32, 128), vmem(34, 32, 128),
        vmem(32, 32, 128), vmem(34, 32, 128), vmem(34, 32, 128),
        vmem(16, 32, 128), vmem(2, 32, 128), vmem(2, 2, 32, 128), vmem(2, 8, 128), vmem(2, 2, 8, 128),
        vmem(18, 32, 128), vmem(18, 32, 128), vmem(18, 32, 128),
        vmem(32, 32, 128), vmem(32, 32, 128), vmem(32, 32, 128), vmem(32, 32, 128),
        vmem(28, 16, 128), vmem(26, 16, 128), vmem(26, 16, 128), vmem(26, 16, 128),
        vmem(2, 16, 128), vmem(2, 2, 16, 128), vmem(2, 2, 16, 128),
        vmem(2, 16, 128), vmem(2, 2, 16, 128), vmem(2, 2, 16, 128),
        vmem(14, 16, 128), vmem(10, 16, 128),
        vmem(14, 8, 128), vmem(12, 8, 128), vmem(12, 8, 128), vmem(12, 8, 128), vmem(6, 8, 128),
        vmem(72, 128), vmem(128, lanes_n), vmem(6, 16 // ns, lanes_n), vmem(3, 2, ns, 16 // ns, lanes_n),
        vmem(2, 2, 16, lanes_n), vmem(2, nb, 16, lanes_n), vmem(8 * nb, 16 * nb, dtype=BF16),
        coarse(), coarse(), coarse(), coarse(), coarse(), coarse(), coarse(), coarse(), coarse(),
        pltpu.SemaphoreType.DMA((2,)),
        pltpu.SemaphoreType.DMA((26,)), pltpu.SemaphoreType.DMA((26,)),
        pltpu.SemaphoreType.DMA((2, 2 * ns)), pltpu.SemaphoreType.DMA((2, 2 * ns)),
        pltpu.SemaphoreType.DMA((2, nb // 2)), pltpu.SemaphoreType.DMA((2, nb // 2)),
    ]
    return pl.pallas_call(
        functools.partial(kernel, nb, ns),
        out_shape=jax.ShapeDtypeStruct(source.shape, F32),
        in_specs=[
            pl.BlockSpec(memory_space=pltpu.SMEM),
            pl.BlockSpec(memory_space=pl.ANY),
            pl.BlockSpec(memory_space=pl.ANY),
        ],
        out_specs=pl.BlockSpec(memory_space=pltpu.VMEM),
        scratch_shapes=scratch,
        compiler_params=pltpu.CompilerParams(
            collective_id=0, has_side_effects=True, vmem_limit_bytes=62 * 1024 * 1024
        ),
    )(counts, source, beta)


def solution(mesh):
    in_specs = (P("sub", None, "box"), P("sub", None, "box"), P())
    out_specs = P("sub", None, "box")
    return jax.shard_map(
        functools.partial(per_device, mesh.shape["box"], mesh.shape["sub"]),
        mesh=mesh, in_specs=in_specs, out_specs=out_specs, check_vma=False,
    )
```

```python
import functools
import jax
import jax.numpy as jnp
from jax import lax
from jax.experimental import pallas as pl
from jax.experimental.pallas import tpu as pltpu
from jax.sharding import PartitionSpec as P

CAP = 4
SWEEPS = 8
OMEGA = 0.8
REST = 0.2
TINY = 1e-20
F32 = jnp.float32
BF16 = jnp.bfloat16
MESH = pl.DeviceIdType.MESH


def split(x):
    high = x.astype(BF16)
    middle = (x - high.astype(F32)).astype(BF16)
    return (high, middle)


def pick_right(x, chosen):
    return sum(jnp.dot(part, chosen, preferred_element_type=F32) for part in split(x))


def pick_left(chosen, x):
    return sum(jnp.dot(chosen, part, preferred_element_type=F32) for part in split(x))


def pick_left_t(chosen, x):
    return sum(
        lax.dot_general(chosen, part, (((1,), (1,)), ((), ())), preferred_element_type=F32)
        for part in split(x)
    )


def ones_where(mask):
    return jnp.where(mask, 1.0, 0.0).astype(BF16)


def iota(shape, dim):
    return lax.broadcasted_iota(jnp.int32, shape, dim)


def turn(x, shift, axis):
    return pltpu.roll(x, shift, axis)


def around(x, step):
    rows = x.shape[-2]
    ax, ay = x.ndim - 1, x.ndim - 2
    return (
        turn(x, step, ax) + turn(x, 128 - step, ax) + turn(x, 1, ay) + turn(x, rows - 1, ay)
    )


def kernel(
    nb, ns,
    counts, source, beta, out,
    b0, f0, u0, w0, r0, kx, ky, rs, xs0, xr0, xd0, xc0, e0m, e0x, e0y, c0, cx, cy, cz,
    b1, f1, u1, w1, xs1b, xr1b, xc1b, xs1f, xr1f, xc1f, y1, e1x,
    b2, f2, u2, w2, y2,
    t3, tx, xa, ga, xb, gb_all, onehot, kx3, ky3, kz3, d3, i3, p3, m3, r3, s3,
    in_sem, send_sem, recv_sem, zsend, zrecv, bsend, brecv,
):
    lanes_n = 16 * ns
    nz3 = 4 * ns
    vn = nb
    me, sub = lax.axis_index("box"), lax.axis_index("sub")
    left, right = lax.rem(me + nb - 1, nb), lax.rem(me + 1, nb)
    down, up = lax.rem(sub + ns - 1, ns), lax.rem(sub + 1, ns)
    floor, roof = sub == 0, sub == ns - 1

    get_b = pltpu.make_async_copy(beta, b0.at[pl.ds(2, 32)], in_sem.at[0])
    get_f = pltpu.make_async_copy(source, f0.at[pl.ds(1, 32)], in_sem.at[1])
    get_b.start()
    get_f.start()

    core, chip, chips = lax.rem(me, 2), me // 2, nb // 2

    def stack_peer(k):
        return 2 * chip + lax.rem(core + k, 2), lax.rem(sub + k // 2, ns)

    def chip_peer(k):
        return 2 * lax.rem(chip + k, chips) + core, sub

    barrier = pltpu.get_barrier_semaphore()

    def greet(peer):
        def body(k, carry):
            pl.semaphore_signal(barrier, inc=1, device_id=peer(k), device_id_type=MESH)
            return carry
        return body

    for there in (left, right):
        for level in (down, sub, up):
            pl.semaphore_signal(barrier, inc=1, device_id=(there, level), device_id_type=MESH)
    for k in range(2 * ns - 1, 0, -1):
        greet(stack_peer)(k, 0)
    for k in range(1, chips):
        greet(chip_peer)(k, 0)

    width = 32 * counts[me]
    width_left = 32 * counts[left]
    half = width // 2
    half_left = width_left // 2
    kk = iota((1, nb * 16), 1)
    kd, kj = kk // 16, (kk % 16) // ns * ns + ns - 1 - kk % ns

    def place(d, carry):
        where_from, begin, mine = carry
        here = counts[d]
        value = jnp.where(kj < 4 * here, 4 * begin + kj, -1)
        where_from = jnp.where(kd == d, value, where_from)
        mine = jnp.where(d == me, begin, mine)
        return where_from, begin + here, mine

    where_from, _, my_start = lax.fori_loop(
        0, nb, place, (jnp.full((1, nb * 16), -1, jnp.int32), jnp.int32(0), jnp.int32(0))
    )
    row = iota((8 * vn, nb * 16), 0)
    onehot[...] = ones_where((row % 8) * vn + row // 8 == where_from)

    lane = iota((32, 128), 1)
    live = lane < width
    edge = (lane == 0) | (lane == width - 1)
    edge_two = (lane < 2) | ((lane >= width - 2) & live)
    inner = lane < width - 1

    ll = iota((128, 128), 0)
    lc = iota((128, 128), 1)
    squeeze = ones_where((ll // 2 == lc) & (ll < width))

    get_b.wait()
    get_f.wait()

    def each(count, first, last, act):
        def body(n, carry):
            for k in range(count):
                act(first + n * count + k)
            return carry
        lax.fori_loop(0, (last - first) // count, body, 0)

    def load_planes(n, carry):
        tb, tf = carry
        for k in range(4):
            z = 4 * n + k
            b = jnp.where(live, b0[z + 2], 0.0)
            f = jnp.where(live, f0[z + 1], 0.0)
            b0[z + 2] = b
            f0[z + 1] = f
            tb = tb + turn(jnp.where(edge_two, b, 0.0), 4 * z, 1)
            tf = tf + turn(jnp.where(edge, f, 0.0), 4 * z, 1)
        return tb, tf

    zero_tile = jnp.zeros((32, 128), F32)
    tb, tf = lax.fori_loop(0, 8, load_planes, (zero_tile, zero_tile))
    xs0[0] = tb
    xs0[1] = tf
    for n, z in ((0, 0), (1, 31)):
        corner = jnp.zeros((8, 128), F32)
        for m, shift in ((0, (128 - 4 * z) % 128), (4, lax.rem(389 - 4 * z - width, 128))):
            column = jnp.where(lane == m, turn(tb, shift, 1), 0.0)
            for q in range(4):
                corner = corner + turn(column[8 * q:8 * q + 8], q, 1)
        xd0[n] = corner


    def squeeze_level0():
        both = rs[:, pl.ds(0, 16, stride=2), :] + rs[:, pl.ds(1, 16, stride=2), :]
        return pick_right(both.reshape(256, 128), squeeze).reshape(16, 16, 128)

    def coarsen(x, scratch, step):
        planes, rows, _ = x.shape
        n = planes // 2
        pairs = x.reshape(n, 2, rows, 128)
        scratch[pl.ds(0, n)] = pairs[:, 0] + pairs[:, 1]
        y = (
            scratch[pl.ds(0, n), pl.ds(0, rows // 2, stride=2), :]
            + scratch[pl.ds(0, n), pl.ds(1, rows // 2, stride=2), :]
        )
        odd = (iota(y.shape, 2) // step) % 2 == 1
        return y + jnp.where(odd, turn(y, step, 2), turn(y, 128 - step, 2))

    def pack(x, tile_ref, reach):
        at = iota((16, 128), 1)
        keep = (at < reach) | ((at >= half - reach) & (at < half))
        for n in range(2):
            total = jnp.zeros((16, 128), F32)
            for z in range(8):
                total = total + turn(jnp.where(keep, x[8 * n + z], 0.0), 16 * z, 1)
            tile_ref[n] = total

    def to_slots(x):
        for z in range(4):
            t3[pl.ds(z, 4, stride=8), :] = x[z]
            t3[pl.ds(z + 4, 4, stride=8), :] = x[z]
        tiles = t3[pl.ds(0, 32)].reshape(4, 1, 8, 128)
        tiles = jnp.broadcast_to(tiles, (4, ns // 2, 8, 128)).reshape(lanes_n, 128)
        tx[...] = jnp.transpose(tiles)
        return tx[pl.ds(0, 16, stride=4), :]

    def pair_b(k):
        rs[k] = b0[2 * k + 2] + b0[2 * k + 3]

    each(4, 0, 16, pair_b)
    own_b1 = 0.125 * squeeze_level0()
    b1[pl.ds(6, 16)] = own_b1
    pack(own_b1, xs1b, 6)
    own_b2 = 0.125 * coarsen(own_b1, y1, 1)

    def couple(e):
        b = b0[e + 1]
        px = jnp.where(inner, b + turn(b, 127, 1), 0.0)
        py = b + turn(b, 31, 0)
        kx[e] = px
        ky[e] = py
        return px + turn(px, 1, 1) + py + turn(py, 1, 0) + (b0[e] + b) + (b + b0[e + 2])

    def start_plane(e, more=0.0):
        w = (2.0 * OMEGA) / jnp.maximum(couple(e) + more, TINY)
        w0[e] = w
        u0[e] = w * f0[e]

    def pull(e):
        u, px, py, b = u0[e], kx[e], ky[e], b0[e + 1]
        return (
            px * turn(u, 127, 1) + turn(px * u, 1, 1) + py * turn(u, 31, 0) + turn(py * u, 1, 0)
            + (b0[e] + b) * u0[e - 1] + (b + b0[e + 2]) * u0[e + 1]
        )

    def residual(z):
        r = REST * f0[z + 1] + 0.5 * pull(z + 1)
        r0[z] = r
        return r

    def pair_r(k):
        rs[k] = residual(2 * k) + residual(2 * k + 1)


    pl.semaphore_wait(barrier, 6 + (2 * ns - 1) + (chips - 1))

    def x_copies(src, dst, for_up, for_down, corner, base):
        made = []
        for side, there in ((0, right), (1, left)):
            for n, (begin, end, level) in enumerate((
                (src, dst.at[side], sub),
                (for_up, corner.at[side, 0], up),
                (for_down, corner.at[side, 1], down),
            )):
                at = base + side * 3 + n
                made.append(
                    pltpu.make_async_remote_copy(
                        src_ref=begin, dst_ref=end,
                        send_sem=send_sem.at[at], recv_sem=recv_sem.at[at],
                        device_id=(there, level), device_id_type=MESH,
                    )
                )
        return made

    def z_copies(ref, own, halo, base):
        made = []
        for n, (begin, to, level) in enumerate(
            ((own, 0, up), (halo, own + halo, down))
        ):
            made.append(
                pltpu.make_async_remote_copy(
                    src_ref=ref.at[pl.ds(begin, halo)], dst_ref=ref.at[pl.ds(to, halo)],
                    send_sem=send_sem.at[base + n], recv_sem=recv_sem.at[base + n],
                    device_id=(me, level), device_id_type=MESH,
                )
            )
        return made

    def start(copies):
        for copy in copies:
            copy.start()

    def wait(copies):
        for copy in copies:
            copy.wait()

    copies0 = x_copies(xs0, xr0, xd0.at[1], xd0.at[0], xc0, 0) + z_copies(b0, 32, 2, 6) + z_copies(f0, 32, 1, 8)
    start(copies0)

    def stack_copy(k, which, slot):
        return pltpu.make_async_remote_copy(
            src_ref=xa.at[which], dst_ref=ga.at[which, slot[0], slot[1]],
            send_sem=zsend.at[which, k], recv_sem=zrecv.at[which, k],
            device_id=stack_peer(k), device_id_type=MESH,
        )

    def chip_copy(k, which, slot):
        return pltpu.make_async_remote_copy(
            src_ref=xb.at[which], dst_ref=gb_all.at[which, pl.ds(2 * slot, 2)],
            send_sem=bsend.at[which, k], recv_sem=brecv.at[which, k],
            device_id=chip_peer(k), device_id_type=MESH,
        )

    def stack_from(k):
        return lax.rem(core + k, 2), lax.rem(sub - k // 2 + ns, ns)

    def chip_from(k):
        return lax.rem(chip - k + chips, chips)

    def send_all(make, which, mine, count):
        def body(k, carry):
            make(k, which, mine).start()
            return carry
        lax.fori_loop(1, count, body, 0)

    def wait_all(make, which, source, count):
        def body(k, carry):
            copy = make(k, which, source(k))
            copy.wait_send()
            copy.wait_recv()
            return carry
        lax.fori_loop(1, count, body, 0)

    slot_at = (iota((ns, lanes_n), 1) // 4) % ns
    row_at = iota((ns, lanes_n), 0)

    def gather_start(x, which):
        tile = to_slots(x)
        for h in range(16 // ns):
            part = jnp.where(row_at == slot_at, tile[h * ns:(h + 1) * ns], 0.0)
            part = jnp.sum(part, axis=0, keepdims=True)
            xa[which, pl.ds(h, 1)] = part
            ga[which, core, sub, pl.ds(h, 1)] = part
        send_all(stack_copy, which, (core, sub), 2 * ns)

    def gather_turn(which):
        wait_all(stack_copy, which, stack_from, 2 * ns)
        for c in range(2):
            for h in range(16 // ns):
                tile = jnp.zeros((ns, lanes_n), F32)
                for k in range(ns):
                    part = jnp.broadcast_to(ga[which, c, k, pl.ds(h, 1)], (ns, lanes_n))
                    part = pltpu.roll(part, 0, 1, stride=4, stride_axis=0)
                    part = turn(part, (4 * (k - ns + 1)) % lanes_n, 1)
                    tile = jnp.where(slot_at == k, part, tile)
                xb[which, c, pl.ds(h * ns, ns)] = tile
                gb_all[which, 2 * chip + c, pl.ds(h * ns, ns)] = tile
        send_all(chip_copy, which, chip, chips)

    def gather_end(which):
        wait_all(chip_copy, which, chip_from, chips)
        rows = gb_all[which].reshape(nb * 16, lanes_n)
        return pick_left(onehot[...], rows).reshape(vn, 8, lanes_n)

    copies_b1 = x_copies(xs1b, xr1b, xs1b.at[1], xs1b.at[0], xc1b, 10)
    copies_b1 = copies_b1 + z_copies(b1, 16, 6, 16)
    start(copies_b1)

    each(5, 2, 32, start_plane)
    each(2, 1, 15, pair_r)
    wait(copies0)

    @pl.when(floor)
    def _():
        b0[pl.ds(0, 2)] = jnp.zeros((2, 32, 128), F32)
        f0[pl.ds(0, 1)] = jnp.zeros((1, 32, 128), F32)

    @pl.when(roof)
    def _():
        b0[pl.ds(34, 2)] = jnp.zeros((2, 32, 128), F32)
        f0[pl.ds(33, 1)] = jnp.zeros((1, 32, 128), F32)

    quarter = lane % 4
    group = lane // 4
    q0, q3 = quarter == 0, quarter == 3
    turn_l1 = lax.rem(129 - width_left + 128, 128)
    turn_l2 = lax.rem(130 - width_left + 128, 128)

    def ghost(from_left, from_right, near_by):
        shift_l = turn_l1 if near_by == 1 else turn_l2
        return jnp.where(
            q0, turn(from_left, shift_l, 1),
            jnp.where(q3, turn(from_right, lax.rem(width - near_by, 128), 1), 0.0),
        )

    ghost_b = ghost(xr0[0, 0], xr0[1, 0], 1)

    def ghost_corner(n, z, outside):
        from_left, from_right = xc0[0, n], xc0[1, n]
        rows = []
        for q in range(4):
            at_left = turn(from_left, (128 + 4 * z - 4 - q) % 128, 1)
            at_right = turn(from_right, lax.rem(4 * z + width + 127 - q, 128), 1)
            rows.append(jnp.where(
                lane[:8] == 4 * z, at_left,
                jnp.where(lane[:8] == lax.rem(4 * z + width - 1, 128), at_right, 0.0),
            ))
        return jnp.where(outside, 0.0, jnp.concatenate(rows, 0))

    ghost_b_low = ghost_corner(0, 31, floor)
    ghost_b_high = ghost_corner(1, 0, roof)
    ghost_b_far = ghost(xr0[0, 0], xr0[1, 0], 2)
    ghost_f = ghost(xr0[0, 1], xr0[1, 1], 1)
    own_edge = jnp.where(q0 | q3, tb, 0.0)
    turned = width // 4 - 1
    first_z = (q0 & (group == 0)) | (q3 & (group == turned))
    last_z = (q0 & (group == 31)) | (q3 & (group == lax.rem(31 + turned, 32)))

    def beside(tile, low, high):
        return (
            turn(tile, 1, 0) + turn(tile, 31, 0)
            + turn(jnp.where(first_z, high, tile), 124, 1)
            + turn(jnp.where(last_z, low, tile), 4, 1)
        )

    ghost_k = ghost_b + own_edge
    ghost_sum = 6.0 * ghost_b + ghost_b_far + own_edge
    ghost_sum = ghost_sum + beside(ghost_b, ghost_b_low, ghost_b_high)
    ghost_u = (2.0 * OMEGA) * ghost_f / jnp.maximum(ghost_sum, TINY)

    below = turn(jnp.where(edge, b0[1], 0.0), 124, 1)
    above = jnp.where(edge, b0[34], 0.0)
    edge_part = 6.0 * own_edge + beside(own_edge, below, above)
    edge_part = edge_part + jnp.where(q0, turn(tb, 127, 1), turn(tb, 1, 1))
    without = (edge_part - own_edge)
    edge_w = (2.0 * OMEGA) / jnp.maximum(without + ghost_k, TINY)
    edge_w = jnp.where(q0 | q3, edge_w, 0.0)
    drift = edge_w * tf - jnp.where(
        q0 | q3, (2.0 * OMEGA) * tf / jnp.maximum(without, TINY), 0.0
    )
    drift_v = own_edge * drift
    gap = own_edge * beside(drift, 0.0, 0.0) + beside(drift_v, 0.0, 0.0) + ghost_k * ghost_u
    gap = jnp.where(
        q0 | q3, gap,
        jnp.where(
            quarter == 1, (tb + turn(own_edge, 1, 1)) * turn(drift, 1, 1),
            (tb + turn(own_edge, 127, 1)) * turn(drift, 127, 1),
        ),
    )
    gap = 0.5 * gap
    gap_pair = gap + turn(gap, 124, 1)

    def back(tile, z):
        return turn(tile, lax.rem(128 - 4 * z, 128), 1)

    start_plane(0, jnp.where(edge, turn(ghost_b_low + below, 4, 1), 0.0))
    start_plane(1)
    start_plane(32)
    start_plane(33, jnp.where(edge, ghost_b_high + above, 0.0))
    pair_r(0)
    pair_r(15)

    def mend(k):
        rs[k] = rs[k] + jnp.where(edge_two, back(gap_pair, 2 * k), 0.0)

    each(16, 0, 16, mend)

    def join(ref, xr, xc, halo):
        at = iota((16, 128), 1)
        inside = at < half
        keep = ((at >= half) & (at < half + halo)) | (at >= 128 - halo)
        sub_at = at % 16

        def beside_own(from_left, from_right):
            from_left = turn(from_left, lax.rem(256 - half_left, 128), 1)
            from_right = turn(from_right, half, 1)
            return jnp.where(
                sub_at >= 16 - halo, from_left, jnp.where(sub_at < halo, from_right, 0.0)
            )

        tiles = [beside_own(xr[0, n], xr[1, n]) for n in range(2)]
        low = beside_own(xc[0, 0], xc[1, 0])
        high = beside_own(xc[0, 1], xc[1, 1])
        for z in range(-halo, 16 + halo):
            tile = low if z < 0 else (high if z >= 16 else tiles[z // 8])
            plane = jnp.where(
                inside, ref[z + halo],
                jnp.where(keep, turn(tile, (128 - 16 * (z % 8)) % 128, 1), 0.0),
            )
            if z < 0:
                plane = jnp.where(floor, 0.0, plane)
            if z >= 16:
                plane = jnp.where(roof, 0.0, plane)
            ref[z + halo] = plane

    def only_inside(x, out):
        n = x.shape[0]
        return jnp.concatenate([
            jnp.where(floor, 0.0, x[:out]), x[out:n - out], jnp.where(roof, 0.0, x[n - out:])
        ], 0)

    def weights(b, step):
        n = b.shape[0]
        middle = b[1:n - 1]
        total = around(middle, step) + b[:n - 2] + b[2:]
        return OMEGA / jnp.maximum(3.0 * middle + 0.5 * total, TINY)

    def gain_of(b, u, v, step):
        n = u.shape[0]
        return b * (around(u[1:n - 1], step) + u[:n - 2] + u[2:]) + (
            around(v[1:n - 1], step) + v[:n - 2] + v[2:]
        )

    def begin_level(b_ref, f_ref, w_ref, u_ref, step):
        n = f_ref.shape[0]
        f = f_ref[...]
        u = w_ref[...] * f
        u_ref[...] = u
        v = b_ref[pl.ds(1, n)] * u
        gain = gain_of(b_ref[pl.ds(2, n - 2)], u, v, step)
        return REST * f[1:n - 1] + 0.5 * gain

    def end_level(b_ref, f_ref, w_ref, u, step):
        n = u.shape[0]
        skip = (f_ref.shape[0] - n) // 2 + 1
        v = b_ref[pl.ds(skip, n)] * u
        b = b_ref[pl.ds(skip + 1, n - 2)]
        gain = gain_of(b, u, v, step)
        return only_inside(REST * u[1:n - 1] + w_ref[pl.ds(skip, n - 2)] * (
            f_ref[pl.ds(skip, n - 2)] + 0.5 * gain
        ), 1)

    own_f1 = 0.5 * squeeze_level0()
    f1[pl.ds(5, 16)] = own_f1
    pack(own_f1, xs1f, 5)
    copies_f1 = x_copies(xs1f, xr1f, xs1f.at[1], xs1f.at[0], xc1f, 18)
    copies_f1 = copies_f1 + z_copies(f1, 16, 5, 24)
    start(copies_f1)
    gather_start(0.125 * coarsen(own_b2, y2, 2), 0)

    def prepare(z, odd):
        e = z + 1
        w = jnp.where(edge, back(edge_w, z), w0[e])
        r = r0[z] + jnp.where(edge_two, back(gap, z), 0.0)
        out[z] = jnp.where(live, w * (f0[e] + r), 0.0)
        px, py, b = kx[e], ky[e], b0[e + 1]
        px_low, py_low = turn(px, 1, 1), turn(py, 1, 0)
        pz_low, pz = b0[e] + b, b + b0[e + 2]
        even_x, even_y = lane % 2 == 0, iota((32, 128), 0) % 2 == 0
        rim = jnp.where(edge, back(ghost_k, z), 0.0)
        same = jnp.where(even_x, px, px_low) + jnp.where(even_y, py, py_low)
        same = same + (pz_low if odd else pz)
        w = jnp.where(live, 0.5 * w, 0.0)
        c0[z] = REST + w * same
        cx[z] = w * (jnp.where(even_x, px_low, px) + rim)
        cy[z] = w * jnp.where(even_y, py_low, py)
        cz[z] = w * (pz if odd else pz_low)

    def prepare_pair(k):
        prepare(2 * k, False)
        prepare(2 * k + 1, True)

    wait(copies_b1)
    join(b1, xr1b, xc1b, 6)
    w1[...] = weights(b1[...], 1)
    b2[...] = 0.125 * coarsen(b1[...], y1, 1)
    w2[...] = weights(b2[...], 2)

    wait(copies_f1)
    join(f1, xr1f, xc1f, 5)
    r1 = begin_level(b1, f1, w1, u1, 1)
    f2[...] = only_inside(0.5 * coarsen(r1, y1, 1), 2)
    r2 = begin_level(b2, f2, w2, u2, 2)
    gather_start(0.5 * coarsen(r2[1:9], y2, 2), 1)
    gather_turn(0)
    each(1, 0, 8, prepare_pair)
    gather_turn(1)
    each(1, 8, 16, prepare_pair)

    not_top = iota((vn, 8, lanes_n), 2) % nz3 < nz3 - 1

    def next_x(p):
        return jnp.concatenate([p[1:], turn(p[:1], 7, 1)], 0)

    def last_x(p):
        return jnp.concatenate([turn(p[vn - 1:], 1, 1), p[:vn - 1]], 0)

    def total3(x):
        tile = jnp.sum(x, axis=0)
        return jnp.sum(jnp.sum(tile, axis=0, keepdims=True), axis=1, keepdims=True)

    coarse_b = gather_end(0)
    px = 0.5 * (coarse_b + next_x(coarse_b))
    py = 0.5 * (coarse_b + turn(coarse_b, lanes_n - nz3, 2))
    pz = jnp.where(not_top, 0.5 * (coarse_b + turn(coarse_b, lanes_n - 1, 2)), 0.0)
    ends = jnp.where(
        not_top, 0.0, 0.5 * coarse_b
    ) + jnp.where(iota((vn, 8, lanes_n), 2) % nz3 == 0, 0.5 * coarse_b, 0.0)
    kx3[...] = px
    ky3[...] = py
    kz3[...] = pz
    coarse_d = px + last_x(px) + py + turn(py, nz3, 2) + pz + turn(pz, 1, 2) + ends
    d3[...] = coarse_d
    i3[...] = 1.0 / coarse_d

    coarse_f = gather_end(1)
    r3[...] = coarse_f
    s3[...] = jnp.zeros((vn, 8, lanes_n), F32)
    p3[...] = jnp.zeros((vn, 8, lanes_n), F32)
    m3[...] = jnp.zeros((vn, 8, lanes_n), F32)

    def image(p):
        px, py, pz = kx3[...], ky3[...], kz3[...]
        return d3[...] * p - (
            px * next_x(p) + last_x(px * p)
            + py * turn(p, lanes_n - nz3, 2) + turn(py * p, nz3, 2)
            + pz * turn(p, lanes_n - 1, 2) + turn(pz * p, 1, 2)
        )

    def iterate(n, carry):
        over_gamma, over_alpha = carry
        r = r3[...]
        z = r * i3[...]
        az = image(z)
        gamma, delta = total3(r * z), total3(z * az)
        beta = 0.0 if n == 0 else gamma * over_gamma
        alpha = gamma / (delta - beta * gamma * over_alpha)
        p = z + beta * p3[...]
        q = az + beta * m3[...]
        p3[...] = p
        m3[...] = q
        s3[...] = s3[...] + alpha * p
        r3[...] = r - alpha * q
        return 1.0 / gamma, 1.0 / alpha

    one = jnp.ones((1, 1), F32)
    carry = (one, one)
    for n in range(SWEEPS):
        carry = iterate(n, carry)
    solved = s3[...]

    l_at, k_at = iota((128, 8 * vn), 0), iota((128, 8 * vn), 1)
    relative = jnp.where(l_at < 124, l_at // 4, -1)
    wanted = lax.rem(4 * my_start + relative + 8 * vn, 8 * vn)
    from_x = ones_where((k_at % 8) * vn + k_at // 8 == wanted)
    by_lane = pick_left(from_x, solved.reshape(8 * vn, lanes_n))
    q_at, r_at = iota((48, lanes_n), 0), iota((48, lanes_n), 1)
    z_at = 4 * sub + q_at // 8 - 1
    from_row = ones_where(
        (r_at == ((q_at % 8) // 2) * nz3 + z_at) & (z_at >= 0) & (z_at < nz3)
    )
    e3 = pick_left_t(from_row, by_lane).reshape(6, 1, 8, 128)
    e3 = jnp.broadcast_to(e3, (6, 2, 8, 128)).reshape(12, 8, 128)

    e2 = end_level(b2, f2, w2, u2[...] + e3, 2)
    e1x[:, pl.ds(0, 8, stride=2), :] = e2
    e1x[:, pl.ds(1, 8, stride=2), :] = e2
    grown = jnp.broadcast_to(e1x[...].reshape(10, 1, 16, 128), (10, 2, 16, 128))
    e1 = end_level(b1, f1, w1, u1[pl.ds(3, 20)] + grown.reshape(20, 16, 128), 1)

    si, sc = iota((128, 256), 0), iota((128, 256), 1)
    sx = sc - 128
    step = jnp.where(sx % 2 == 0, sx // 2 - 1, sx // 2 + 1)
    step = jnp.where(step < 0, 127, step)
    stretch = ones_where(
        ((sc < width) & (si == sc // 2)) | ((sx >= 0) & (sx < width) & (si == step))
    )
    wide = pick_right(e1.reshape(288, 128), stretch)
    main = wide[:, :128].reshape(18, 16, 128)
    side = wide[:, 128:].reshape(18, 16, 128)
    e0m[:, pl.ds(0, 16, stride=2), :] = main
    e0m[:, pl.ds(1, 16, stride=2), :] = main
    e0x[:, pl.ds(0, 16, stride=2), :] = side
    e0x[:, pl.ds(1, 16, stride=2), :] = side
    e0y[:, pl.ds(0, 16, stride=2), :] = turn(main, 1, 1)
    e0y[:, pl.ds(1, 16, stride=2), :] = turn(main, 15, 1)

    def finish_pair(k):
        e, ex, ey = e0m[k + 1], e0x[k + 1], e0y[k + 1]
        for z, ez in ((2 * k, e0m[k]), (2 * k + 1, e0m[k + 2])):
            out[z] = out[z] + c0[z] * e + cx[z] * ex + cy[z] * ey + cz[z] * ez

    each(2, 0, 16, finish_pair)


def per_device(nb, ns, source, beta, counts):
    lanes_n = 16 * ns

    def vmem(*shape, dtype=F32):
        return pltpu.VMEM(shape, dtype)

    def coarse():
        return vmem(nb, 8, lanes_n)

    scratch = [
        vmem(36, 32, 128), vmem(34, 32, 128), vmem(34, 32, 128), vmem(34, 32, 128),
        vmem(32, 32, 128), vmem(34, 32, 128), vmem(34, 32, 128),
        vmem(16, 32, 128), vmem(2, 32, 128), vmem(2, 2, 32, 128), vmem(2, 8, 128), vmem(2, 2, 8, 128),
        vmem(18, 32, 128), vmem(18, 32, 128), vmem(18, 32, 128),
        vmem(32, 32, 128), vmem(32, 32, 128), vmem(32, 32, 128), vmem(32, 32, 128),
        vmem(28, 16, 128), vmem(26, 16, 128), vmem(26, 16, 128), vmem(26, 16, 128),
        vmem(2, 16, 128), vmem(2, 2, 16, 128), vmem(2, 2, 16, 128),
        vmem(2, 16, 128), vmem(2, 2, 16, 128), vmem(2, 2, 16, 128),
        vmem(14, 16, 128), vmem(10, 16, 128),
        vmem(14, 8, 128), vmem(12, 8, 128), vmem(12, 8, 128), vmem(12, 8, 128), vmem(6, 8, 128),
        vmem(72, 128), vmem(128, lanes_n), vmem(6, 16 // ns, lanes_n), vmem(3, 2, ns, 16 // ns, lanes_n),
        vmem(2, 2, 16, lanes_n), vmem(2, nb, 16, lanes_n), vmem(8 * nb, 16 * nb, dtype=BF16),
        coarse(), coarse(), coarse(), coarse(), coarse(), coarse(), coarse(), coarse(), coarse(),
        pltpu.SemaphoreType.DMA((2,)),
        pltpu.SemaphoreType.DMA((26,)), pltpu.SemaphoreType.DMA((26,)),
        pltpu.SemaphoreType.DMA((2, 2 * ns)), pltpu.SemaphoreType.DMA((2, 2 * ns)),
        pltpu.SemaphoreType.DMA((2, nb // 2)), pltpu.SemaphoreType.DMA((2, nb // 2)),
    ]
    return pl.pallas_call(
        functools.partial(kernel, nb, ns),
        out_shape=jax.ShapeDtypeStruct(source.shape, F32),
        in_specs=[
            pl.BlockSpec(memory_space=pltpu.SMEM),
            pl.BlockSpec(memory_space=pl.ANY),
            pl.BlockSpec(memory_space=pl.ANY),
        ],
        out_specs=pl.BlockSpec(memory_space=pltpu.VMEM),
        scratch_shapes=scratch,
        compiler_params=pltpu.CompilerParams(
            collective_id=0, has_side_effects=True, vmem_limit_bytes=62 * 1024 * 1024
        ),
    )(counts, source, beta)


def solution(mesh):
    in_specs = (P("sub", None, "box"), P("sub", None, "box"), P())
    out_specs = P("sub", None, "box")
    return jax.shard_map(
        functools.partial(per_device, mesh.shape["box"], mesh.shape["sub"]),
        mesh=mesh, in_specs=in_specs, out_specs=out_specs, check_vma=False,
    )
```
